256 devices in a mesh: ctx: 16 (over z_hi, x), dp: 16 (over z_lo, y, core).
Axes of the slice: x: 4, y: 4, z: 8 (z_hi: 4, z_lo: 2; z = z_hi * 2 + z_lo), core: 2. Of those that a mesh axis runs over, the one named last changes fastest.
Arguments:
- doc_states: bfloat16 [4096, 4096], P('dp', 'ctx'), may hold values from -3 to 3
- context: bfloat16 [128, 4096], P('ctx'), may hold values from -6 to 6
- norm_gain: float32 [4096], replicated, may hold values from 0.5 to 1.5
- w_query: bfloat16 [4096, 2048], P(None, 'ctx'), may hold values from -0.09375 to 0.09375
- w_key: bfloat16 [4096, 2048], P(None, 'ctx'), may hold values from -0.09375 to 0.09375
- w_value: bfloat16 [4096, 2048], P(None, 'ctx'), may hold values from -0.09375 to 0.09375
- w_out: bfloat16 [2048, 4096], P('ctx'), may hold values from -0.125 to 0.125
- partners: int32 [64], P('dp'), may hold values from 0 to 63, as said below
Outputs:
- loss: float32 [], replicated
- grad_context: float32 [128, 4096], P('ctx')
- grad_query: float32 [4096, 2048], P('dp', 'ctx')
- grad_key: float32 [4096, 2048], P('dp', 'ctx')
- grad_value: float32 [4096, 2048], P('dp', 'ctx')
- grad_out: float32 [2048, 4096], P('ctx', 'dp')
The draws below stay inside these ranges and needn't reach their ends.
Inputs may be any that keep to these rules, and one draw needn't show every extreme that they name: partners[i] != i, and every document is the partner of exactly one document.
All inputs are finite; a program needn't handle non-finite values.
Results may differ from the reference program's by a relative error of at most 0.017.
Values may be sent and summed in bfloat16 or wider, within the bound.
No kernel may reach another device: no remote copies, remote signals or barrier semaphores. Data moves between devices by JAX's collectives and lax.ppermute only.
A program may use at most 64 MiB of HBM per device.

```python
import jax
import jax.numpy as jnp
from jax import lax

D = 4096
HD = 128
HEADS = 16
QW = 2048
DOC_LEN = 64
DOCS = 64
NCTX = 128


def draw_partners(key, part):
    key = jax.random.fold_in(key, 7)
    ordering = jax.random.permutation(key, DOCS).astype(jnp.int32)
    following = jnp.roll(ordering, -1)
    return jnp.zeros((DOCS,), jnp.int32).at[ordering].set(following)


def steps_of(own_key, extent, cuts, smallest, top_value):
    gain = 1.0
    for position, blocks in cuts:
        steps = jax.random.uniform(jax.random.fold_in(jax.random.fold_in(own_key, 6), position), (blocks,), jnp.float32, smallest / len(cuts), top_value / len(cuts))
        gain = gain * jnp.repeat(jnp.exp(steps), extent[position] // blocks).reshape((-1,) + (1,) * (len(extent) - 1 - position))
    return gain


def normal_values(own_key, dims, scale, reach, split=(), kind=jnp.bfloat16):
    entries = scale * jax.random.normal(own_key, dims, jnp.float32)
    if split:
        entries = entries * steps_of(own_key, dims, split, -0.22, 0.18)
    return jnp.clip(entries, -reach, reach).astype(kind)


def setup_inputs(seed: int = 0) -> dict:
    key_list = jax.random.split(jax.random.key(seed), 9)
    return {
        "doc_states": normal_values(key_list[0], (DOCS * DOC_LEN, D), 0.5, 3.0, ((0, 16), (1, 16))),
        "context": normal_values(key_list[1], (NCTX, D), 1.0, 6.0, ((0, 16),)),
        "norm_gain": jnp.clip(1.0 + 0.1 * jax.random.normal(key_list[2], (D,), jnp.float32), 0.5, 1.5),
        "w_query": normal_values(key_list[3], (D, QW), D ** -0.5, 0.09375, ((1, 16),)),
        "w_key": normal_values(key_list[4], (D, QW), D ** -0.5, 0.09375, ((1, 16),)),
        "w_value": normal_values(key_list[5], (D, QW), D ** -0.5, 0.09375, ((1, 16),)),
        "w_out": normal_values(key_list[6], (QW, D), QW ** -0.5, 0.125, ((0, 16),)),
        "partners": draw_partners(jax.random.fold_in(key_list[8], 71), 0),
    }


epsilon = 1e-05
sharpness_divisor = 0.05
loss_scale = 65536.0
exact_arithmetic_setting = lax.Precision.HIGHEST

def to_wide(array):
    return array.astype(jnp.float32)

def rms_norm(matrix, gain_row):
    widened = to_wide(matrix)
    inverse_rms = lax.rsqrt(lax.optimization_barrier(jnp.mean(widened * widened, axis=-1, keepdims=True)) + epsilon)
    return ((widened * inverse_rms * gain_row).astype(jnp.bfloat16), inverse_rms)

def attend(queries, doc_keys, doc_values, ctx_keys, ctx_values):
    factor = queries.shape[-1] ** (-0.5)
    ctx_scores = jnp.einsum('blhe,che->bhlc', to_wide(queries), to_wide(ctx_keys), precision=exact_arithmetic_setting) * factor
    own_scores = jnp.einsum('blhe,bmhe->bhlm', to_wide(queries), to_wide(doc_keys), precision=exact_arithmetic_setting) * factor
    ctx_exps = jnp.exp(ctx_scores)
    own_exps = jnp.exp(own_scores)
    normalizer = lax.optimization_barrier(jnp.sum(ctx_exps, axis=-1, keepdims=True)) + lax.optimization_barrier(jnp.sum(own_exps, axis=-1, keepdims=True))
    ctx_probs = ctx_exps / normalizer
    own_probs = own_exps / normalizer
    ctx_weights = ctx_probs.astype(jnp.bfloat16)
    own_weights = own_probs.astype(jnp.bfloat16)
    mixture = jnp.einsum('bhlc,che->blhe', to_wide(ctx_weights), to_wide(ctx_values), precision=exact_arithmetic_setting)
    mixture = mixture + jnp.einsum('bhlm,bmhe->blhe', to_wide(own_weights), to_wide(doc_values), precision=exact_arithmetic_setting)
    return (mixture.astype(jnp.bfloat16), (ctx_probs, own_probs, ctx_weights, own_weights))

def attend_back(grad_mixture, queries, doc_keys, doc_values, ctx_keys, ctx_values, saved):
    ctx_probs, own_probs, ctx_weights, own_weights = saved
    factor = queries.shape[-1] ** (-0.5)
    upstream = to_wide(grad_mixture)
    ctx_dweights = jnp.einsum('blhe,che->bhlc', upstream, to_wide(ctx_values), precision=exact_arithmetic_setting)
    own_dweights = jnp.einsum('blhe,bmhe->bhlm', upstream, to_wide(doc_values), precision=exact_arithmetic_setting)
    inner_sum = lax.optimization_barrier(jnp.sum(ctx_probs * ctx_dweights, axis=-1, keepdims=True)) + lax.optimization_barrier(jnp.sum(own_probs * own_dweights, axis=-1, keepdims=True))
    ctx_dscores = (ctx_probs * (ctx_dweights - inner_sum) * factor).astype(jnp.bfloat16)
    own_dscores = (own_probs * (own_dweights - inner_sum) * factor).astype(jnp.bfloat16)
    grad_queries = jnp.einsum('bhlc,che->blhe', to_wide(ctx_dscores), to_wide(ctx_keys), precision=exact_arithmetic_setting)
    grad_queries = grad_queries + jnp.einsum('bhlm,bmhe->blhe', to_wide(own_dscores), to_wide(doc_keys), precision=exact_arithmetic_setting)
    grad_keys = jnp.einsum('bhlm,blhe->bmhe', to_wide(own_dscores), to_wide(queries), precision=exact_arithmetic_setting)
    grad_values = jnp.einsum('bhlm,blhe->bmhe', to_wide(own_weights), upstream, precision=exact_arithmetic_setting)
    grad_ctx_keys = jnp.einsum('bhlc,blhe->che', to_wide(ctx_dscores), to_wide(queries), precision=exact_arithmetic_setting)
    grad_ctx_values = jnp.einsum('bhlc,blhe->che', to_wide(ctx_weights), upstream, precision=exact_arithmetic_setting)
    return (grad_queries.astype(jnp.bfloat16), grad_keys.astype(jnp.bfloat16), grad_values.astype(jnp.bfloat16), grad_ctx_keys, grad_ctx_values)

def reference(doc_states, context, norm_gain, w_query, w_key, w_value, w_out, partners):
    tokens = DOCS * DOC_LEN
    normed, doc_inverse = rms_norm(doc_states, norm_gain)
    ctx_normed, ctx_inverse = rms_norm(context, norm_gain)

    def project(matrix, weight):
        return jnp.dot(matrix, weight, preferred_element_type=jnp.float32).astype(jnp.bfloat16)
    queries = project(normed, w_query).reshape(DOCS, DOC_LEN, HEADS, HD)
    doc_keys = project(normed, w_key).reshape(DOCS, DOC_LEN, HEADS, HD)
    doc_values = project(normed, w_value).reshape(DOCS, DOC_LEN, HEADS, HD)
    ctx_keys = project(ctx_normed, w_key).reshape(NCTX, HEADS, HD)
    ctx_values = project(ctx_normed, w_value).reshape(NCTX, HEADS, HD)
    mixture, saved = attend(queries, doc_keys, doc_values, ctx_keys, ctx_values)
    mixture_rows = mixture.reshape(tokens, QW)
    branch = jnp.dot(mixture_rows, w_out, preferred_element_type=jnp.float32)
    pooled = lax.optimization_barrier(jnp.mean((to_wide(doc_states) + branch).reshape(DOCS, DOC_LEN, D), axis=1))
    mean_mixture = lax.optimization_barrier(jnp.mean(to_wide(mixture_rows).reshape(DOCS, DOC_LEN, QW), axis=1))
    euclidean_magnitude = jnp.sqrt(lax.optimization_barrier(jnp.sum(pooled * pooled, axis=1)) + 1e-06)
    rescaled_document_codes = pooled / euclidean_magnitude[:, None]
    cosine_affinity_grid = jnp.dot(pooled, pooled.T, precision=exact_arithmetic_setting)
    raw_affinity_table = cosine_affinity_grid / (euclidean_magnitude[:, None] * euclidean_magnitude[None, :]) / sharpness_divisor
    doc_ids = jnp.arange(DOCS, dtype=jnp.int32)
    others = doc_ids[:, None] != doc_ids[None, :]
    exp_scores = jnp.where(others, jnp.exp(raw_affinity_table), 0.0)
    row_totals = lax.optimization_barrier(jnp.sum(exp_scores, axis=1))
    chosen = (partners[:, None] == doc_ids[None, :]).astype(jnp.float32)
    picked = lax.optimization_barrier(jnp.sum(raw_affinity_table * chosen, axis=1))
    loss = jnp.mean(jnp.log(row_totals) - picked)
    couple_weighting = (exp_scores / row_totals[:, None] - chosen) / DOCS * loss_scale
    direction_loss_slope = (jnp.dot(couple_weighting, rescaled_document_codes, precision=exact_arithmetic_setting) + jnp.dot(couple_weighting.T, rescaled_document_codes, precision=exact_arithmetic_setting)) / sharpness_divisor
    radial = lax.optimization_barrier(jnp.sum(rescaled_document_codes * direction_loss_slope, axis=1))
    grad_pooled = (direction_loss_slope - rescaled_document_codes * radial[:, None]) / euclidean_magnitude[:, None]
    doc_grads = jnp.dot(grad_pooled / DOC_LEN, to_wide(w_out).T, precision=exact_arithmetic_setting).astype(jnp.bfloat16)
    grad_mixture = jnp.broadcast_to(doc_grads[:, None, :], (DOCS, DOC_LEN, QW)).reshape(DOCS, DOC_LEN, HEADS, HD)
    grad_out = jnp.dot(mean_mixture.T, grad_pooled, precision=exact_arithmetic_setting)
    grad_queries, grad_keys, grad_values, grad_ctx_keys, grad_ctx_values = attend_back(grad_mixture, queries, doc_keys, doc_values, ctx_keys, ctx_values, saved)
    ctx_key_rows = grad_ctx_keys.reshape(NCTX, QW)
    ctx_value_rows = grad_ctx_values.reshape(NCTX, QW)
    grad_query = jnp.dot(normed.T, grad_queries.reshape(tokens, QW), preferred_element_type=jnp.float32)
    grad_key = jnp.dot(normed.T, grad_keys.reshape(tokens, QW), preferred_element_type=jnp.float32)
    grad_key = grad_key + jnp.dot(to_wide(ctx_normed).T, ctx_key_rows, precision=exact_arithmetic_setting)
    grad_value = jnp.dot(normed.T, grad_values.reshape(tokens, QW), preferred_element_type=jnp.float32)
    grad_value = grad_value + jnp.dot(to_wide(ctx_normed).T, ctx_value_rows, precision=exact_arithmetic_setting)
    grad_ctx_normed = jnp.dot(ctx_key_rows, to_wide(w_key).T, precision=exact_arithmetic_setting) + jnp.dot(ctx_value_rows, to_wide(w_value).T, precision=exact_arithmetic_setting)
    context_wide = to_wide(context)
    scaled = norm_gain * grad_ctx_normed
    grad_context = ctx_inverse * scaled - context_wide * ctx_inverse ** 3 * lax.optimization_barrier(jnp.mean(context_wide * scaled, axis=1, keepdims=True))
    return (loss, grad_context, grad_query, grad_key, grad_value, grad_out)
```

```python
import jax
import jax.numpy as jnp
from jax import lax
from jax.sharding import Mesh, PartitionSpec as P

HD = 128
DOC_LEN = 64

EPS = 1e-05
TEMPERATURE = 0.05
LOSS_SCALE = 65536.0
EXACT = lax.Precision.HIGHEST

CTX = ("zh", "x")
DP = ("zl", "y", "co")
EVERY = CTX + DP

f32 = jnp.float32
bf16 = jnp.bfloat16


def wide(a):
    return a.astype(f32)


def pieces(a, count):
    out = []
    for _ in range(count):
        head = lax.reduce_precision(a, 8, 7)
        out.append(head.astype(bf16))
        a = a - head
    return out


def dot(a, b):
    return jnp.dot(a, b, preferred_element_type=f32)


def split_dot(a, b, count):
    rows = a.shape[0]
    got = dot(jnp.concatenate(pieces(a, count), axis=0), b)
    return sum(got[i * rows : (i + 1) * rows] for i in reversed(range(count)))


def ein(form, a, b):
    return jnp.einsum(form, a, b, preferred_element_type=f32)


def inverse_rms(a):
    return lax.rsqrt(jnp.mean(a * a, axis=-1, keepdims=True) + EPS)


def spread(block, axis, size):
    copies = jnp.broadcast_to(block[None], (size,) + block.shape)
    return lax.all_to_all(copies, axis, 0, 0)


def probabilities(queries, doc_keys, ctx_keys):
    factor = HD**-0.5
    ctx_exps = jnp.exp(ein("ble,ce->blc", queries, ctx_keys) * factor)
    own_exps = jnp.exp(ein("ble,bme->blm", queries, doc_keys) * factor)
    total = jnp.sum(ctx_exps, -1, keepdims=True) + jnp.sum(own_exps, -1, keepdims=True)
    return ctx_exps / total, own_exps / total


def shards(doc_states, context, gain, w_query, w_key, w_value, w_out, partners):
    n_ctx, n_dp = 16, 16
    tok = doc_states.shape[0]
    feat = doc_states.shape[1]
    docs = tok // DOC_LEN
    width = feat * n_ctx
    swap = [(c * 16 + d, d * 16 + c) for c in range(16) for d in range(16)]
    dp_id = lax.axis_index(DP)
    co_id = lax.axis_index("co")

    own_ctx = wide(context)
    own_ctx_inv = inverse_rms(own_ctx)
    own_ctx_normed = (own_ctx * own_ctx_inv * gain).astype(bf16)
    ctx_normed = lax.all_gather(lax.ppermute(own_ctx_normed, EVERY, swap), DP, axis=0, tiled=True)
    columns = lax.all_gather(lax.ppermute(doc_states, EVERY, swap), CTX, axis=0, tiled=True)

    by_zh = lax.all_gather(doc_states, "zh")
    rows = wide(spread(by_zh, "x", 4).transpose(2, 1, 0, 3).reshape(tok, width))
    doc_inv = inverse_rms(rows)
    normed = (rows * doc_inv * gain).astype(bf16)
    queries = dot(normed, w_query).astype(bf16)
    doc_keys = dot(normed, w_key).astype(bf16)
    doc_values = dot(normed, w_value).astype(bf16)
    ctx_keys = dot(ctx_normed, w_key).astype(bf16)
    ctx_values = dot(ctx_normed, w_value).astype(bf16)
    everyones = lax.all_gather(
        jnp.concatenate([queries, doc_keys, doc_values], axis=1), DP, axis=0, tiled=True
    )

    own_q, own_k, own_v = (a.reshape(docs, DOC_LEN, HD) for a in (queries, doc_keys, doc_values))
    ctx_probs, own_probs = probabilities(own_q, own_k, ctx_keys)
    mixture = ein("blc,ce->ble", ctx_probs.astype(bf16), ctx_values)
    mixture = mixture + ein("blm,bme->ble", own_probs.astype(bf16), own_v)
    mean_mixture = jnp.mean(wide(mixture.astype(bf16)), axis=1)
    branch = split_dot(mean_mixture, w_out, 3)
    branch = lax.psum(lax.psum(branch, "x"), "zh")
    pooled = jnp.mean(rows.reshape(docs, DOC_LEN, width), axis=1) + branch

    extra = jnp.concatenate([doc_inv.reshape(docs, DOC_LEN), wide(partners)[:, None]], axis=1)
    extra = jnp.pad(extra, ((0, 0), (0, HD - extra.shape[1])))
    message = jnp.concatenate([pooled, mean_mixture, extra], axis=1)
    message = spread(message, DP, n_dp).reshape(n_dp * docs, -1)
    pooled = message[:, :width]
    mean_mixture = message[:, width : width + HD]
    doc_inv = message[:, width + HD : width + HD + DOC_LEN]
    partners = message[:, width + HD + DOC_LEN].astype(jnp.int32)
    total = n_dp * docs

    length = jnp.sqrt(jnp.sum(pooled * pooled, axis=1) + 1e-06)
    unit = pooled / length[:, None]
    gram = jnp.dot(pooled, pooled.T, precision=EXACT)
    scores = gram / (length[:, None] * length[None, :]) / TEMPERATURE
    ids = jnp.arange(total, dtype=jnp.int32)
    exps = jnp.where(ids[:, None] != ids[None, :], jnp.exp(scores), 0.0)
    sums = jnp.sum(exps, axis=1)
    chosen = (partners[:, None] == ids[None, :]).astype(f32)
    loss = jnp.mean(jnp.log(sums) - jnp.sum(scores * chosen, axis=1))
    coeff = (exps / sums[:, None] - chosen) / total * LOSS_SCALE
    grad_unit = jnp.dot(coeff + coeff.T, unit, precision=EXACT) / TEMPERATURE
    radial = jnp.sum(unit * grad_unit, axis=1, keepdims=True)
    grad_pooled = (grad_unit - unit * radial) / length[:, None]
    grad_part = lax.dynamic_slice_in_dim(grad_pooled, dp_id * feat, feat, 1)
    grad_out = jnp.dot(mean_mixture.T, grad_part, precision=EXACT)
    grad_mixture = split_dot(grad_pooled / DOC_LEN, w_out.T, 3).astype(bf16)

    factor = HD**-0.5
    all_q, all_k, all_v = (
        everyones[:, i * HD : (i + 1) * HD].reshape(total, DOC_LEN, HD) for i in range(3)
    )
    ctx_probs, own_probs = probabilities(all_q, all_k, ctx_keys)
    ctx_dweights = ein("be,ce->bc", grad_mixture, ctx_values)[:, None, :]
    own_dweights = ein("be,bme->bm", grad_mixture, all_v)[:, None, :]
    inner = jnp.sum(ctx_probs * ctx_dweights, -1, keepdims=True)
    inner = inner + jnp.sum(own_probs * own_dweights, -1, keepdims=True)
    ctx_dscores = (ctx_probs * (ctx_dweights - inner) * factor).astype(bf16)
    own_dscores = (own_probs * (own_dweights - inner) * factor).astype(bf16)
    grad_queries = ein("blc,ce->ble", ctx_dscores, ctx_keys)
    grad_queries = (grad_queries + ein("blm,bme->ble", own_dscores, all_k)).astype(bf16)
    grad_keys = ein("blm,ble->bme", own_dscores, all_q).astype(bf16)
    own_weights = jnp.sum(wide(own_probs.astype(bf16)), axis=1)
    grad_values = (own_weights[:, :, None] * wide(grad_mixture)[:, None, :]).astype(bf16)
    ctx_weights = jnp.sum(wide(ctx_probs.astype(bf16)), axis=1)
    grad_ctx_keys = ein("blc,ble->ce", ctx_dscores, all_q)
    grad_ctx_values = jnp.dot(ctx_weights.T, wide(grad_mixture), precision=EXACT)

    half = width // 2
    key_half = lax.dynamic_slice_in_dim(w_key, co_id * half, half, 0)
    value_half = lax.dynamic_slice_in_dim(w_value, co_id * half, half, 0)
    part = split_dot(grad_ctx_keys, key_half.T, 2) + split_dot(grad_ctx_values, value_half.T, 2)
    part = part.astype(bf16).reshape(4, 4, -1, half).transpose(1, 0, 2, 3)
    part = jnp.sum(wide(lax.all_to_all(part, "x", 0, 0)), axis=0)
    part = jnp.sum(lax.all_to_all(part, "zh", 0, 0), axis=0)
    both = lax.all_gather(part, "co", axis=1, tiled=True)
    scaled = gain * both
    grad_context = own_ctx_inv * scaled - own_ctx * own_ctx_inv**3 * jnp.mean(
        own_ctx * scaled, axis=1, keepdims=True
    )

    gain_part = lax.dynamic_slice_in_dim(gain, dp_id * feat, feat, 0)
    columns = (wide(columns) * doc_inv.reshape(-1, 1) * gain_part).astype(bf16)
    ctx_columns = lax.dynamic_slice_in_dim(ctx_normed, dp_id * feat, feat, 1)
    grads = jnp.concatenate([grad_queries, grad_keys, grad_values], axis=2)
    grads = dot(columns.T, grads.reshape(-1, 3 * HD))
    from_ctx = split_dot(
        jnp.concatenate([grad_ctx_keys, grad_ctx_values], axis=1).T, ctx_columns, 2
    ).T
    grad_query = grads[:, :HD]
    grad_key = grads[:, HD : 2 * HD] + from_ctx[:, :HD]
    grad_value = grads[:, 2 * HD :] + from_ctx[:, HD:]
    return loss, grad_context, grad_query, grad_key, grad_value, grad_out


def solution(mesh):
    split = Mesh(mesh.devices.reshape(4, 4, 2, 4, 2), EVERY)
    in_specs = (
        P(DP, CTX),
        P(CTX, None),
        P(),
        P(None, CTX),
        P(None, CTX),
        P(None, CTX),
        P(CTX, None),
        P(DP),
    )
    out_specs = (P(), P(CTX, None), P(DP, CTX), P(DP, CTX), P(DP, CTX), P(CTX, DP))
    return jax.shard_map(
        shards, mesh=split, in_specs=in_specs, out_specs=out_specs, check_vma=False
    )
```

```python
import jax
import jax.numpy as jnp
from jax import lax
from jax.sharding import Mesh, PartitionSpec as P

HD = 128
DOC_LEN = 64

EPS = 1e-05
TEMPERATURE = 0.05
LOSS_SCALE = 65536.0
EXACT = lax.Precision.HIGHEST

CTX = ("zh", "x")
DP = ("zl", "y", "co")
EVERY = CTX + DP

f32 = jnp.float32
bf16 = jnp.bfloat16


def wide(a):
    return a.astype(f32)


def pieces(a, count):
    out = []
    for _ in range(count):
        head = lax.reduce_precision(a, 8, 7)
        out.append(head.astype(bf16))
        a = a - head
    return out


def dot(a, b):
    return jnp.dot(a, b, preferred_element_type=f32)


def split_dot(a, b, count):
    rows = a.shape[0]
    got = dot(jnp.concatenate(pieces(a, count), axis=0), b)
    return sum(got[i * rows : (i + 1) * rows] for i in reversed(range(count)))


def ein(form, a, b):
    return jnp.einsum(form, a, b, preferred_element_type=f32)


def inverse_rms(a):
    return lax.rsqrt(jnp.mean(a * a, axis=-1, keepdims=True) + EPS)


def spread(block, axis, size):
    copies = jnp.broadcast_to(block[None], (size,) + block.shape)
    return lax.all_to_all(copies, axis, 0, 0)


def probabilities(queries, doc_keys, ctx_keys):
    factor = HD**-0.5
    ctx_exps = jnp.exp(ein("ble,ce->blc", queries, ctx_keys) * factor)
    own_exps = jnp.exp(ein("ble,bme->blm", queries, doc_keys) * factor)
    total = jnp.sum(ctx_exps, -1, keepdims=True) + jnp.sum(own_exps, -1, keepdims=True)
    return ctx_exps / total, own_exps / total


def shards(doc_states, context, gain, w_query, w_key, w_value, w_out, partners):
    n_ctx, n_dp = 16, 16
    tok = doc_states.shape[0]
    feat = doc_states.shape[1]
    docs = tok // DOC_LEN
    width = feat * n_ctx
    swap = [(c * 16 + d, d * 16 + c) for c in range(16) for d in range(16)]
    dp_id = lax.axis_index(DP)
    co_id = lax.axis_index("co")

    own_ctx = wide(context)
    own_ctx_inv = inverse_rms(own_ctx)
    own_ctx_normed = (own_ctx * own_ctx_inv * gain).astype(bf16)
    named_rows = lax.ppermute(own_ctx_normed, EVERY, swap)
    few = jnp.concatenate([dot(named_rows, w_key), dot(named_rows, w_value)], axis=1).astype(bf16)
    few = spread(few, DP, n_dp).reshape(-1, 2 * HD)
    ctx_keys, ctx_values = few[:, :HD], few[:, HD:]
    ctx_part = lax.dynamic_slice_in_dim(own_ctx_normed, dp_id * feat, feat, 1)
    columns = lax.ppermute(doc_states, EVERY, swap)
    columns = lax.all_gather(jnp.concatenate([columns, ctx_part], axis=0), CTX)
    ctx_columns = columns[:, tok:].reshape(-1, feat)
    columns = columns[:, :tok].reshape(-1, feat)

    by_zh = lax.all_gather(doc_states, "zh")
    rows = wide(spread(by_zh, "x", 4).transpose(2, 1, 0, 3).reshape(tok, width))
    doc_inv = inverse_rms(rows)
    normed = (rows * doc_inv * gain).astype(bf16)
    queries = dot(normed, w_query).astype(bf16)
    doc_keys = dot(normed, w_key).astype(bf16)
    doc_values = dot(normed, w_value).astype(bf16)
    everyones = lax.all_gather(
        jnp.concatenate([queries, doc_keys, doc_values], axis=1), DP, axis=0, tiled=True
    )

    own_q, own_k, own_v = (a.reshape(docs, DOC_LEN, HD) for a in (queries, doc_keys, doc_values))
    ctx_probs, own_probs = probabilities(own_q, own_k, ctx_keys)
    mixture = ein("blc,ce->ble", ctx_probs.astype(bf16), ctx_values)
    mixture = mixture + ein("blm,bme->ble", own_probs.astype(bf16), own_v)
    mean_mixture = jnp.mean(wide(mixture.astype(bf16)), axis=1)
    branch = split_dot(mean_mixture, w_out, 3)
    branch = jnp.sum(spread(branch, "x", 4), axis=0)
    branch = jnp.sum(spread(branch, "zh", 4), axis=0)
    pooled = jnp.mean(rows.reshape(docs, DOC_LEN, width), axis=1) + branch

    extra = jnp.concatenate([doc_inv.reshape(docs, DOC_LEN), wide(partners)[:, None]], axis=1)
    extra = jnp.pad(extra, ((0, 0), (0, HD - extra.shape[1])))
    message = jnp.concatenate([pooled, mean_mixture, extra], axis=1)
    message = spread(message, DP, n_dp).reshape(n_dp * docs, -1)
    pooled = message[:, :width]
    mean_mixture = message[:, width : width + HD]
    doc_inv = message[:, width + HD : width + HD + DOC_LEN]
    partners = message[:, width + HD + DOC_LEN].astype(jnp.int32)
    total = n_dp * docs

    length = jnp.sqrt(jnp.sum(pooled * pooled, axis=1) + 1e-06)
    unit = pooled / length[:, None]
    gram = jnp.dot(pooled, pooled.T, precision=EXACT)
    scores = gram / (length[:, None] * length[None, :]) / TEMPERATURE
    ids = jnp.arange(total, dtype=jnp.int32)
    exps = jnp.where(ids[:, None] != ids[None, :], jnp.exp(scores), 0.0)
    sums = jnp.sum(exps, axis=1)
    chosen = (partners[:, None] == ids[None, :]).astype(f32)
    loss = jnp.mean(jnp.log(sums) - jnp.sum(scores * chosen, axis=1))
    coeff = (exps / sums[:, None] - chosen) / total * LOSS_SCALE
    grad_unit = jnp.dot(coeff + coeff.T, unit, precision=EXACT) / TEMPERATURE
    radial = jnp.sum(unit * grad_unit, axis=1, keepdims=True)
    grad_pooled = (grad_unit - unit * radial) / length[:, None]
    grad_part = lax.dynamic_slice_in_dim(grad_pooled, dp_id * feat, feat, 1)
    grad_out = jnp.dot(mean_mixture.T, grad_part, precision=EXACT)
    grad_mixture = split_dot(grad_pooled / DOC_LEN, w_out.T, 3).astype(bf16)

    factor = HD**-0.5
    all_q, all_k, all_v = (
        everyones[:, i * HD : (i + 1) * HD].reshape(total, DOC_LEN, HD) for i in range(3)
    )
    ctx_probs, own_probs = probabilities(all_q, all_k, ctx_keys)
    ctx_dweights = ein("be,ce->bc", grad_mixture, ctx_values)[:, None, :]
    own_dweights = ein("be,bme->bm", grad_mixture, all_v)[:, None, :]
    inner = jnp.sum(ctx_probs * ctx_dweights, -1, keepdims=True)
    inner = inner + jnp.sum(own_probs * own_dweights, -1, keepdims=True)
    ctx_dscores = (ctx_probs * (ctx_dweights - inner) * factor).astype(bf16)
    own_dscores = (own_probs * (own_dweights - inner) * factor).astype(bf16)
    grad_queries = ein("blc,ce->ble", ctx_dscores, ctx_keys)
    grad_queries = (grad_queries + ein("blm,bme->ble", own_dscores, all_k)).astype(bf16)
    grad_keys = ein("blm,ble->bme", own_dscores, all_q).astype(bf16)
    own_weights = jnp.sum(wide(own_probs.astype(bf16)), axis=1)
    grad_values = (own_weights[:, :, None] * wide(grad_mixture)[:, None, :]).astype(bf16)
    ctx_weights = jnp.sum(wide(ctx_probs.astype(bf16)), axis=1)
    grad_ctx_keys = ein("blc,ble->ce", ctx_dscores, all_q)
    grad_ctx_values = jnp.dot(ctx_weights.T, wide(grad_mixture), precision=EXACT)

    half = width // 2
    key_half = lax.dynamic_slice_in_dim(w_key, co_id * half, half, 0)
    value_half = lax.dynamic_slice_in_dim(w_value, co_id * half, half, 0)
    part = split_dot(grad_ctx_keys, key_half.T, 2) + split_dot(grad_ctx_values, value_half.T, 2)
    part = part.astype(bf16).reshape(4, 4, -1, half).transpose(1, 0, 2, 3)
    part = jnp.sum(wide(lax.all_to_all(part, "x", 0, 0)), axis=0)
    part = jnp.sum(lax.all_to_all(part, "zh", 0, 0), axis=0)
    both = lax.all_gather(part, "co", axis=1, tiled=True)
    scaled = gain * both
    grad_context = own_ctx_inv * scaled - own_ctx * own_ctx_inv**3 * jnp.mean(
        own_ctx * scaled, axis=1, keepdims=True
    )

    gain_part = lax.dynamic_slice_in_dim(gain, dp_id * feat, feat, 0)
    columns = (wide(columns) * doc_inv.reshape(-1, 1) * gain_part).astype(bf16)
    grads = jnp.concatenate([grad_queries, grad_keys, grad_values], axis=2)
    grads = dot(columns.T, grads.reshape(-1, 3 * HD))
    from_ctx = split_dot(
        jnp.concatenate([grad_ctx_keys, grad_ctx_values], axis=1).T, ctx_columns, 2
    ).T
    grad_query = grads[:, :HD]
    grad_key = grads[:, HD : 2 * HD] + from_ctx[:, :HD]
    grad_value = grads[:, 2 * HD :] + from_ctx[:, HD:]
    return loss, grad_context, grad_query, grad_key, grad_value, grad_out


def solution(mesh):
    split = Mesh(mesh.devices.reshape(4, 4, 2, 4, 2), EVERY)
    in_specs = (
        P(DP, CTX),
        P(CTX, None),
        P(),
        P(None, CTX),
        P(None, CTX),
        P(None, CTX),
        P(CTX, None),
        P(DP),
    )
    out_specs = (P(), P(CTX, None), P(DP, CTX), P(DP, CTX), P(DP, CTX), P(CTX, DP))
    return jax.shard_map(
        shards, mesh=split, in_specs=in_specs, out_specs=out_specs, check_vma=False
    )
```

```python
import jax
import jax.numpy as jnp
from jax import lax
from jax.sharding import Mesh, PartitionSpec as P

HD = 128
DOC_LEN = 64

EPS = 1e-05
TEMPERATURE = 0.05
LOSS_SCALE = 65536.0
EXACT = lax.Precision.HIGHEST

CTX = ("zh", "x")
DP = ("zl", "y", "co")
EVERY = CTX + DP

f32 = jnp.float32
bf16 = jnp.bfloat16


def wide(a):
    return a.astype(f32)


def pieces(a, count):
    out = []
    for _ in range(count):
        head = lax.reduce_precision(a, 8, 7)
        out.append(head.astype(bf16))
        a = a - head
    return out


def dot(a, b):
    return jnp.dot(a, b, preferred_element_type=f32)


def split_dot(a, b, count):
    rows = a.shape[0]
    got = dot(jnp.concatenate(pieces(a, count), axis=0), b)
    return sum(got[i * rows : (i + 1) * rows] for i in reversed(range(count)))


def ein(form, a, b):
    return jnp.einsum(form, a, b, preferred_element_type=f32)


def inverse_rms(a):
    return lax.rsqrt(jnp.mean(a * a, axis=-1, keepdims=True) + EPS)


def spread(block, axis, size):
    copies = jnp.broadcast_to(block[None], (size,) + block.shape)
    return lax.all_to_all(copies, axis, 0, 0)


def other_of_two(a, axis):
    return lax.ppermute(a, axis, [(0, 1), (1, 0)])


def pair(a, axis):
    b = other_of_two(a, axis)
    return jnp.where(lax.axis_index(axis) == 0, jnp.stack([a, b]), jnp.stack([b, a]))


def ring(a, axis):
    one, two, three = (
        lax.ppermute(a, axis, [(i, (i + k) % 4) for i in range(4)]) for k in (1, 2, 3)
    )
    cycle = jnp.stack([three, two, one, a, three, two, one])
    return lax.dynamic_slice_in_dim(cycle, 3 - lax.axis_index(axis), 4, 0)


def probabilities(queries, doc_keys, ctx_keys):
    factor = HD**-0.5
    ctx_exps = jnp.exp(ein("ble,ce->blc", queries, ctx_keys) * factor)
    own_exps = jnp.exp(ein("ble,bme->blm", queries, doc_keys) * factor)
    total = jnp.sum(ctx_exps, -1, keepdims=True) + jnp.sum(own_exps, -1, keepdims=True)
    return ctx_exps / total, own_exps / total


def shards(doc_states, context, gain, w_query, w_key, w_value, w_out, partners):
    tok, feat = doc_states.shape
    docs = tok // DOC_LEN
    width = w_query.shape[0]
    co_id = lax.axis_index("co")
    chip_id = lax.axis_index(("zl", "y"))
    dp_id = lax.axis_index(DP)

    swap = [(c * 16 + d, d * 16 + c) for c in range(16) for d in range(16)]
    own_ctx = wide(context)
    own_ctx_inv = inverse_rms(own_ctx)
    own_ctx_normed = (own_ctx * own_ctx_inv * gain).astype(bf16)
    named_rows = lax.ppermute(own_ctx_normed, EVERY, swap)
    few = jnp.concatenate([dot(named_rows, w_key), dot(named_rows, w_value)], axis=1).astype(bf16)
    few = ring(pair(pair(few, "co"), "zl"), "y")
    few = few.transpose(1, 0, 2, 3, 4).reshape(-1, 2 * HD)
    ctx_keys, ctx_values = few[:, :HD], few[:, HD:]

    by_zh = lax.all_gather(doc_states, "zh")
    rows = spread(by_zh, "x", 4).transpose(2, 1, 0, 3).reshape(tok, width)
    rows_wide = wide(rows)
    doc_inv = inverse_rms(rows_wide)
    normed = (rows_wide * doc_inv * gain).astype(bf16)
    queries = dot(normed, w_query).astype(bf16)
    doc_keys = dot(normed, w_key).astype(bf16)
    doc_values = dot(normed, w_value).astype(bf16)
    everyones = jnp.concatenate([queries, doc_keys, doc_values], axis=1)
    everyones = ring(pair(everyones, "zl"), "y")

    own_q, own_k, own_v = (a.reshape(docs, DOC_LEN, HD) for a in (queries, doc_keys, doc_values))
    ctx_probs, own_probs = probabilities(own_q, own_k, ctx_keys)
    mixture = ein("blc,ce->ble", ctx_probs.astype(bf16), ctx_values)
    mixture = mixture + ein("blm,bme->ble", own_probs.astype(bf16), own_v)
    averaging = (jnp.arange(tok)[None, :] // DOC_LEN == jnp.arange(docs)[:, None]).astype(bf16)
    averaging = averaging * jnp.asarray(1 / DOC_LEN, bf16)
    mean_mixture = dot(averaging, mixture.astype(bf16).reshape(tok, HD))
    branch = split_dot(mean_mixture, w_out, 3)
    branch = jnp.sum(spread(branch, "x", 4), axis=0)
    branch = jnp.sum(spread(branch, "zh", 4), axis=0)
    pooled = dot(averaging, rows) + branch

    extra = jnp.concatenate([doc_inv.reshape(docs, DOC_LEN), wide(partners)[:, None]], axis=1)
    extra = jnp.pad(extra, ((0, 0), (0, HD - extra.shape[1])))
    message = jnp.concatenate([pooled, mean_mixture, extra], axis=1)
    message = pair(spread(message, ("zl", "y"), 8), "co")
    side = 8 * docs
    total = 2 * side
    message = message.reshape(total, -1)
    pooled = message[:, :width]
    mean_mixture = message[:, width : width + HD]
    doc_inv = message[:, width + HD : width + HD + DOC_LEN]
    partners = message[:, width + HD + DOC_LEN].astype(jnp.int32)
    place = jnp.arange(total, dtype=jnp.int32)
    ids = ((place % side) // docs * 2 + place // side) * docs + place % docs

    length = jnp.sqrt(jnp.sum(pooled * pooled, axis=1) + 1e-06)
    unit = pooled / length[:, None]
    gram = jnp.dot(pooled, pooled.T, precision=EXACT)
    scores = gram / (length[:, None] * length[None, :]) / TEMPERATURE
    exps = jnp.where(ids[:, None] != ids[None, :], jnp.exp(scores), 0.0)
    sums = jnp.sum(exps, axis=1)
    chosen = (partners[:, None] == ids[None, :]).astype(f32)
    loss = jnp.mean(jnp.log(sums) - jnp.sum(scores * chosen, axis=1))
    coeff = (exps / sums[:, None] - chosen) / total * LOSS_SCALE
    grad_unit = jnp.dot(coeff + coeff.T, unit, precision=EXACT) / TEMPERATURE
    radial = jnp.sum(unit * grad_unit, axis=1, keepdims=True)
    grad_pooled = (grad_unit - unit * radial) / length[:, None]
    grad_part = lax.dynamic_slice_in_dim(grad_pooled, dp_id * feat, feat, 1)
    grad_out = jnp.dot(mean_mixture.T, grad_part, precision=EXACT)
    grad_side = lax.dynamic_slice_in_dim(grad_pooled, co_id * side, side, 0)
    grad_mixture = split_dot(grad_side / DOC_LEN, w_out.T, 3).astype(bf16)
    doc_inv = lax.dynamic_slice_in_dim(doc_inv, co_id * side, side, 0)

    factor = HD**-0.5
    everyones = everyones.transpose(1, 0, 2, 3).reshape(side * DOC_LEN, 3 * HD)
    all_q, all_k, all_v = (
        everyones[:, i * HD : (i + 1) * HD].reshape(side, DOC_LEN, HD) for i in range(3)
    )
    ctx_probs, own_probs = probabilities(all_q, all_k, ctx_keys)
    ctx_dweights = ein("be,ce->bc", grad_mixture, ctx_values)[:, None, :]
    own_dweights = ein("be,bme->bm", grad_mixture, all_v)[:, None, :]
    inner = jnp.sum(ctx_probs * ctx_dweights, -1, keepdims=True)
    inner = inner + jnp.sum(own_probs * own_dweights, -1, keepdims=True)
    ctx_dscores = (ctx_probs * (ctx_dweights - inner) * factor).astype(bf16)
    own_dscores = (own_probs * (own_dweights - inner) * factor).astype(bf16)
    own_weights = jnp.sum(wide(own_probs.astype(bf16)), axis=1)
    ctx_weights = jnp.sum(wide(ctx_probs.astype(bf16)), axis=1)
    grad_ctx_keys = ein("blc,ble->ce", ctx_dscores, all_q)
    grad_ctx_values = jnp.dot(ctx_weights.T, wide(grad_mixture), precision=EXACT)
    grad_ctx = jnp.concatenate([grad_ctx_keys, grad_ctx_values], axis=1)
    grad_ctx = grad_ctx + other_of_two(grad_ctx, "co")
    grad_queries = ein("blc,ce->ble", ctx_dscores, ctx_keys)
    grad_queries = (grad_queries + ein("blm,bme->ble", own_dscores, all_k)).astype(bf16)
    grad_keys = ein("blm,ble->bme", own_dscores, all_q).astype(bf16)
    grad_values = (own_weights[:, :, None] * wide(grad_mixture)[:, None, :]).astype(bf16)

    half = width // 2
    key_half = lax.dynamic_slice_in_dim(w_key, co_id * half, half, 0)
    value_half = lax.dynamic_slice_in_dim(w_value, co_id * half, half, 0)
    part = split_dot(grad_ctx[:, :HD], key_half.T, 2) + split_dot(grad_ctx[:, HD:], value_half.T, 2)
    part = lax.all_to_all(part.astype(bf16).reshape(16, -1, half), CTX, 0, 0)
    part = pair(jnp.sum(wide(part), axis=0), "co")
    scaled = gain * part.transpose(1, 0, 2).reshape(-1, width)
    grad_context = own_ctx_inv * scaled - own_ctx * own_ctx_inv**3 * jnp.mean(
        own_ctx * scaled, axis=1, keepdims=True
    )

    turn = [
        (((cy * 2 + s) * 16 + dy * 2 + k), ((dy * 2 + s) * 16 + cy * 2 + k))
        for cy in range(8)
        for dy in range(8)
        for s in range(2)
        for k in range(2)
    ]
    columns = lax.ppermute(doc_states, EVERY, turn)
    ctx_part = lax.dynamic_slice_in_dim(own_ctx_normed, dp_id * feat, feat, 1)
    columns = jnp.concatenate([columns, ctx_part], axis=0)
    columns, branch = lax.optimization_barrier((columns, branch))
    columns = ring(ring(columns, "zh"), "x").transpose(1, 0, 2, 3).reshape(16, -1, feat)
    ctx_columns = columns[:, tok:].reshape(-1, feat)
    gain_part = lax.dynamic_slice_in_dim(gain, chip_id * 2 * feat, 2 * feat, 0)
    columns = wide(columns[:, :tok]).reshape(8, 2, tok, feat) * doc_inv.reshape(8, 1, tok, 1)
    columns = (columns * gain_part.reshape(1, 2, 1, feat)).astype(bf16)
    columns = columns.transpose(0, 2, 1, 3).reshape(8 * tok, 2 * feat)
    grads = jnp.concatenate([grad_queries, grad_keys, grad_values], axis=2)
    grads = dot(columns.T, grads.reshape(8 * tok, 3 * HD)).reshape(2, feat, 3 * HD)
    mine = lax.dynamic_index_in_dim(grads, co_id, 0, keepdims=False)
    theirs = lax.dynamic_index_in_dim(grads, 1 - co_id, 0, keepdims=False)
    grads = mine + other_of_two(theirs, "co")
    from_ctx = split_dot(grad_ctx.T, ctx_columns, 2).T
    grad_query = grads[:, :HD]
    grad_key = grads[:, HD : 2 * HD] + from_ctx[:, :HD]
    grad_value = grads[:, 2 * HD :] + from_ctx[:, HD:]
    return loss, grad_context, grad_query, grad_key, grad_value, grad_out


def solution(mesh):
    split = Mesh(mesh.devices.reshape(4, 4, 2, 4, 2), EVERY)
    in_specs = (
        P(DP, CTX),
        P(CTX, None),
        P(),
        P(None, CTX),
        P(None, CTX),
        P(None, CTX),
        P(CTX, None),
        P(DP),
    )
    out_specs = (P(), P(CTX, None), P(DP, CTX), P(DP, CTX), P(DP, CTX), P(CTX, DP))
    return jax.shard_map(
        shards, mesh=split, in_specs=in_specs, out_specs=out_specs, check_vma=False
    )
```

```python
import jax
import jax.numpy as jnp
from jax import lax
from jax.experimental import pallas as pl
from jax.experimental.pallas import tpu as pltpu
from jax.sharding import Mesh, PartitionSpec as P

HD = 128
DOC_LEN = 64

EPS = 1e-05
TEMPERATURE = 0.05
LOSS_SCALE = 65536.0
EXACT = lax.Precision.HIGHEST
FACTOR = HD**-0.5

CTX = ("zh", "x")
DP = ("zl", "y", "co")
EVERY = CTX + DP

f32 = jnp.float32
bf16 = jnp.bfloat16

ROWS_BY_ROWS = (((1,), (1,)), ((), ()))
COLS_BY_COLS = (((0,), (0,)), ((), ()))


def wide(a):
    return a.astype(f32)


def dot(a, b):
    return jnp.dot(a, b, preferred_element_type=f32)


def dot_nt(a, b, precision=None):
    return lax.dot_general(a, b, ROWS_BY_ROWS, precision=precision, preferred_element_type=f32)


def dot_tn(a, b, precision=None):
    return lax.dot_general(a, b, COLS_BY_COLS, precision=precision, preferred_element_type=f32)


def stacked_pieces(a, count):
    out = []
    for _ in range(count):
        head = a.astype(bf16)
        out.append(head)
        a = a - wide(head)
    return jnp.concatenate(out, axis=0)


def folded(a, count):
    rows = a.shape[0] // count
    return sum(a[i * rows : (i + 1) * rows] for i in reversed(range(count)))


def iota(shape, axis):
    return lax.broadcasted_iota(jnp.int32, shape, axis)


def as_row(column):
    n = column.shape[0]
    return jnp.sum(jnp.where(iota((n, n), 0) == iota((n, n), 1), column, 0.0), 0, keepdims=True)


def as_column(row):
    n = row.shape[1]
    return jnp.sum(jnp.where(iota((n, n), 0) == iota((n, n), 1), row, 0.0), 1, keepdims=True)


def inverse_rms(a):
    return lax.rsqrt(jnp.mean(a * a, axis=-1, keepdims=True) + EPS)


def probabilities(q, k, ctx_keys):
    n = q.shape[0]
    same = iota((n, n), 0) // DOC_LEN == iota((n, n), 1) // DOC_LEN
    ctx_exps = jnp.exp(dot_nt(q, ctx_keys) * FACTOR)
    own_exps = jnp.where(same, jnp.exp(dot_nt(q, k) * FACTOR), 0.0)
    total = jnp.sum(ctx_exps, 1, keepdims=True) + jnp.sum(own_exps, 1, keepdims=True)
    return ctx_exps / total, own_exps / total


def call(kernel, out_shape, in_specs, scratch=(), vmem=40, flops=10**9):
    in_specs = [
        pl.BlockSpec(memory_space=pltpu.SMEM if s == "s" else pltpu.VMEM) for s in in_specs
    ]
    return pl.pallas_call(
        kernel,
        out_shape=out_shape,
        in_specs=in_specs,
        out_specs=jax.tree.map(lambda _: pl.BlockSpec(memory_space=pltpu.VMEM), out_shape),
        scratch_shapes=scratch,
        compiler_params=pltpu.CompilerParams(vmem_limit_bytes=vmem * 2**20),
        cost_estimate=pl.CostEstimate(flops=flops, bytes_accessed=4 * 10**6, transcendentals=0),
    )


def shape(*dims, dtype=f32):
    return jax.ShapeDtypeStruct(dims, dtype)


def forward_kernel(pos, gain, wq, wk, wv, wo, ctx, *refs):
    blocks, (qkv, own, branch, mix, inv_row) = refs[:16], refs[16:]
    tok, feat = blocks[0].shape
    docs = tok // DOC_LEN
    averaging = jnp.where(iota((8, tok), 0) == iota((8, tok), 1) // DOC_LEN, 1 / DOC_LEN, 0.0)
    averaging = averaging.astype(bf16)
    squares = jnp.zeros((tok, 1), f32)
    for block in blocks:
        rows = wide(block[...])
        squares = squares + jnp.sum(rows * rows, axis=1, keepdims=True)
    inv = lax.rsqrt(squares / (16 * feat) + EPS)
    inv_row[...] = as_row(inv)
    total = jnp.zeros((tok, 3 * HD), f32)
    for i, block in enumerate(blocks):
        place = ((pos[0] - i % 4) & 3) * 4 + ((pos[1] - i // 4) & 3)
        here = pl.ds(pl.multiple_of(place * feat, feat), feat)
        rows = block[...]
        normed = (wide(rows) * inv * gain[:, here]).astype(bf16)
        weights = jnp.concatenate([wq[here, :], wk[here, :], wv[here, :]], axis=1)
        total = total + dot(normed, weights)
        own[:, here] = dot(averaging, rows)[:docs]
    total = total.astype(bf16)
    qkv[...] = total
    q, k, v = total[:, :HD], total[:, HD : 2 * HD], total[:, 2 * HD :]
    ctx_probs, own_probs = probabilities(q, k, ctx[:, :HD])
    mixture = dot(ctx_probs.astype(bf16), ctx[:, HD:]) + dot(own_probs.astype(bf16), v)
    mean = dot(averaging, mixture.astype(bf16))
    mix[...] = mean[:docs]
    branch[...] = folded(dot(stacked_pieces(mean, 3), wo[...]), 3)[:docs]


def loss_kernel(pos, wo, *refs):
    messages = refs[:8]
    loss, grad_mixture, grad_out, inv, pooled, mix, extra, slope = refs[8:]
    width = wo.shape[1]
    co, y, dp = pos[4], pos[3], (pos[2] * 4 + pos[3]) * 2 + pos[4]
    for i, message in enumerate(messages):
        core = co if i < 4 else 1 - co
        line = (y - i % 4) & 3
        here = pl.ds(pl.multiple_of((core * 4 + line) * 8, 8), 8)
        pooled[here, :] = message[:, :width]
        mix[here, :] = message[:, width : width + HD]
        extra[here, :] = message[:, width + HD : width + 2 * HD]
        if i < 4:
            inv[line] = message[:, width + 2 * HD :]
    n = pooled.shape[0]
    vectors = pooled[...]
    length = jnp.sqrt(jnp.sum(vectors * vectors, axis=1, keepdims=True) + 1e-06)
    unit = vectors / length
    gram = dot_nt(vectors, vectors, EXACT)
    scores = gram / (length * as_row(length)) / TEMPERATURE
    diagonal = iota((n, n), 0) == iota((n, n), 1)

    def document(axis):
        at = iota((n, n), axis)
        return (((at >> 2) & 1) * 32 + ((at >> 3) & 3) * 8 + (at >> 5) * 4 + (at & 3)).astype(f32)

    partners = extra[:, 0:1]
    chosen = jnp.where(partners == document(1), 1.0, 0.0)
    chosen_back = jnp.where(as_row(partners) == document(0), 1.0, 0.0)
    exps = jnp.where(diagonal, 0.0, jnp.exp(scores))
    sums = jnp.sum(exps, axis=1, keepdims=True)
    picked = jnp.sum(scores * chosen, axis=1, keepdims=True)
    loss[...] = jnp.sum(jnp.log(sums) - picked, axis=0, keepdims=True) / n
    coeff = (exps / sums - chosen) / n * LOSS_SCALE
    coeff_back = (exps / as_row(sums) - chosen_back) / n * LOSS_SCALE
    grad_unit = jnp.dot(coeff + coeff_back, unit, precision=EXACT, preferred_element_type=f32)
    grad_unit = grad_unit / TEMPERATURE
    radial = jnp.sum(unit * grad_unit, axis=1, keepdims=True)
    slope[...] = (grad_unit - unit * radial) / length
    part = slope[:, pl.ds(pl.multiple_of(dp * (width // 16), width // 16), width // 16)]
    grad_out[...] = dot_tn(mix[...], part, EXACT)
    side = slope[pl.ds(pl.multiple_of(co * (n // 2), 8), n // 2), :] / DOC_LEN
    grad_mixture[...] = folded(dot_nt(stacked_pieces(side, 3), wo[...]), 3).astype(bf16)


def backward_kernel(pos, ctx, grad_mixture, *refs):
    pieces, (grads, grad_ctx, partial) = refs[:8], refs[8:]
    tok = pieces[0].shape[0]
    ctx_keys, ctx_values = ctx[:, :HD], ctx[:, HD:]
    upstream = grad_mixture[...]
    for i, piece in enumerate(pieces):
        chip = ((pos[3] - i % 4) & 3) * 2 + (pos[2] if i < 4 else 1 - pos[2])
        q, k, v = (piece[:, j * HD : (j + 1) * HD] for j in range(3))
        ctx_probs, own_probs = probabilities(q, k, ctx_keys)
        docs = iota((tok, upstream.shape[0]), 0) // DOC_LEN + chip * (tok // DOC_LEN)
        pick = jnp.where(docs == iota((tok, upstream.shape[0]), 1), 1.0, 0.0).astype(bf16)
        gm = dot(pick, upstream).astype(bf16)
        ctx_dweights, own_dweights = dot_nt(gm, ctx_values), dot_nt(gm, v)
        inner = jnp.sum(ctx_probs * ctx_dweights, 1, keepdims=True)
        inner = inner + jnp.sum(own_probs * own_dweights, 1, keepdims=True)
        ctx_dscores = (ctx_probs * (ctx_dweights - inner) * FACTOR).astype(bf16)
        own_dscores = (own_probs * (own_dweights - inner) * FACTOR).astype(bf16)
        grad_q = dot(ctx_dscores, ctx_keys) + dot(own_dscores, k)
        grad_k = dot_tn(own_dscores, q)
        grad_v = dot_tn(own_probs.astype(bf16), gm)
        grads[chip] = jnp.concatenate([grad_q, grad_k, grad_v], axis=1).astype(bf16)
        partial[chip] = jnp.concatenate(
            [dot_tn(ctx_dscores, q), dot_tn(ctx_probs.astype(bf16), gm)], axis=1
        )
    grad_ctx[...] = sum(partial[i] for i in range(8))


def context_kernel(pos, one, two, wk, wv, total, out0, out1, out2, out3, part):
    half = part.shape[1]
    grad = one[...] + two[...]
    total[...] = grad
    here = pl.ds(pl.multiple_of(pos[4] * half, half), half)
    got = dot_nt(stacked_pieces(grad[:, :HD], 2), wk[here, :])
    got = got + dot_nt(stacked_pieces(grad[:, HD:], 2), wv[here, :])
    part[...] = folded(got, 2)
    for k, out in enumerate((out0, out1, out2, out3)):
        at = (pos[1] + k) & 3
        rows = [part[pl.ds(pl.multiple_of(z * 32 + at * 8, 8), 8), :] for z in range(4)]
        out[...] = jnp.concatenate(rows, axis=0).astype(out.dtype)


def middle_kernel(pos, own, one, two, three, out0, out1, out2, out3, total):
    total[...] = (own[...] + wide(two[...])) + (wide(one[...]) + wide(three[...]))
    for k, out in enumerate((out0, out1, out2, out3)):
        at = (pos[0] + k) & 3
        out[...] = total[pl.ds(pl.multiple_of(at * 8, 8), 8), :]


def finish_kernel(pos, context, gain, mine, theirs, out):
    half = mine.shape[1]
    low = pos[4] == 0
    grad = jnp.concatenate(
        [jnp.where(low, mine[...], theirs[...]), jnp.where(low, theirs[...], mine[...])], axis=1
    )
    rows = wide(context[...])
    inv = inverse_rms(rows)
    scaled = gain[...] * grad
    out[...] = inv * scaled - rows * inv**3 * jnp.mean(rows * scaled, axis=1, keepdims=True)


def weight_kernel(pos, gain, inv, grads, grad_ctx, *refs):
    columns, (mine, theirs, total, ctx_columns) = refs[:4], refs[4:]
    feat = columns[0].shape[2]
    tok = grads.shape[1]
    chip_here = pos[2] * 4 + pos[3]
    total[...] = jnp.zeros_like(total)
    for i in range(16):
        place = ((pos[0] - i % 4) & 3) * 4 + ((pos[1] - i // 4) & 3)
        s = place & 1
        zl, y = place >> 3, (place >> 1) & 3
        block = columns[i // 4][i % 4]
        inv_row = jnp.where(iota((8, tok), 0) == zl * 4, inv[y], 0.0)
        inv_column = as_column(jnp.sum(inv_row, axis=0, keepdims=True))
        here = pl.ds(pl.multiple_of((chip_here * 2 + s) * feat, feat), feat)
        normed = (wide(block[:tok]) * inv_column * gain[:, here]).astype(bf16)
        total[s] = total[s] + dot_tn(normed, grads[y * 2 + zl])
        ctx_columns[pl.ds(pl.multiple_of(place * 8, 8), 8), :] = wide(block[tok:])[:8]
    ctx = ctx_columns[...].astype(bf16)
    grad = grad_ctx[...]
    head = grad.astype(bf16)
    rest = (grad - wide(head)).astype(bf16)
    from_ctx = dot_tn(ctx, rest) + dot_tn(ctx, head)
    theirs[...] = total[1 - pos[4]]
    mine[:, :HD] = total[pos[4], :, :HD]
    mine[:, HD:] = total[pos[4], :, HD:] + from_ctx


def shift(a, axis, k):
    return lax.ppermute(a, axis, [(i, (i + k) % 4) for i in range(4)])


def others(a, axis):
    return [shift(a, axis, k) for k in (1, 2, 3)]


def other(a, axis):
    return lax.ppermute(a, axis, [(0, 1), (1, 0)])


def pair(a, axis):
    b = other(a, axis)
    first = lax.axis_index(axis) == 0
    return jnp.where(first, jnp.concatenate([a, b]), jnp.concatenate([b, a]))


def ring_sum(a, axis):
    one, two, three = others(a, axis)
    return (a + two) + (one + three)


def shards(doc_states, context, gain, w_query, w_key, w_value, w_out, partners):
    tok, feat = doc_states.shape
    docs = tok // DOC_LEN
    width = w_query.shape[0]
    dp_id = lax.axis_index(DP)
    pos = jnp.stack([lax.axis_index(a) for a in EVERY]).astype(jnp.int32)
    gain_row = gain.reshape(1, width)

    by_zh = [doc_states] + others(doc_states, "zh")
    right = [shift(a, "x", 1) for a in by_zh]
    left = [shift(a, "x", 3) for a in by_zh]
    far = [shift(a, "x", 1) for a in right[:2]] + [shift(a, "x", 3) for a in left[2:]]
    blocks = by_zh + right + far + left

    swap = [(c * 16 + d, d * 16 + c) for c in range(16) for d in range(16)]
    own_ctx = wide(context)
    own_ctx_normed = (own_ctx * inverse_rms(own_ctx) * gain).astype(bf16)
    named_rows = lax.ppermute(own_ctx_normed, EVERY, swap)
    few = jnp.concatenate([dot(named_rows, w_key), dot(named_rows, w_value)], axis=1).astype(bf16)
    few = pair(few, "co")
    one, two, three = others(few, "y")
    few = lax.dynamic_slice_in_dim(
        jnp.stack([three, two, one, few, three, two, one]), 3 - lax.axis_index("y"), 4, 0
    )
    ctx_kv = pair(few.reshape(-1, 2 * HD), "zl")

    qkv, own_mean, branch, mix, inv_row = call(
        forward_kernel,
        (
            shape(tok, 3 * HD, dtype=bf16),
            shape(docs, width),
            shape(docs, width),
            shape(docs, HD),
            shape(1, tok),
        ),
        ["s"] + ["v"] * 22,
    )(pos, gain_row, w_query, w_key, w_value, w_out, ctx_kv, *blocks)

    qkv_zl = other(qkv, "zl")
    pieces = [qkv] + others(qkv, "y") + [qkv_zl] + others(qkv_zl, "y")

    pooled = own_mean + ring_sum(ring_sum(branch, "x"), "zh")
    message = jnp.concatenate(
        [
            pooled,
            mix,
            jnp.pad(wide(partners)[:, None], ((0, 0), (0, HD - 1))),
            jnp.pad(inv_row, ((0, docs - 1), (0, 0))),
        ],
        axis=1,
    )
    message = pair(message, "zl")
    messages = [message] + others(message, "y")
    messages = messages + [other(m, "co") for m in messages]
    total = 64
    loss, grad_mixture, grad_out, inv = call(
        loss_kernel,
        (
            shape(1, 1),
            shape(total // 2, HD, dtype=bf16),
            shape(HD, feat),
            shape(4, 8, tok),
        ),
        ["s"] + ["v"] * 9,
        scratch=[
            pltpu.VMEM((total, width), f32),
            pltpu.VMEM((total, HD), f32),
            pltpu.VMEM((total, HD), f32),
            pltpu.VMEM((total, width), f32),
        ],
    )(pos, w_out, *messages)

    grads, grad_ctx = call(
        backward_kernel,
        (shape(8, tok, 3 * HD, dtype=bf16), shape(HD, 2 * HD)),
        ["s"] + ["v"] * 10,
        scratch=[pltpu.VMEM((8, HD, 2 * HD), f32)],
    )(pos, ctx_kv, grad_mixture, *pieces)

    half = width // 2
    rows = 4 * context.shape[0]
    grad_ctx, part, *sent = call(
        context_kernel,
        (shape(HD, 2 * HD), shape(rows, half)) + (shape(rows, half, dtype=bf16),) * 3,
        ["s"] + ["v"] * 4,
        scratch=[pltpu.VMEM((4 * rows, half), f32)],
    )(pos, grad_ctx, other(grad_ctx, "co"), w_key, w_value)
    came = [shift(a, "x", k) for k, a in zip((1, 2, 3), sent)]
    part, *sent = call(
        middle_kernel,
        (shape(rows // 4, half),) * 4,
        ["s"] + ["v"] * 4,
        scratch=[pltpu.VMEM((rows, half), f32)],
    )(pos, part, *came)
    one, two, three = [shift(a, "zh", k) for k, a in zip((1, 2, 3), sent)]
    part = (part + two) + (one + three)
    grad_context = call(finish_kernel, shape(*context.shape), ["s"] + ["v"] * 4)(
        pos, context, gain_row, part, other(part, "co")
    )

    turn = [
        ((cy * 2 + s) * 16 + dy * 2 + k, (dy * 2 + s) * 16 + cy * 2 + k)
        for cy in range(8)
        for dy in range(8)
        for s in range(2)
        for k in range(2)
    ]
    doc_states, _ = lax.optimization_barrier((doc_states, qkv))
    columns = lax.ppermute(doc_states, EVERY, turn)
    ctx_part = lax.dynamic_slice_in_dim(own_ctx_normed, dp_id * feat, feat, 1)
    columns = jnp.concatenate([columns, ctx_part, jnp.zeros_like(ctx_part)], axis=0)
    columns = jnp.stack([columns] + others(columns, "zh"))
    columns = [columns] + others(columns, "x")
    mine, theirs = call(
        weight_kernel,
        (shape(feat, 3 * HD),) * 2,
        ["s"] + ["v"] * 8,
        scratch=[pltpu.VMEM((2, feat, 3 * HD), f32), pltpu.VMEM((HD, feat), f32)],
    )(pos, gain_row, inv, grads, grad_ctx, *columns)
    mine = mine + other(theirs, "co")
    grad_query, grad_key, grad_value = (mine[:, i * HD : (i + 1) * HD] for i in range(3))
    return loss.reshape(()), grad_context, grad_query, grad_key, grad_value, grad_out


def solution(mesh):
    split = Mesh(mesh.devices.reshape(4, 4, 2, 4, 2), EVERY)
    in_specs = (
        P(DP, CTX),
        P(CTX, None),
        P(),
        P(None, CTX),
        P(None, CTX),
        P(None, CTX),
        P(CTX, None),
        P(DP),
    )
    out_specs = (P(), P(CTX, None), P(DP, CTX), P(DP, CTX), P(DP, CTX), P(CTX, DP))
    return jax.shard_map(
        shards, mesh=split, in_specs=in_specs, out_specs=out_specs, check_vma=False
    )
```

```python
import jax
import jax.numpy as jnp
from jax import lax
from jax.experimental import pallas as pl
from jax.experimental.pallas import tpu as pltpu
from jax.sharding import Mesh, PartitionSpec as P

HD = 128
DOC_LEN = 64

EPS = 1e-05
TEMPERATURE = 0.05
LOSS_SCALE = 65536.0
EXACT = lax.Precision.HIGHEST
FACTOR = HD**-0.5

CTX = ("zh", "x")
DP = ("zl", "y", "co")
EVERY = CTX + DP

f32 = jnp.float32
bf16 = jnp.bfloat16

ROWS_BY_ROWS = (((1,), (1,)), ((), ()))
COLS_BY_COLS = (((0,), (0,)), ((), ()))


def wide(a):
    return a.astype(f32)


def dot(a, b):
    return jnp.dot(a, b, preferred_element_type=f32)


def dot_nt(a, b, precision=None):
    return lax.dot_general(a, b, ROWS_BY_ROWS, precision=precision, preferred_element_type=f32)


def dot_tn(a, b, precision=None):
    return lax.dot_general(a, b, COLS_BY_COLS, precision=precision, preferred_element_type=f32)


def stacked_pieces(a, count):
    out = []
    for _ in range(count):
        head = a.astype(bf16)
        out.append(head)
        a = a - wide(head)
    return jnp.concatenate(out, axis=0)


def folded(a, count):
    rows = a.shape[0] // count
    return sum(a[i * rows : (i + 1) * rows] for i in reversed(range(count)))


def iota(shape, axis):
    return lax.broadcasted_iota(jnp.int32, shape, axis)


def as_row(column):
    n = column.shape[0]
    return jnp.sum(jnp.where(iota((n, n), 0) == iota((n, n), 1), column, 0.0), 0, keepdims=True)


def inverse_rms(a):
    return lax.rsqrt(jnp.mean(a * a, axis=-1, keepdims=True) + EPS)


def probabilities(q, k, ctx_keys):
    n = q.shape[0]
    same = iota((n, n), 0) // DOC_LEN == iota((n, n), 1) // DOC_LEN
    ctx_exps = jnp.exp(dot_nt(q, ctx_keys) * FACTOR)
    own_exps = jnp.where(same, jnp.exp(dot_nt(q, k) * FACTOR), 0.0)
    total = jnp.sum(ctx_exps, 1, keepdims=True) + jnp.sum(own_exps, 1, keepdims=True)
    return ctx_exps / total, own_exps / total


def call(kernel, out_shape, in_specs, scratch=(), vmem=40, flops=10**9):
    in_specs = [
        pl.BlockSpec(memory_space=pltpu.SMEM if s == "s" else pltpu.VMEM) for s in in_specs
    ]
    return pl.pallas_call(
        kernel,
        out_shape=out_shape,
        in_specs=in_specs,
        out_specs=jax.tree.map(lambda _: pl.BlockSpec(memory_space=pltpu.VMEM), out_shape),
        scratch_shapes=scratch,
        compiler_params=pltpu.CompilerParams(vmem_limit_bytes=vmem * 2**20),
        cost_estimate=pl.CostEstimate(flops=flops, bytes_accessed=4 * 10**6, transcendentals=0),
    )


def shape(*dims, dtype=f32):
    return jax.ShapeDtypeStruct(dims, dtype)


def forward_kernel(pos, gain, wq, wk, wv, wo, ctx, here0, right, left, far0, far1, *refs):
    qkv, own, branch, mix, normed = refs
    blocks = [(here0, i, 0, i) for i in range(4)] + [(right, i, 1, i) for i in range(4)]
    blocks += [(left, i, 3, i) for i in range(4)]
    blocks += [(far0, i, 2, i) for i in range(2)] + [(far1, i, 2, i + 2) for i in range(2)]
    tok, feat = here0.shape[1:]
    docs = tok // DOC_LEN
    averaging = jnp.where(iota((8, tok), 0) == iota((8, tok), 1) // DOC_LEN, 1 / DOC_LEN, 0.0)
    averaging = averaging.astype(bf16)
    squares = jnp.zeros((tok, 1), f32)
    for ref, i, _, _ in blocks:
        rows = wide(ref[i])
        squares = squares + jnp.sum(rows * rows, axis=1, keepdims=True)
    inv = lax.rsqrt(squares / (16 * feat) + EPS)
    total = jnp.zeros((tok, 3 * HD), f32)
    for ref, i, along_x, along_z in blocks:
        place = ((pos[0] - along_z) & 3) * 4 + ((pos[1] - along_x) & 3)
        here = pl.ds(pl.multiple_of(place * feat, feat), feat)
        rows = ref[i]
        ready = (wide(rows) * inv * gain[:, here]).astype(bf16)
        normed[:, here] = ready
        weights = jnp.concatenate([wq[here, :], wk[here, :], wv[here, :]], axis=1)
        total = total + dot(ready, weights)
        own[:, here] = dot(averaging, rows)[:docs]
    total = total.astype(bf16)
    qkv[...] = total
    q, k, v = total[:, :HD], total[:, HD : 2 * HD], total[:, 2 * HD :]
    ctx_probs, own_probs = probabilities(q, k, ctx[:, :HD])
    mixture = dot(ctx_probs.astype(bf16), ctx[:, HD:]) + dot(own_probs.astype(bf16), v)
    mean = dot(averaging, mixture.astype(bf16))
    mix[...] = mean[:docs]
    branch[...] = folded(dot(stacked_pieces(mean, 3), wo[...]), 3)[:docs]


def loss_kernel(pos, wo, mine, theirs, loss, grad_mixture, grad_out, pooled, mix, extra, slope):
    width = wo.shape[1]
    co, y, dp = pos[4], pos[3], (pos[2] * 4 + pos[3]) * 2 + pos[4]
    for i in range(8):
        messages, core = (mine, co) if i < 4 else (theirs, 1 - co)
        here = pl.ds(pl.multiple_of((core * 4 + ((y - i % 4) & 3)) * 8, 8), 8)
        pooled[here, :] = messages[i % 4, :, :width]
        mix[here, :] = messages[i % 4, :, width : width + HD]
        extra[here, :] = messages[i % 4, :, width + HD :]
    n = pooled.shape[0]
    vectors = pooled[...]
    length = jnp.sqrt(jnp.sum(vectors * vectors, axis=1, keepdims=True) + 1e-06)
    unit = vectors / length
    gram = dot_nt(vectors, vectors, EXACT)
    scores = gram / (length * as_row(length)) / TEMPERATURE
    diagonal = iota((n, n), 0) == iota((n, n), 1)

    def document(axis):
        at = iota((n, n), axis)
        return (((at >> 2) & 1) * 32 + ((at >> 3) & 3) * 8 + (at >> 5) * 4 + (at & 3)).astype(f32)

    partners = extra[:, 0:1]
    chosen = jnp.where(partners == document(1), 1.0, 0.0)
    chosen_back = jnp.where(as_row(partners) == document(0), 1.0, 0.0)
    exps = jnp.where(diagonal, 0.0, jnp.exp(scores))
    sums = jnp.sum(exps, axis=1, keepdims=True)
    picked = jnp.sum(scores * chosen, axis=1, keepdims=True)
    loss[...] = jnp.sum(jnp.log(sums) - picked, axis=0, keepdims=True) / n
    coeff = (exps / sums - chosen) / n * LOSS_SCALE
    coeff_back = (exps / as_row(sums) - chosen_back) / n * LOSS_SCALE
    grad_unit = jnp.dot(coeff + coeff_back, unit, precision=EXACT, preferred_element_type=f32)
    grad_unit = grad_unit / TEMPERATURE
    radial = jnp.sum(unit * grad_unit, axis=1, keepdims=True)
    slope[...] = (grad_unit - unit * radial) / length
    part = slope[:, pl.ds(pl.multiple_of(dp * (width // 16), width // 16), width // 16)]
    grad_out[...] = dot_tn(mix[...], part, EXACT)
    side = slope[pl.ds(pl.multiple_of(co * (n // 2), 8), n // 2), :] / DOC_LEN
    grad_mixture[...] = folded(dot_nt(stacked_pieces(side, 3), wo[...]), 3).astype(bf16)


def score_gradients(piece, chip, ctx, upstream):
    tok = piece.shape[0]
    q, k, v = (piece[:, j * HD : (j + 1) * HD] for j in range(3))
    ctx_probs, own_probs = probabilities(q, k, ctx[:, :HD])
    docs = iota((tok, upstream.shape[0]), 0) // DOC_LEN + chip * (tok // DOC_LEN)
    pick = jnp.where(docs == iota((tok, upstream.shape[0]), 1), 1.0, 0.0).astype(bf16)
    gm = dot(pick, upstream).astype(bf16)
    ctx_dweights, own_dweights = dot_nt(gm, ctx[:, HD:]), dot_nt(gm, v)
    inner = jnp.sum(ctx_probs * ctx_dweights, 1, keepdims=True)
    inner = inner + jnp.sum(own_probs * own_dweights, 1, keepdims=True)
    ctx_dscores = (ctx_probs * (ctx_dweights - inner) * FACTOR).astype(bf16)
    own_dscores = (own_probs * (own_dweights - inner) * FACTOR).astype(bf16)
    return q, k, gm, ctx_probs.astype(bf16), own_probs.astype(bf16), ctx_dscores, own_dscores


def backward_kernel(pos, ctx, grad_mixture, pieces, own, grads, grad_ctx):
    upstream = grad_mixture[...]
    total = jnp.zeros(grad_ctx.shape, f32)
    for i in range(8):
        q, _, gm, ctx_weights, _, ctx_dscores, _ = score_gradients(
            pieces[i], i % 4 * 2 + i // 4, ctx, upstream
        )
        total = total + jnp.concatenate([dot_tn(ctx_dscores, q), dot_tn(ctx_weights, gm)], axis=1)
    grad_ctx[...] = total
    q, k, gm, _, own_weights, ctx_dscores, own_dscores = score_gradients(
        own[...], pos[3] * 2 + pos[2], ctx, upstream
    )
    grad_q = dot(ctx_dscores, ctx[:, :HD]) + dot(own_dscores, k)
    grad_k = dot_tn(own_dscores, q)
    grad_v = dot_tn(own_weights, gm)
    grads[...] = jnp.concatenate([grad_q, grad_k, grad_v], axis=1).astype(bf16)


def context_kernel(pos, one, two, wk, wv, total, out0, out1, out2, out3, part):
    half = part.shape[1]
    grad = one[...] + two[...]
    total[...] = grad
    here = pl.ds(pl.multiple_of(pos[4] * half, half), half)
    got = dot_nt(stacked_pieces(grad[:, :HD], 2), wk[here, :])
    got = got + dot_nt(stacked_pieces(grad[:, HD:], 2), wv[here, :])
    part[...] = folded(got, 2)
    for k, out in enumerate((out0, out1, out2, out3)):
        at = (pos[1] + k) & 3
        rows = [part[pl.ds(pl.multiple_of(z * 32 + at * 8, 8), 8), :] for z in range(4)]
        out[...] = jnp.concatenate(rows, axis=0).astype(out.dtype)


def middle_kernel(pos, own, one, two, three, out0, out1, out2, out3, total):
    total[...] = (own[...] + wide(two[...])) + (wide(one[...]) + wide(three[...]))
    for k, out in enumerate((out0, out1, out2, out3)):
        at = (pos[0] + k) & 3
        out[...] = total[pl.ds(pl.multiple_of(at * 8, 8), 8), :]


def finish_kernel(pos, context, gain, mine, theirs, out):
    half = mine.shape[1]
    low = pos[4] == 0
    grad = jnp.concatenate(
        [jnp.where(low, mine[...], theirs[...]), jnp.where(low, theirs[...], mine[...])], axis=1
    )
    rows = wide(context[...])
    inv = inverse_rms(rows)
    scaled = gain[...] * grad
    out[...] = inv * scaled - rows * inv**3 * jnp.mean(rows * scaled, axis=1, keepdims=True)


def weight_kernel(pos, normed, grads, named_rows, grad_ctx, mine, theirs):
    feat = mine.shape[1]
    chip = pos[2] * 4 + pos[3]
    own_rows = grad_ctx[pl.ds(pl.multiple_of((chip * 2 + pos[4]) * 8, 8), 8), :]
    head = wide(own_rows.astype(bf16))
    ctx_grads = jnp.concatenate([head, own_rows - head], axis=0).astype(bf16)
    named = wide(named_rows[...])
    named = jnp.concatenate([named, named], axis=0).astype(bf16)
    rows = jnp.concatenate([normed[...], named], axis=0)
    right = jnp.concatenate([jnp.zeros((ctx_grads.shape[0], HD), bf16), ctx_grads], axis=1)
    right = jnp.concatenate([grads[...], right], axis=0)
    for i in range(16):
        got = dot_tn(rows[:, i * feat : (i + 1) * feat], right)

        @pl.when(pos[4] == i % 2)
        def _():
            mine[i // 2] = got

        @pl.when(pos[4] != i % 2)
        def _():
            theirs[i // 2] = got.astype(bf16)


def weight_y_kernel(pos, mine, came, out0, out1, out2, out3):
    for k, out in enumerate((out0, out1, out2, out3)):
        line = (pos[3] + k) & 3
        for zl in range(2):
            out[zl] = (mine[zl * 4 + line] + wide(came[zl * 4 + line])).astype(out.dtype)


def weight_z_kernel(pos, own, one, two, three, mine, theirs):
    for zl in range(2):
        got = (own[zl] + wide(two[zl])) + (wide(one[zl]) + wide(three[zl]))

        @pl.when(pos[2] == zl)
        def _():
            mine[...] = got

        @pl.when(pos[2] != zl)
        def _():
            theirs[...] = got.astype(bf16)


def shift(a, axis, k):
    return lax.ppermute(a, axis, [(i, (i + k) % 4) for i in range(4)])


def others(a, axis):
    return [shift(a, axis, k) for k in (1, 2, 3)]


def other(a, axis):
    return lax.ppermute(a, axis, [(0, 1), (1, 0)])


def pair(a, axis):
    b = other(a, axis)
    first = lax.axis_index(axis) == 0
    return jnp.where(first, jnp.concatenate([a, b]), jnp.concatenate([b, a]))


def ring_sum(a, axis):
    one, two, three = others(a, axis)
    return (a + two) + (one + three)


def spread(block, axis, size):
    copies = jnp.broadcast_to(block[None], (size,) + block.shape)
    return lax.all_to_all(copies, axis, 0, 0)


def shards(doc_states, context, gain, w_query, w_key, w_value, w_out, partners):
    tok, feat = doc_states.shape
    docs = tok // DOC_LEN
    width = w_query.shape[0]
    pos = jnp.stack([lax.axis_index(a) for a in EVERY]).astype(jnp.int32)
    gain_row = gain.reshape(1, width)

    by_zh = [doc_states] + others(doc_states, "zh")
    context, by_zh[1] = lax.optimization_barrier((context, by_zh[1]))
    by_zh = jnp.stack(by_zh)
    right, left = shift(by_zh, "x", 1), shift(by_zh, "x", 3)
    rows = [by_zh, right, left, shift(right[:2], "x", 1), shift(left[2:], "x", 3)]

    swap = [(c * 16 + d, d * 16 + c) for c in range(16) for d in range(16)]
    own_ctx = wide(context)
    own_ctx_normed = (own_ctx * inverse_rms(own_ctx) * gain).astype(bf16)
    named_rows = lax.ppermute(own_ctx_normed, EVERY, swap)
    few = jnp.concatenate([dot(named_rows, w_key), dot(named_rows, w_value)], axis=1).astype(bf16)
    ctx_kv = spread(few, DP, 16).reshape(-1, 2 * HD)

    qkv, own_mean, branch, mix, normed = call(
        forward_kernel,
        (
            shape(tok, 3 * HD, dtype=bf16),
            shape(docs, width),
            shape(docs, width),
            shape(docs, HD),
            shape(tok, width, dtype=bf16),
        ),
        ["s"] + ["v"] * 11,
    )(pos, gain_row, w_query, w_key, w_value, w_out, ctx_kv, *rows)

    pieces = spread(qkv, ("zl", "y"), 8)

    pooled = own_mean + ring_sum(ring_sum(branch, "x"), "zh")
    message = jnp.concatenate(
        [pooled, mix, jnp.pad(wide(partners)[:, None], ((0, 0), (0, HD - 1)))], axis=1
    )
    message = pair(message, "zl")
    messages = jnp.stack([message] + others(message, "y"))
    total = 64
    loss, grad_mixture, grad_out = call(
        loss_kernel,
        (shape(1, 1), shape(total // 2, HD, dtype=bf16), shape(HD, feat)),
        ["s"] + ["v"] * 3,
        scratch=[
            pltpu.VMEM((total, width), f32),
            pltpu.VMEM((total, HD), f32),
            pltpu.VMEM((total, HD), f32),
            pltpu.VMEM((total, width), f32),
        ],
    )(pos, w_out, messages, other(messages, "co"))

    grads, grad_ctx = call(
        backward_kernel,
        (shape(tok, 3 * HD, dtype=bf16), shape(HD, 2 * HD)),
        ["s"] + ["v"] * 4,
    )(pos, ctx_kv, grad_mixture, pieces, qkv)

    half = width // 2
    rows = 4 * context.shape[0]
    grad_ctx, part, *sent = call(
        context_kernel,
        (shape(HD, 2 * HD), shape(rows, half)) + (shape(rows, half, dtype=bf16),) * 3,
        ["s"] + ["v"] * 4,
        scratch=[pltpu.VMEM((4 * rows, half), f32)],
    )(pos, grad_ctx, other(grad_ctx, "co"), w_key, w_value)
    came = [shift(a, "x", k) for k, a in zip((1, 2, 3), sent)]
    part, *sent = call(
        middle_kernel,
        (shape(rows // 4, half),) * 4,
        ["s"] + ["v"] * 4,
        scratch=[pltpu.VMEM((rows, half), f32)],
    )(pos, part, *came)
    one, two, three = [shift(a, "zh", k) for k, a in zip((1, 2, 3), sent)]
    part = (part + two) + (one + three)
    grad_context = call(finish_kernel, shape(*context.shape), ["s"] + ["v"] * 4)(
        pos, context, gain_row, part, other(part, "co")
    )

    mine, theirs = call(
        weight_kernel,
        (shape(8, feat, 3 * HD), shape(8, feat, 3 * HD, dtype=bf16)),
        ["s"] + ["v"] * 4,
    )(pos, normed, grads, named_rows, grad_ctx)
    mine, *sent = call(
        weight_y_kernel,
        (shape(2, feat, 3 * HD),) + (shape(2, feat, 3 * HD, dtype=bf16),) * 3,
        ["s"] + ["v"] * 2,
    )(pos, mine, other(theirs, "co"))
    came = [shift(a, "y", k) for k, a in zip((1, 2, 3), sent)]
    mine, theirs = call(
        weight_z_kernel,
        (shape(feat, 3 * HD), shape(feat, 3 * HD, dtype=bf16)),
        ["s"] + ["v"] * 4,
    )(pos, mine, *came)
    mine = mine + wide(other(theirs, "zl"))
    grad_query, grad_key, grad_value = (mine[:, i * HD : (i + 1) * HD] for i in range(3))
    return loss.reshape(()), grad_context, grad_query, grad_key, grad_value, grad_out


def solution(mesh):
    split = Mesh(mesh.devices.reshape(4, 4, 2, 4, 2), EVERY)
    in_specs = (
        P(DP, CTX),
        P(CTX, None),
        P(),
        P(None, CTX),
        P(None, CTX),
        P(None, CTX),
        P(CTX, None),
        P(DP),
    )
    out_specs = (P(), P(CTX, None), P(DP, CTX), P(DP, CTX), P(DP, CTX), P(CTX, DP))
    return jax.shard_map(
        shards, mesh=split, in_specs=in_specs, out_specs=out_specs, check_vma=False
    )
```

```python
import jax
import jax.numpy as jnp
from jax import lax
from jax.experimental import pallas as pl
from jax.experimental.pallas import tpu as pltpu
from jax.sharding import Mesh, PartitionSpec as P

HD = 128
DOC_LEN = 64

EPS = 1e-05
TEMPERATURE = 0.05
LOSS_SCALE = 65536.0
EXACT = lax.Precision.HIGHEST
FACTOR = HD**-0.5

CTX = ("zh", "x")
DP = ("zl", "y", "co")
EVERY = CTX + DP

f32 = jnp.float32
bf16 = jnp.bfloat16

ROWS_BY_ROWS = (((1,), (1,)), ((), ()))
COLS_BY_COLS = (((0,), (0,)), ((), ()))


def wide(a):
    return a.astype(f32)


def dot(a, b):
    return jnp.dot(a, b, preferred_element_type=f32)


def dot_nt(a, b, precision=None):
    return lax.dot_general(a, b, ROWS_BY_ROWS, precision=precision, preferred_element_type=f32)


def dot_tn(a, b, precision=None):
    return lax.dot_general(a, b, COLS_BY_COLS, precision=precision, preferred_element_type=f32)


def stacked_pieces(a, count):
    out = []
    for _ in range(count):
        head = a.astype(bf16)
        out.append(head)
        a = a - wide(head)
    return jnp.concatenate(out, axis=0)


def folded(a, count):
    rows = a.shape[0] // count
    return sum(a[i * rows : (i + 1) * rows] for i in reversed(range(count)))


def iota(shape, axis):
    return lax.broadcasted_iota(jnp.int32, shape, axis)


def as_row(column):
    n = column.shape[0]
    return jnp.sum(jnp.where(iota((n, n), 0) == iota((n, n), 1), column, 0.0), 0, keepdims=True)


def position():
    return [lax.axis_index(a) for a in EVERY]


def inverse_rms(a):
    return lax.rsqrt(jnp.mean(a * a, axis=-1, keepdims=True) + EPS)


def probabilities(q, k, ctx_keys):
    n = q.shape[0]
    same = iota((n, n), 0) // DOC_LEN == iota((n, n), 1) // DOC_LEN
    ctx_exps = jnp.exp(dot_nt(q, ctx_keys) * FACTOR)
    own_exps = jnp.where(same, jnp.exp(dot_nt(q, k) * FACTOR), 0.0)
    total = jnp.sum(ctx_exps, 1, keepdims=True) + jnp.sum(own_exps, 1, keepdims=True)
    return ctx_exps / total, own_exps / total


def call(kernel, out_shape, in_specs, scratch=(), vmem=40, flops=10**9):
    in_specs = [
        pl.BlockSpec(memory_space=pl.ANY if s == "a" else pltpu.VMEM) for s in in_specs
    ]
    return pl.pallas_call(
        kernel,
        out_shape=out_shape,
        in_specs=in_specs,
        out_specs=jax.tree.map(lambda _: pl.BlockSpec(memory_space=pltpu.VMEM), out_shape),
        scratch_shapes=scratch,
        compiler_params=pltpu.CompilerParams(vmem_limit_bytes=vmem * 2**20),
        cost_estimate=pl.CostEstimate(flops=flops, bytes_accessed=4 * 10**6, transcendentals=0),
    )


def shape(*dims, dtype=f32):
    return jax.ShapeDtypeStruct(dims, dtype)


def forward_kernel(gain, wq, wk, wv, wo, ctx, here0, right, left, far0, far1, *refs):
    qkv, copies, own, branch, mix, normed, weights, last, sems = refs
    pos = position()
    fetch = [
        pltpu.make_async_copy(w, weights.at[:, pl.ds(i * HD, HD)], sems.at[i])
        for i, w in enumerate((wq, wk, wv))
    ]
    fetch.append(pltpu.make_async_copy(wo, last, sems.at[3]))
    for copy in fetch:
        copy.start()
    blocks = [(here0, i, 0, i) for i in range(4)] + [(right, i, 1, i) for i in range(4)]
    blocks += [(left, i, 3, i) for i in range(4)]
    blocks += [(far0, i, 2, i) for i in range(2)] + [(far1, i, 2, i + 2) for i in range(2)]
    tok, feat = here0.shape[1:]
    docs = tok // DOC_LEN
    averaging = jnp.where(iota((8, tok), 0) == iota((8, tok), 1) // DOC_LEN, 1 / DOC_LEN, 0.0)
    averaging = averaging.astype(bf16)
    squares = jnp.zeros((tok, 1), f32)
    for ref, i, _, _ in blocks:
        rows = wide(ref[i])
        squares = squares + jnp.sum(rows * rows, axis=1, keepdims=True)
    inv = lax.rsqrt(squares / (16 * feat) + EPS)
    total = jnp.zeros((tok, 3 * HD), f32)
    for copy in fetch[:3]:
        copy.wait()
    for ref, i, along_x, along_z in blocks:
        place = ((pos[0] - along_z) & 3) * 4 + ((pos[1] - along_x) & 3)
        here = pl.ds(pl.multiple_of(place * feat, feat), feat)
        rows = ref[i]
        ready = (wide(rows) * inv * gain[:, here]).astype(bf16)
        normed[:, here] = ready
        total = total + dot(ready, weights[here, :])
        own[:, here] = dot(averaging, rows)[:docs]
    total = total.astype(bf16)
    qkv[...] = total
    for i in range(copies.shape[0]):
        copies[i] = total
    q, k, v = total[:, :HD], total[:, HD : 2 * HD], total[:, 2 * HD :]
    ctx_probs, own_probs = probabilities(q, k, ctx[:, :HD])
    mixture = dot(ctx_probs.astype(bf16), ctx[:, HD:]) + dot(own_probs.astype(bf16), v)
    mean = dot(averaging, mixture.astype(bf16))
    mix[...] = mean[:docs]
    fetch[3].wait()
    branch[...] = folded(dot(stacked_pieces(mean, 3), last[...]), 3)[:docs]


def loss_kernel(wo, mine, theirs, loss, grad_mixture, grad_out, pooled, mix, extra, slope):
    pos = position()
    width = wo.shape[1]
    co, y, dp = pos[4], pos[3], (pos[2] * 4 + pos[3]) * 2 + pos[4]
    for i in range(8):
        messages, core = (mine, co) if i < 4 else (theirs, 1 - co)
        here = pl.ds(pl.multiple_of((core * 4 + ((y - i % 4) & 3)) * 8, 8), 8)
        pooled[here, :] = messages[i % 4, :, :width]
        mix[here, :] = messages[i % 4, :, width : width + HD]
        extra[here, :] = messages[i % 4, :, width + HD :]
    n = pooled.shape[0]
    vectors = pooled[...]
    length = jnp.sqrt(jnp.sum(vectors * vectors, axis=1, keepdims=True) + 1e-06)
    unit = vectors / length
    gram = dot_nt(vectors, vectors, EXACT)
    scores = gram / (length * as_row(length)) / TEMPERATURE
    diagonal = iota((n, n), 0) == iota((n, n), 1)

    def document(axis):
        at = iota((n, n), axis)
        return (((at >> 2) & 1) * 32 + ((at >> 3) & 3) * 8 + (at >> 5) * 4 + (at & 3)).astype(f32)

    partners = extra[:, 0:1]
    chosen = jnp.where(partners == document(1), 1.0, 0.0)
    chosen_back = jnp.where(as_row(partners) == document(0), 1.0, 0.0)
    exps = jnp.where(diagonal, 0.0, jnp.exp(scores))
    sums = jnp.sum(exps, axis=1, keepdims=True)
    picked = jnp.sum(scores * chosen, axis=1, keepdims=True)
    loss[...] = jnp.sum(jnp.log(sums) - picked, axis=0, keepdims=True) / n
    coeff = (exps / sums - chosen) / n * LOSS_SCALE
    coeff_back = (exps / as_row(sums) - chosen_back) / n * LOSS_SCALE
    grad_unit = jnp.dot(coeff + coeff_back, unit, precision=EXACT, preferred_element_type=f32)
    grad_unit = grad_unit / TEMPERATURE
    radial = jnp.sum(unit * grad_unit, axis=1, keepdims=True)
    slope[...] = (grad_unit - unit * radial) / length
    part = slope[:, pl.ds(pl.multiple_of(dp * (width // 16), width // 16), width // 16)]
    grad_out[...] = dot_tn(mix[...], part, EXACT)
    side = slope[pl.ds(pl.multiple_of(co * (n // 2), 8), n // 2), :] / DOC_LEN
    grad_mixture[...] = wide(folded(dot_nt(stacked_pieces(side, 3), wo[...]), 3).astype(bf16))


def by_token(a):
    rows = [jnp.broadcast_to(a[i : i + 1], (DOC_LEN, a.shape[1])) for i in range(4)]
    return jnp.concatenate(rows, axis=0)


def score_gradients(piece, ctx, ctx_dweights, own_dweights):
    q, k, _ = (piece[:, j * HD : (j + 1) * HD] for j in range(3))
    ctx_probs, own_probs = probabilities(q, k, ctx[:, :HD])
    ctx_dweights, own_dweights = by_token(ctx_dweights), by_token(own_dweights)
    inner = jnp.sum(ctx_probs * ctx_dweights, 1, keepdims=True)
    inner = inner + jnp.sum(own_probs * own_dweights, 1, keepdims=True)
    ctx_dscores = (ctx_probs * (ctx_dweights - inner) * FACTOR).astype(bf16)
    own_dscores = (own_probs * (own_dweights - inner) * FACTOR).astype(bf16)
    return ctx_probs.astype(bf16), own_probs.astype(bf16), ctx_dscores, own_dscores


def backward_kernel(ctx, grad_mixture, pieces, own, grads, grad_ctx):
    pos = position()
    tok = own.shape[0]
    wide_upstream = grad_mixture[...]
    upstream = wide_upstream.astype(bf16)
    docs = upstream.shape[0]
    ctx_dweights = dot_nt(upstream, ctx[:, HD:])
    adding = jnp.where(iota((8, tok), 0) == iota((8, tok), 1) // DOC_LEN, 1.0, 0.0).astype(bf16)
    total = jnp.zeros((HD, HD), f32)
    weight_sums = [None] * 8
    for i in range(8):
        chip = i % 4 * 2 + i // 4
        here = slice(chip * 4, chip * 4 + 4)
        own_dweights = dot_nt(upstream, pieces[i, :, 2 * HD :])
        ctx_weights, _, ctx_dscores, _ = score_gradients(
            pieces[i], ctx, ctx_dweights[here], own_dweights[here]
        )
        total = total + dot_tn(ctx_dscores, pieces[i, :, :HD])
        weight_sums[chip] = dot(adding, ctx_weights)[:4]
    grad_ctx[:, :HD] = total
    grad_ctx[:, HD:] = dot_tn(jnp.concatenate(weight_sums, axis=0), wide_upstream, EXACT)
    pick = iota((8, docs), 0) + (pos[3] * 2 + pos[2]) * 4 == iota((8, docs), 1)
    upstream = dot(jnp.where(pick, 1.0, 0.0).astype(bf16), upstream)
    q, k, v = (own[:, j * HD : (j + 1) * HD] for j in range(3))
    _, own_weights, ctx_dscores, own_dscores = score_gradients(
        own[...], ctx, dot_nt(upstream.astype(bf16), ctx[:, HD:]), dot_nt(upstream.astype(bf16), v)
    )
    grad_q = dot(ctx_dscores, ctx[:, :HD]) + dot(own_dscores, k)
    grad_k = dot_tn(own_dscores, q)
    grad_v = dot_tn(own_weights, by_token(upstream).astype(bf16))
    grads[...] = jnp.concatenate([grad_q, grad_k, grad_v], axis=1).astype(bf16)


def context_kernel(one, two, wk, wv, total, out0, out1, out2, out3, part):
    pos = position()
    half = part.shape[1]
    grad = one[...] + two[...]
    total[...] = grad
    here = pl.ds(pl.multiple_of(pos[4] * half, half), half)
    got = dot_nt(stacked_pieces(grad[:, :HD], 2), wk[here, :])
    got = got + dot_nt(stacked_pieces(grad[:, HD:], 2), wv[here, :])
    part[...] = folded(got, 2)
    for k, out in enumerate((out0, out1, out2, out3)):
        at = (pos[1] + k) & 3
        rows = [part[pl.ds(pl.multiple_of(z * 32 + at * 8, 8), 8), :] for z in range(4)]
        out[...] = jnp.concatenate(rows, axis=0).astype(out.dtype)


def middle_kernel(own, one, two, three, out0, out1, out2, out3, total):
    pos = position()
    total[...] = (own[...] + wide(two[...])) + (wide(one[...]) + wide(three[...]))
    for k, out in enumerate((out0, out1, out2, out3)):
        at = (pos[0] + k) & 3
        out[...] = total[pl.ds(pl.multiple_of(at * 8, 8), 8), :]


def finish_kernel(context, gain, mine, theirs, out):
    pos = position()
    half = mine.shape[1]
    low = pos[4] == 0
    grad = jnp.concatenate(
        [jnp.where(low, mine[...], theirs[...]), jnp.where(low, theirs[...], mine[...])], axis=1
    )
    rows = wide(context[...])
    inv = inverse_rms(rows)
    scaled = gain[...] * grad
    out[...] = inv * scaled - rows * inv**3 * jnp.mean(rows * scaled, axis=1, keepdims=True)


def weight_kernel(normed, grads, mine, theirs):
    pos = position()
    feat = mine.shape[1]
    right = grads[...]
    for i in range(16):
        got = dot_tn(normed[:, i * feat : (i + 1) * feat], right)

        @pl.when(pos[4] == i % 2)
        def _():
            mine[i // 2] = got

        @pl.when(pos[4] != i % 2)
        def _():
            theirs[i // 2] = got.astype(bf16)


def weight_y_kernel(mine, came, named_rows, grad_ctx, out0, out1, out2, out3):
    pos = position()
    feat = mine.shape[1]
    here = grad_ctx[pl.ds(pl.multiple_of((pos[2] * 4 + pos[3]) * 16, 16), 16), :]
    here = stacked_pieces(here, 2)
    for k, out in enumerate((out0, out1, out2, out3)):
        line = (pos[3] + k) & 3
        for zl in range(2):
            chip = zl * 4 + line
            columns = pl.ds(pl.multiple_of((chip * 2 + pos[4]) * feat, feat), feat)
            got = mine[chip] + wide(came[chip])
            from_ctx = dot_tn(jnp.concatenate([named_rows[:, columns]] * 2, axis=0), here)
            out[zl, :, :HD] = got[:, :HD].astype(out.dtype)
            out[zl, :, HD:] = (got[:, HD:] + from_ctx).astype(out.dtype)


def weight_z_kernel(own, one, two, three, mine, theirs):
    pos = position()
    for zl in range(2):
        got = (own[zl] + wide(two[zl])) + (wide(one[zl]) + wide(three[zl]))

        @pl.when(pos[2] == zl)
        def _():
            mine[...] = got

        @pl.when(pos[2] != zl)
        def _():
            theirs[...] = got.astype(bf16)


def shift(a, axis, k):
    return lax.ppermute(a, axis, [(i, (i + k) % 4) for i in range(4)])


def others(a, axis):
    return [shift(a, axis, k) for k in (1, 2, 3)]


def other(a, axis):
    return lax.ppermute(a, axis, [(0, 1), (1, 0)])


def pair(a, axis):
    b = other(a, axis)
    first = lax.axis_index(axis) == 0
    return jnp.where(first, jnp.concatenate([a, b]), jnp.concatenate([b, a]))


def ring_sum(a, axis):
    one, two, three = others(a, axis)
    return (a + two) + (one + three)


def spread(block, axis, size):
    copies = jnp.broadcast_to(block[None], (size,) + block.shape)
    return lax.all_to_all(copies, axis, 0, 0)


def shards(doc_states, context, gain, w_query, w_key, w_value, w_out, partners):
    tok, feat = doc_states.shape
    docs = tok // DOC_LEN
    width = w_query.shape[0]
    gain_row = gain.reshape(1, width)

    swap = [(c * 16 + d, d * 16 + c) for c in range(16) for d in range(16)]
    own_ctx = wide(context)
    own_ctx_normed = (own_ctx * inverse_rms(own_ctx) * gain).astype(bf16)
    named_rows = lax.ppermute(own_ctx_normed, EVERY, swap)

    by_zh = jnp.stack([doc_states] + others(doc_states, "zh"))
    right, left = shift(by_zh, "x", 1), shift(by_zh, "x", 3)

    named_rows, by_zh = lax.optimization_barrier((named_rows, by_zh))
    few = jnp.concatenate([dot(named_rows, w_key), dot(named_rows, w_value)], axis=1).astype(bf16)
    ctx_kv = spread(few, DP, 16).reshape(-1, 2 * HD)
    ctx_kv, right, left = lax.optimization_barrier((ctx_kv, right, left))
    rows = [by_zh, right, left, shift(right[:2], "x", 1), shift(left[2:], "x", 3)]

    qkv, copies, own_mean, branch, mix, normed = call(
        forward_kernel,
        (
            shape(tok, 3 * HD, dtype=bf16),
            shape(8, tok, 3 * HD, dtype=bf16),
            shape(docs, width),
            shape(docs, width),
            shape(docs, HD),
            shape(tok, width, dtype=bf16),
        ),
        ["v"] + ["a"] * 4 + ["v"] * 6,
        scratch=[
            pltpu.VMEM((width, 3 * HD), bf16),
            pltpu.VMEM((HD, width), bf16),
            pltpu.SemaphoreType.DMA((4,)),
        ],
    )(gain_row, w_query, w_key, w_value, w_out, ctx_kv, *rows)

    pieces = lax.all_to_all(copies, ("zl", "y"), 0, 0)

    pooled = own_mean + ring_sum(ring_sum(branch, "x"), "zh")
    pooled, pieces = lax.optimization_barrier((pooled, pieces))
    message = jnp.concatenate(
        [pooled, mix, jnp.pad(wide(partners)[:, None], ((0, 0), (0, HD - 1)))], axis=1
    )
    message = pair(message, "zl")
    messages = jnp.stack([message] + others(message, "y"))
    total = 64
    loss, grad_mixture, grad_out = call(
        loss_kernel,
        (shape(1, 1), shape(total // 2, HD), shape(HD, feat)),
        ["v"] * 3,
        scratch=[
            pltpu.VMEM((total, width), f32),
            pltpu.VMEM((total, HD), f32),
            pltpu.VMEM((total, HD), f32),
            pltpu.VMEM((total, width), f32),
        ],
    )(w_out, messages, other(messages, "co"))

    grads, grad_ctx = call(
        backward_kernel,
        (shape(tok, 3 * HD, dtype=bf16), shape(HD, 2 * HD)),
        ["v"] * 4,
    )(ctx_kv, grad_mixture, pieces, qkv)

    half = width // 2
    rows = 4 * context.shape[0]
    grad_ctx, part, *sent = call(
        context_kernel,
        (shape(HD, 2 * HD), shape(rows, half)) + (shape(rows, half, dtype=bf16),) * 3,
        ["v"] * 4,
        scratch=[pltpu.VMEM((4 * rows, half), f32)],
    )(grad_ctx, other(grad_ctx, "co"), w_key, w_value)
    came = [shift(a, "x", k) for k, a in zip((1, 2, 3), sent)]
    part, *sent = call(
        middle_kernel,
        (shape(rows // 4, half),) * 4,
        ["v"] * 4,
        scratch=[pltpu.VMEM((rows, half), f32)],
    )(part, *came)
    one, two, three = [shift(a, "zh", k) for k, a in zip((1, 2, 3), sent)]
    part = (part + two) + (one + three)
    grad_context = call(finish_kernel, shape(*context.shape), ["v"] * 4, flops=5 * 10**10)(
        context, gain_row, part, other(part, "co")
    )

    mine, theirs = call(
        weight_kernel,
        (shape(8, feat, 3 * HD), shape(8, feat, 3 * HD, dtype=bf16)),
        ["v"] * 2,
    )(normed, grads)
    mine, *sent = call(
        weight_y_kernel,
        (shape(2, feat, 3 * HD),) + (shape(2, feat, 3 * HD, dtype=bf16),) * 3,
        ["v"] * 4,
    )(mine, other(theirs, "co"), pair(named_rows, "co"), grad_ctx)
    came = [shift(a, "y", k) for k, a in zip((1, 2, 3), sent)]
    mine, theirs = call(
        weight_z_kernel,
        (shape(feat, 3 * HD), shape(feat, 3 * HD, dtype=bf16)),
        ["v"] * 4,
    )(mine, *came)
    mine = mine + wide(other(theirs, "zl"))
    grad_query, grad_key, grad_value = (mine[:, i * HD : (i + 1) * HD] for i in range(3))
    return loss.reshape(()), grad_context, grad_query, grad_key, grad_value, grad_out


def solution(mesh):
    split = Mesh(mesh.devices.reshape(4, 4, 2, 4, 2), EVERY)
    in_specs = (
        P(DP, CTX),
        P(CTX, None),
        P(),
        P(None, CTX),
        P(None, CTX),
        P(None, CTX),
        P(CTX, None),
        P(DP),
    )
    out_specs = (P(), P(CTX, None), P(DP, CTX), P(DP, CTX), P(DP, CTX), P(CTX, DP))
    return jax.shard_map(
        shards, mesh=split, in_specs=in_specs, out_specs=out_specs, check_vma=False
    )
```

```python
import functools

import jax
import jax.numpy as jnp
from jax import lax
from jax.experimental import pallas as pl
from jax.experimental.pallas import tpu as pltpu
from jax.sharding import Mesh, PartitionSpec as P

HD = 128
DOC_LEN = 64

EPS = 1e-05
TEMPERATURE = 0.05
LOSS_SCALE = 65536.0
EXACT = lax.Precision.HIGHEST
FACTOR = HD**-0.5

CTX = ("zh", "x")
DP = ("zl", "y", "co")
EVERY = CTX + DP

f32 = jnp.float32
bf16 = jnp.bfloat16

ROWS_BY_ROWS = (((1,), (1,)), ((), ()))
COLS_BY_COLS = (((0,), (0,)), ((), ()))


def wide(a):
    return a.astype(f32)


def dot(a, b):
    return jnp.dot(a, b, preferred_element_type=f32)


def dot_nt(a, b, precision=None):
    return lax.dot_general(a, b, ROWS_BY_ROWS, precision=precision, preferred_element_type=f32)


def dot_tn(a, b, precision=None):
    return lax.dot_general(a, b, COLS_BY_COLS, precision=precision, preferred_element_type=f32)


def stacked_pieces(a, count):
    out = []
    for _ in range(count):
        head = a.astype(bf16)
        out.append(head)
        a = a - wide(head)
    return jnp.concatenate(out, axis=0)


def folded(a, count):
    rows = a.shape[0] // count
    return sum(a[i * rows : (i + 1) * rows] for i in reversed(range(count)))


def iota(shape, axis):
    return lax.broadcasted_iota(jnp.int32, shape, axis)


def as_row(column):
    n = column.shape[0]
    return jnp.sum(jnp.where(iota((n, n), 0) == iota((n, n), 1), column, 0.0), 0, keepdims=True)


def position():
    return [lax.axis_index(a) for a in EVERY]


def inverse_rms(a):
    return lax.rsqrt(jnp.mean(a * a, axis=-1, keepdims=True) + EPS)


def probabilities(q, k, ctx_keys):
    n = q.shape[0]
    same = iota((n, n), 0) // DOC_LEN == iota((n, n), 1) // DOC_LEN
    ctx_exps = jnp.exp(dot_nt(q, ctx_keys) * FACTOR)
    own_exps = jnp.where(same, jnp.exp(dot_nt(q, k) * FACTOR), 0.0)
    total = jnp.sum(ctx_exps, 1, keepdims=True) + jnp.sum(own_exps, 1, keepdims=True)
    return ctx_exps / total, own_exps / total


def call(kernel, out_shape, in_specs, scratch=(), vmem=40, flops=10**9):
    in_specs = [
        pl.BlockSpec(memory_space=pl.ANY if s == "a" else pltpu.VMEM) for s in in_specs
    ]
    return pl.pallas_call(
        kernel,
        out_shape=out_shape,
        in_specs=in_specs,
        out_specs=jax.tree.map(lambda _: pl.BlockSpec(memory_space=pltpu.VMEM), out_shape),
        scratch_shapes=scratch,
        compiler_params=pltpu.CompilerParams(vmem_limit_bytes=vmem * 2**20),
        cost_estimate=pl.CostEstimate(flops=flops, bytes_accessed=4 * 10**6, transcendentals=0),
    )


def shape(*dims, dtype=f32):
    return jax.ShapeDtypeStruct(dims, dtype)


def forward_kernel(gain, wq, wk, wv, wo, ctx, here0, right, left, far0, far1, *refs):
    qkv, own, branch, mix, normed, weights, last, sems = refs
    pos = position()
    fetch = [
        pltpu.make_async_copy(w, weights.at[:, pl.ds(i * HD, HD)], sems.at[i])
        for i, w in enumerate((wq, wk, wv))
    ]
    fetch.append(pltpu.make_async_copy(wo, last, sems.at[3]))
    for copy in fetch:
        copy.start()
    blocks = [(here0, i, 0, i) for i in range(4)] + [(right, i, 1, i) for i in range(4)]
    blocks += [(left, i, 3, i) for i in range(4)]
    blocks += [(far0, i, 2, i) for i in range(2)] + [(far1, i, 2, i + 2) for i in range(2)]
    tok, feat = here0.shape[1:]
    docs = tok // DOC_LEN
    averaging = jnp.where(iota((8, tok), 0) == iota((8, tok), 1) // DOC_LEN, 1 / DOC_LEN, 0.0)
    averaging = averaging.astype(bf16)
    squares = jnp.zeros((tok, 1), f32)
    for ref, i, _, _ in blocks:
        rows = wide(ref[i])
        squares = squares + jnp.sum(rows * rows, axis=1, keepdims=True)
    inv = lax.rsqrt(squares / (16 * feat) + EPS)
    total = jnp.zeros((tok, 3 * HD), f32)
    for copy in fetch[:3]:
        copy.wait()
    for ref, i, along_x, along_z in blocks:
        place = ((pos[0] - along_z) & 3) * 4 + ((pos[1] - along_x) & 3)
        here = pl.ds(pl.multiple_of(place * feat, feat), feat)
        rows = ref[i]
        ready = (wide(rows) * inv * gain[:, here]).astype(bf16)
        normed[:, here] = ready
        total = total + dot(ready, weights[here, :])
        own[:, here] = dot(averaging, rows)[:docs]
    total = total.astype(bf16)
    qkv[...] = total
    q, k, v = total[:, :HD], total[:, HD : 2 * HD], total[:, 2 * HD :]
    ctx_probs, own_probs = probabilities(q, k, ctx[:, :HD])
    ctx_weights = ctx_probs.astype(bf16)
    mixture = dot(ctx_weights, ctx[:, HD:]) + dot(own_probs.astype(bf16), v)
    mean = dot(averaging, mixture.astype(bf16))
    mix[:, :HD] = mean[:docs]
    mix[:, HD:] = dot(averaging, ctx_weights)[:docs] * DOC_LEN
    fetch[3].wait()
    branch[...] = folded(dot(stacked_pieces(mean, 3), last[...]), 3)[:docs]


def by_token(a):
    rows = [jnp.broadcast_to(a[i : i + 1], (DOC_LEN, a.shape[1])) for i in range(4)]
    return jnp.concatenate(rows, axis=0)


def backward(own, ctx, upstream, grads, grad_ctx_keys):
    q, k, v = (own[:, j * HD : (j + 1) * HD] for j in range(3))
    ctx_probs, own_probs = probabilities(q, k, ctx[:, :HD])
    ctx_dweights = by_token(dot_nt(upstream.astype(bf16), ctx[:, HD:]))
    own_dweights = by_token(dot_nt(upstream.astype(bf16), v))
    inner = jnp.sum(ctx_probs * ctx_dweights, 1, keepdims=True)
    inner = inner + jnp.sum(own_probs * own_dweights, 1, keepdims=True)
    ctx_dscores = (ctx_probs * (ctx_dweights - inner) * FACTOR).astype(bf16)
    own_dscores = (own_probs * (own_dweights - inner) * FACTOR).astype(bf16)
    grad_ctx_keys[...] = dot_tn(ctx_dscores, q)
    grads[:, :HD] = (dot(ctx_dscores, ctx[:, :HD]) + dot(own_dscores, k)).astype(bf16)
    grads[:, HD : 2 * HD] = dot_tn(own_dscores, q).astype(bf16)
    grad_v = dot_tn(own_probs.astype(bf16), by_token(upstream).astype(bf16))
    grads[:, 2 * HD :] = grad_v.astype(bf16)


def loss_kernel(wo, mine, theirs, ctx, own, *refs):
    loss, grad_out, grads, grad_ctx_keys, grad_ctx_values, pooled, mix, weights, extra, slope, up = refs
    pos = position()
    width = wo.shape[1]
    co, y, dp = pos[4], pos[3], (pos[2] * 4 + pos[3]) * 2 + pos[4]
    for i in range(8):
        messages, core = (mine, co) if i < 4 else (theirs, 1 - co)
        here = pl.ds(pl.multiple_of((core * 4 + ((y - i % 4) & 3)) * 8, 8), 8)
        pooled[here, :] = messages[i % 4, :, :width]
        mix[here, :] = messages[i % 4, :, width : width + HD]
        weights[here, :] = messages[i % 4, :, width + HD : width + 2 * HD]
        extra[here, :] = messages[i % 4, :, width + 2 * HD :]
    n = pooled.shape[0]
    vectors = pooled[...]
    length = jnp.sqrt(jnp.sum(vectors * vectors, axis=1, keepdims=True) + 1e-06)
    unit = vectors / length
    gram = dot_nt(vectors, vectors, EXACT)
    scores = gram / (length * as_row(length)) / TEMPERATURE
    diagonal = iota((n, n), 0) == iota((n, n), 1)

    def document(axis):
        at = iota((n, n), axis)
        return (((at >> 2) & 1) * 32 + ((at >> 3) & 3) * 8 + (at >> 5) * 4 + (at & 3)).astype(f32)

    partners = extra[:, 0:1]
    chosen = jnp.where(partners == document(1), 1.0, 0.0)
    chosen_back = jnp.where(as_row(partners) == document(0), 1.0, 0.0)
    exps = jnp.where(diagonal, 0.0, jnp.exp(scores))
    sums = jnp.sum(exps, axis=1, keepdims=True)
    picked = jnp.sum(scores * chosen, axis=1, keepdims=True)
    loss[...] = jnp.sum(jnp.log(sums) - picked, axis=0, keepdims=True) / n
    coeff = (exps / sums - chosen) / n * LOSS_SCALE
    coeff_back = (exps / as_row(sums) - chosen_back) / n * LOSS_SCALE
    grad_unit = jnp.dot(coeff + coeff_back, unit, precision=EXACT, preferred_element_type=f32)
    grad_unit = grad_unit / TEMPERATURE
    radial = jnp.sum(unit * grad_unit, axis=1, keepdims=True)
    slope[...] = (grad_unit - unit * radial) / length
    part = slope[:, pl.ds(pl.multiple_of(dp * (width // 16), width // 16), width // 16)]
    grad_out[...] = dot_tn(mix[...], part, EXACT)
    upstream = folded(dot_nt(stacked_pieces(slope[...] / DOC_LEN, 3), wo[...]), 3)
    up[...] = wide(upstream.astype(bf16))
    grad_ctx_values[...] = dot_tn(weights[...], up[...], EXACT)
    upstream = up[pl.ds(pl.multiple_of(co * (n // 2) + y * 8, 8), 8), :]
    upstream = jnp.where(pos[2] == 0, upstream[:4], upstream[4:])
    upstream = jnp.concatenate([upstream, upstream], axis=0)
    backward(own, ctx, upstream, grads, grad_ctx_keys)


def context_kernel(own, one, two, three, values, wk, wv, total, out0, out1, out2, out3, part):
    pos = position()
    half = part.shape[1]
    grad = (own[...] + two[...]) + (one[...] + three[...])
    grad = jnp.concatenate([grad, values[...]], axis=1)
    total[...] = grad
    here = pl.ds(pl.multiple_of(pos[4] * half, half), half)
    got = dot_nt(stacked_pieces(grad[:, :HD], 2), wk[here, :])
    got = got + dot_nt(stacked_pieces(grad[:, HD:], 2), wv[here, :])
    part[...] = folded(got, 2)
    for k, out in enumerate((out0, out1, out2, out3)):
        at = (pos[1] + k) & 3
        rows = [part[pl.ds(pl.multiple_of(z * 32 + at * 8, 8), 8), :] for z in range(4)]
        out[...] = jnp.concatenate(rows, axis=0).astype(out.dtype)


def middle_kernel(own, one, two, three, out0, out1, out2, out3, total):
    pos = position()
    total[...] = (own[...] + wide(two[...])) + (wide(one[...]) + wide(three[...]))
    for k, out in enumerate((out0, out1, out2, out3)):
        at = (pos[0] + k) & 3
        out[...] = total[pl.ds(pl.multiple_of(at * 8, 8), 8), :]


def finish_kernel(context, gain, mine, theirs, out):
    pos = position()
    half = mine.shape[1]
    low = pos[4] == 0
    grad = jnp.concatenate(
        [jnp.where(low, mine[...], theirs[...]), jnp.where(low, theirs[...], mine[...])], axis=1
    )
    rows = wide(context[...])
    inv = inverse_rms(rows)
    scaled = gain[...] * grad
    out[...] = inv * scaled - rows * inv**3 * jnp.mean(rows * scaled, axis=1, keepdims=True)


def weight_kernel(side, normed, grads, out):
    feat = out.shape[1]
    core = position()[4]
    core = core if side == 0 else 1 - core
    right = grads[...]
    for i in range(8):
        here = pl.ds(pl.multiple_of((i * 2 + core) * feat, feat), feat)
        out[i] = dot_tn(normed[:, here], right).astype(bf16)


def weight_y_kernel(mine, came, named_rows, grad_ctx, out0, out1, out2, out3):
    pos = position()
    feat = mine.shape[1]
    here = grad_ctx[pl.ds(pl.multiple_of((pos[2] * 4 + pos[3]) * 16, 16), 16), :]
    here = stacked_pieces(here, 2)
    for k, out in enumerate((out0, out1, out2, out3)):
        line = (pos[3] + k) & 3
        for zl in range(2):
            chip = zl * 4 + line
            columns = pl.ds(pl.multiple_of((chip * 2 + pos[4]) * feat, feat), feat)
            got = wide(mine[chip]) + wide(came[chip])
            from_ctx = dot_tn(jnp.concatenate([named_rows[:, columns]] * 2, axis=0), here)
            out[zl, :, :HD] = got[:, :HD].astype(out.dtype)
            out[zl, :, HD:] = (got[:, HD:] + from_ctx).astype(out.dtype)


def weight_z_kernel(own, one, two, three, mine, theirs):
    pos = position()
    for zl in range(2):
        got = (own[zl] + wide(two[zl])) + (wide(one[zl]) + wide(three[zl]))

        @pl.when(pos[2] == zl)
        def _():
            mine[...] = got

        @pl.when(pos[2] != zl)
        def _():
            theirs[...] = got.astype(bf16)


def shift(a, axis, k):
    return lax.ppermute(a, axis, [(i, (i + k) % 4) for i in range(4)])


def others(a, axis):
    return [shift(a, axis, k) for k in (1, 2, 3)]


def other(a, axis):
    return lax.ppermute(a, axis, [(0, 1), (1, 0)])


def pair(a, axis):
    b = other(a, axis)
    first = lax.axis_index(axis) == 0
    return jnp.where(first, jnp.concatenate([a, b]), jnp.concatenate([b, a]))


def ring_sum(a, axis):
    one, two, three = others(a, axis)
    return (a + two) + (one + three)


def spread(block, axis, size):
    copies = jnp.broadcast_to(block[None], (size,) + block.shape)
    return lax.all_to_all(copies, axis, 0, 0)


def shards(doc_states, context, gain, w_query, w_key, w_value, w_out, partners):
    tok, feat = doc_states.shape
    docs = tok // DOC_LEN
    width = w_query.shape[0]
    gain_row = gain.reshape(1, width)

    swap = [(c * 16 + d, d * 16 + c) for c in range(16) for d in range(16)]
    own_ctx = wide(context)
    own_ctx_normed = (own_ctx * inverse_rms(own_ctx) * gain).astype(bf16)
    named_rows = lax.ppermute(own_ctx_normed, EVERY, swap)

    by_zh = jnp.stack([doc_states] + others(doc_states, "zh"))
    right, left = shift(by_zh, "x", 1), shift(by_zh, "x", 3)

    named_rows, by_zh = lax.optimization_barrier((named_rows, by_zh))
    few = jnp.concatenate([dot(named_rows, w_key), dot(named_rows, w_value)], axis=1).astype(bf16)
    ctx_kv = spread(few, DP, 16).reshape(-1, 2 * HD)
    ctx_kv, right, left = lax.optimization_barrier((ctx_kv, right, left))
    rows = [by_zh, right, left, shift(right[:2], "x", 1), shift(left[2:], "x", 3)]

    qkv, own_mean, branch, mix, normed = call(
        forward_kernel,
        (
            shape(tok, 3 * HD, dtype=bf16),
            shape(docs, width),
            shape(docs, width),
            shape(docs, 2 * HD),
            shape(tok, width, dtype=bf16),
        ),
        ["v"] + ["a"] * 4 + ["v"] * 6,
        scratch=[
            pltpu.VMEM((width, 3 * HD), bf16),
            pltpu.VMEM((HD, width), bf16),
            pltpu.SemaphoreType.DMA((4,)),
        ],
    )(gain_row, w_query, w_key, w_value, w_out, ctx_kv, *rows)

    pooled = own_mean + ring_sum(ring_sum(branch, "x"), "zh")
    message = jnp.concatenate(
        [pooled, mix, jnp.pad(wide(partners)[:, None], ((0, 0), (0, HD - 1)))], axis=1
    )
    message = pair(message, "zl")
    messages = jnp.stack([message] + others(message, "y"))
    total = 64
    loss, grad_out, grads, grad_ctx_keys, grad_ctx_values = call(
        loss_kernel,
        (
            shape(1, 1),
            shape(HD, feat),
            shape(tok, 3 * HD, dtype=bf16),
            shape(HD, HD),
            shape(HD, HD),
        ),
        ["v"] * 5,
        scratch=[
            pltpu.VMEM((total, width), f32),
            pltpu.VMEM((total, HD), f32),
            pltpu.VMEM((total, HD), f32),
            pltpu.VMEM((total, HD), f32),
            pltpu.VMEM((total, width), f32),
            pltpu.VMEM((total, HD), f32),
        ],
    )(w_out, messages, other(messages, "co"), ctx_kv, qkv)

    half = width // 2
    rows = 4 * context.shape[0]
    grad_ctx_keys = grad_ctx_keys + other(grad_ctx_keys, "co")
    grad_ctx_keys = grad_ctx_keys + other(grad_ctx_keys, "zl")
    grad_ctx, part, *sent = call(
        context_kernel,
        (shape(HD, 2 * HD), shape(rows, half)) + (shape(rows, half, dtype=bf16),) * 3,
        ["v"] * 7,
        scratch=[pltpu.VMEM((4 * rows, half), f32)],
    )(grad_ctx_keys, *others(grad_ctx_keys, "y"), grad_ctx_values, w_key, w_value)
    came = [shift(a, "x", k) for k, a in zip((1, 2, 3), sent)]
    part, *sent = call(
        middle_kernel,
        (shape(rows // 4, half),) * 4,
        ["v"] * 4,
        scratch=[pltpu.VMEM((rows, half), f32)],
    )(part, *came)
    one, two, three = [shift(a, "zh", k) for k, a in zip((1, 2, 3), sent)]
    part = (part + two) + (one + three)
    grad_context = call(finish_kernel, shape(*context.shape), ["v"] * 4, flops=10**9)(
        context, gain_row, part, other(part, "co")
    )

    theirs, mine = (
        call(
            functools.partial(weight_kernel, side),
            shape(8, feat, 3 * HD, dtype=bf16),
            ["v"] * 2,
        )(normed, grads)
        for side in (1, 0)
    )
    mine, *sent = call(
        weight_y_kernel,
        (shape(2, feat, 3 * HD),) + (shape(2, feat, 3 * HD, dtype=bf16),) * 3,
        ["v"] * 4,
    )(mine, other(theirs, "co"), pair(named_rows, "co"), grad_ctx)
    came = [shift(a, "y", k) for k, a in zip((1, 2, 3), sent)]
    mine, theirs = call(
        weight_z_kernel,
        (shape(feat, 3 * HD), shape(feat, 3 * HD, dtype=bf16)),
        ["v"] * 4,
    )(mine, *came)
    mine = mine + wide(other(theirs, "zl"))
    grad_query, grad_key, grad_value = (mine[:, i * HD : (i + 1) * HD] for i in range(3))
    return loss.reshape(()), grad_context, grad_query, grad_key, grad_value, grad_out


def solution(mesh):
    split = Mesh(mesh.devices.reshape(4, 4, 2, 4, 2), EVERY)
    in_specs = (
        P(DP, CTX),
        P(CTX, None),
        P(),
        P(None, CTX),
        P(None, CTX),
        P(None, CTX),
        P(CTX, None),
        P(DP),
    )
    out_specs = (P(), P(CTX, None), P(DP, CTX), P(DP, CTX), P(DP, CTX), P(CTX, DP))
    return jax.shard_map(
        shards, mesh=split, in_specs=in_specs, out_specs=out_specs, check_vma=False
    )
```

```python
import functools

import jax
import jax.numpy as jnp
from jax import lax
from jax.experimental import pallas as pl
from jax.experimental.pallas import tpu as pltpu
from jax.sharding import Mesh, PartitionSpec as P

HD = 128
DOC_LEN = 64

EPS = 1e-05
TEMPERATURE = 0.05
LOSS_SCALE = 65536.0
EXACT = lax.Precision.HIGHEST
FACTOR = HD**-0.5

CTX = ("zh", "x")
DP = ("zl", "y", "co")
EVERY = CTX + DP

f32 = jnp.float32
bf16 = jnp.bfloat16

ROWS_BY_ROWS = (((1,), (1,)), ((), ()))
COLS_BY_COLS = (((0,), (0,)), ((), ()))


def wide(a):
    return a.astype(f32)


def dot(a, b):
    return jnp.dot(a, b, preferred_element_type=f32)


def dot_nt(a, b, precision=None):
    return lax.dot_general(a, b, ROWS_BY_ROWS, precision=precision, preferred_element_type=f32)


def dot_tn(a, b, precision=None):
    return lax.dot_general(a, b, COLS_BY_COLS, precision=precision, preferred_element_type=f32)


def split(a, count):
    out = []
    for _ in range(count):
        head = a.astype(bf16)
        out.append(head)
        a = a - wide(head)
    return out


def stacked_pieces(a, count):
    return jnp.concatenate(split(a, count), axis=0)


def folded(a, count):
    rows = a.shape[0] // count
    return sum(a[i * rows : (i + 1) * rows] for i in reversed(range(count)))


def iota(shape, axis):
    return lax.broadcasted_iota(jnp.int32, shape, axis)


def as_row(column):
    n = column.shape[0]
    return jnp.sum(jnp.where(iota((n, n), 0) == iota((n, n), 1), column, 0.0), 0, keepdims=True)


def position():
    return [lax.axis_index(a) for a in EVERY]


def inverse_rms(a):
    return lax.rsqrt(jnp.mean(a * a, axis=-1, keepdims=True) + EPS)


def probabilities(q, k, ctx_keys):
    n = q.shape[0]
    same = iota((n, n), 0) // DOC_LEN == iota((n, n), 1) // DOC_LEN
    ctx_exps = jnp.exp(dot_nt(q, ctx_keys) * FACTOR)
    own_exps = jnp.where(same, jnp.exp(dot_nt(q, k) * FACTOR), 0.0)
    total = jnp.sum(ctx_exps, 1, keepdims=True) + jnp.sum(own_exps, 1, keepdims=True)
    return ctx_exps / total, own_exps / total


def call(kernel, out_shape, in_specs, scratch=(), vmem=40, flops=10**9):
    in_specs = [
        pl.BlockSpec(memory_space=pl.ANY if s == "a" else pltpu.VMEM) for s in in_specs
    ]
    return pl.pallas_call(
        kernel,
        out_shape=out_shape,
        in_specs=in_specs,
        out_specs=jax.tree.map(lambda _: pl.BlockSpec(memory_space=pltpu.VMEM), out_shape),
        scratch_shapes=scratch,
        compiler_params=pltpu.CompilerParams(vmem_limit_bytes=vmem * 2**20),
        cost_estimate=pl.CostEstimate(flops=flops, bytes_accessed=4 * 10**6, transcendentals=0),
    )


def shape(*dims, dtype=f32):
    return jax.ShapeDtypeStruct(dims, dtype)


def forward_kernel(gain, wq, wk, wv, wo, ctx, own_block, o1, o2, o3, z0, z1, z2, z3, *refs):
    qkv, own, branch, mix, normed, ctx_columns, weights, last, sems = refs
    pos = position()
    fetch = [
        pltpu.make_async_copy(w, weights.at[:, pl.ds(i * HD, HD)], sems.at[i])
        for i, w in enumerate((wq, wk, wv))
    ]
    fetch.append(pltpu.make_async_copy(wo, last, sems.at[3]))
    for copy in fetch:
        copy.start()
    tok, feat = own_block.shape
    blocks = []
    for along_x, (near, far) in enumerate(((own_block, z0), (o1, z1), (o2, z2), (o3, z3))):
        blocks.append((near, 0, along_x, 0))
        blocks += [(far, i * tok, along_x, i + 1) for i in range(3)]
        for along_z in range(4):
            place = ((pos[0] - along_z) & 3) * 4 + ((pos[1] - along_x) & 3)
            rows = wide(far[3 * tok + along_z * 16 : 3 * tok + along_z * 16 + 16, :])
            ctx_columns[pl.ds(pl.multiple_of(place * 8, 8), 8), :] = rows[:8]
    docs = tok // DOC_LEN
    averaging = jnp.where(iota((8, tok), 0) == iota((8, tok), 1) // DOC_LEN, 1 / DOC_LEN, 0.0)
    averaging = averaging.astype(bf16)
    squares = jnp.zeros((tok, 1), f32)
    for ref, i, _, _ in blocks:
        rows = wide(ref[i : i + tok, :])
        squares = squares + jnp.sum(rows * rows, axis=1, keepdims=True)
    inv = lax.rsqrt(squares / (16 * feat) + EPS)
    total = jnp.zeros((tok, 3 * HD), f32)
    for copy in fetch[:3]:
        copy.wait()
    for ref, i, along_x, along_z in blocks:
        place = ((pos[0] - along_z) & 3) * 4 + ((pos[1] - along_x) & 3)
        here = pl.ds(pl.multiple_of(place * feat, feat), feat)
        rows = ref[i : i + tok, :]
        ready = (wide(rows) * inv * gain[:, here]).astype(bf16)
        normed[:, here] = ready
        total = total + dot(ready, weights[here, :])
        own[:, here] = dot(averaging, rows)[:docs]
    total = total.astype(bf16)
    qkv[...] = total
    q, k, v = total[:, :HD], total[:, HD : 2 * HD], total[:, 2 * HD :]
    ctx_probs, own_probs = probabilities(q, k, ctx[:, :HD])
    ctx_weights = ctx_probs.astype(bf16)
    mixture = dot(ctx_weights, ctx[:, HD:]) + dot(own_probs.astype(bf16), v)
    mean = dot(averaging, mixture.astype(bf16))
    mix[:, :HD] = mean[:docs]
    mix[:, HD:] = dot(averaging, ctx_weights)[:docs] * DOC_LEN
    fetch[3].wait()
    branch[...] = folded(dot(stacked_pieces(mean, 3), last[...]), 3)[:docs]


def by_token(a):
    rows = [jnp.broadcast_to(a[i : i + 1], (DOC_LEN, a.shape[1])) for i in range(4)]
    return jnp.concatenate(rows, axis=0)


def backward(own, ctx, upstream, grads, grad_ctx_keys):
    q, k, v = (own[:, j * HD : (j + 1) * HD] for j in range(3))
    ctx_probs, own_probs = probabilities(q, k, ctx[:, :HD])
    ctx_dweights = by_token(dot_nt(upstream.astype(bf16), ctx[:, HD:]))
    own_dweights = by_token(dot_nt(upstream.astype(bf16), v))
    inner = jnp.sum(ctx_probs * ctx_dweights, 1, keepdims=True)
    inner = inner + jnp.sum(own_probs * own_dweights, 1, keepdims=True)
    ctx_dscores = (ctx_probs * (ctx_dweights - inner) * FACTOR).astype(bf16)
    own_dscores = (own_probs * (own_dweights - inner) * FACTOR).astype(bf16)
    grad_ctx_keys[...] = dot_tn(ctx_dscores, q)
    grads[:, :HD] = (dot(ctx_dscores, ctx[:, :HD]) + dot(own_dscores, k)).astype(bf16)
    grads[:, HD : 2 * HD] = dot_tn(own_dscores, q).astype(bf16)
    grad_v = dot_tn(own_probs.astype(bf16), by_token(upstream).astype(bf16))
    grads[:, 2 * HD :] = grad_v.astype(bf16)


def loss_kernel(wo, mine, theirs, ctx, own, *refs):
    loss, grad_out, grads, grad_ctx_keys, grad_ctx_values, pooled, mix, weights, extra, slope, up = refs
    pos = position()
    width = wo.shape[1]
    co, y, dp = pos[4], pos[3], (pos[2] * 4 + pos[3]) * 2 + pos[4]
    for i in range(8):
        messages, core = (mine, co) if i < 4 else (theirs, 1 - co)
        here = pl.ds(pl.multiple_of((core * 4 + ((y - i % 4) & 3)) * 8, 8), 8)
        pooled[here, :] = messages[i % 4, :, :width]
        mix[here, :] = messages[i % 4, :, width : width + HD]
        weights[here, :] = messages[i % 4, :, width + HD : width + 2 * HD]
        extra[here, :] = messages[i % 4, :, width + 2 * HD :]
    n = pooled.shape[0]
    vectors = pooled[...]
    length = jnp.sqrt(jnp.sum(vectors * vectors, axis=1, keepdims=True) + 1e-06)
    unit = vectors / length
    parts = stacked_pieces(vectors, 3)
    products = dot_nt(parts, parts)
    gram = jnp.zeros((n, n), f32)
    for i, j in ((2, 1), (1, 2), (2, 0), (1, 1), (0, 2), (1, 0), (0, 1), (0, 0)):
        gram = gram + products[i * n : (i + 1) * n, j * n : (j + 1) * n]
    scores = gram / (length * as_row(length)) / TEMPERATURE
    diagonal = iota((n, n), 0) == iota((n, n), 1)

    def document(axis):
        at = iota((n, n), axis)
        return (((at >> 2) & 1) * 32 + ((at >> 3) & 3) * 8 + (at >> 5) * 4 + (at & 3)).astype(f32)

    partners = extra[:, 0:1]
    chosen = jnp.where(partners == document(1), 1.0, 0.0)
    chosen_back = jnp.where(as_row(partners) == document(0), 1.0, 0.0)
    exps = jnp.where(diagonal, 0.0, jnp.exp(scores))
    sums = jnp.sum(exps, axis=1, keepdims=True)
    picked = jnp.sum(scores * chosen, axis=1, keepdims=True)
    loss[...] = jnp.sum(jnp.log(sums) - picked, axis=0, keepdims=True) / n
    coeff = (exps / sums - chosen) / n * LOSS_SCALE
    coeff_back = (exps / as_row(sums) - chosen_back) / n * LOSS_SCALE
    lead, second, third = split(coeff + coeff_back, 3)
    units = split(unit, 3)
    left = jnp.concatenate([third, second, second, lead, lead, lead], axis=1)
    right = jnp.concatenate([units[i] for i in (0, 1, 0, 2, 1, 0)], axis=0)
    grad_unit = dot(left, right) / TEMPERATURE
    radial = jnp.sum(unit * grad_unit, axis=1, keepdims=True)
    slope[...] = (grad_unit - unit * radial) / length
    part = slope[:, pl.ds(pl.multiple_of(dp * (width // 16), width // 16), width // 16)]
    grad_out[...] = dot_tn(mix[...], part, EXACT)
    upstream = folded(dot_nt(stacked_pieces(slope[...] / DOC_LEN, 3), wo[...]), 3)
    up[...] = wide(upstream.astype(bf16))
    grad_ctx_values[...] = dot_tn(weights[...], up[...], EXACT)
    upstream = up[pl.ds(pl.multiple_of(co * (n // 2) + y * 8, 8), 8), :]
    upstream = jnp.where(pos[2] == 0, upstream[:4], upstream[4:])
    upstream = jnp.concatenate([upstream, upstream], axis=0)
    backward(own, ctx, upstream, grads, grad_ctx_keys)


def context_kernel(own, one, two, three, values, wk, wv, total, out0, out1, out2, out3, part):
    pos = position()
    half = part.shape[1]
    grad = (own[...] + two[...]) + (one[...] + three[...])
    grad = jnp.concatenate([grad, values[...]], axis=1)
    total[...] = grad
    here = pl.ds(pl.multiple_of(pos[4] * half, half), half)
    got = dot_nt(stacked_pieces(grad[:, :HD], 2), wk[here, :])
    got = got + dot_nt(stacked_pieces(grad[:, HD:], 2), wv[here, :])
    part[...] = folded(got, 2)
    for k, out in enumerate((out0, out1, out2, out3)):
        at = (pos[1] + k) & 3
        rows = [part[pl.ds(pl.multiple_of(z * 32 + at * 8, 8), 8), :] for z in range(4)]
        out[...] = jnp.concatenate(rows, axis=0).astype(out.dtype)


def middle_kernel(own, one, two, three, out0, out1, out2, out3, total):
    pos = position()
    total[...] = (own[...] + wide(two[...])) + (wide(one[...]) + wide(three[...]))
    for k, out in enumerate((out0, out1, out2, out3)):
        at = (pos[0] + k) & 3
        out[...] = total[pl.ds(pl.multiple_of(at * 8, 8), 8), :]


def finish_kernel(context, gain, mine, theirs, out):
    pos = position()
    half = mine.shape[1]
    low = pos[4] == 0
    grad = jnp.concatenate(
        [jnp.where(low, mine[...], theirs[...]), jnp.where(low, theirs[...], mine[...])], axis=1
    )
    rows = wide(context[...])
    inv = inverse_rms(rows)
    scaled = gain[...] * grad
    out[...] = inv * scaled - rows * inv**3 * jnp.mean(rows * scaled, axis=1, keepdims=True)


def weight_kernel(side, normed, grads, out):
    feat = out.shape[1]
    core = position()[4]
    core = core if side == 0 else 1 - core
    right = grads[...]
    for i in range(8):
        here = pl.ds(pl.multiple_of((i * 2 + core) * feat, feat), feat)
        out[i] = dot_tn(normed[:, here], right).astype(bf16)


def weight_y_kernel(mine, came, out0, out1, out2, out3):
    y = position()[3]
    for k, out in enumerate((out0, out1, out2, out3)):
        for zl in range(2):
            chip = zl * 4 + ((y + k) & 3)
            out[zl] = (wide(mine[chip]) + wide(came[chip])).astype(out.dtype)


def weight_z_kernel(own, one, two, three, mine, theirs):
    pos = position()
    for zl in range(2):
        got = (own[zl] + wide(two[zl])) + (wide(one[zl]) + wide(three[zl]))

        @pl.when(pos[2] == zl)
        def _():
            mine[...] = got

        @pl.when(pos[2] != zl)
        def _():
            theirs[...] = got.astype(bf16)


def weight_last_kernel(mine, theirs, ctx_columns, grad_ctx, grad_query, grad_key, grad_value):
    total = mine[...] + wide(theirs[...])
    columns = ctx_columns[...].astype(bf16)
    lead, rest = split(grad_ctx[...], 2)
    from_ctx = dot_tn(columns, rest) + dot_tn(columns, lead)
    grad_query[...] = total[:, :HD]
    grad_key[...] = total[:, HD : 2 * HD] + from_ctx[:, :HD]
    grad_value[...] = total[:, 2 * HD :] + from_ctx[:, HD:]


def shift(a, axis, k):
    return lax.ppermute(a, axis, [(i, (i + k) % 4) for i in range(4)])


def others(a, axis):
    return [shift(a, axis, k) for k in (1, 2, 3)]


def other(a, axis):
    return lax.ppermute(a, axis, [(0, 1), (1, 0)])


def pair(a, axis):
    b = other(a, axis)
    first = lax.axis_index(axis) == 0
    return jnp.where(first, jnp.concatenate([a, b]), jnp.concatenate([b, a]))


def ring_sum(a, axis):
    one, two, three = others(a, axis)
    return (a + two) + (one + three)


def spread(block, axis, size):
    copies = jnp.broadcast_to(block[None], (size,) + block.shape)
    return lax.all_to_all(copies, axis, 0, 0)


def shards(doc_states, context, gain, w_query, w_key, w_value, w_out, partners):
    tok, feat = doc_states.shape
    docs = tok // DOC_LEN
    width = w_query.shape[0]
    gain_row = gain.reshape(1, width)

    by_zh = others(doc_states, "zh")
    own_by_x = others(doc_states, "x")

    swap = [(c * 16 + d, d * 16 + c) for c in range(16) for d in range(16)]
    own_ctx = wide(context)
    own_ctx_normed = (own_ctx * inverse_rms(own_ctx) * gain).astype(bf16)
    named_rows = lax.ppermute(own_ctx_normed, EVERY, swap)
    columns = lax.dynamic_slice_in_dim(own_ctx_normed, lax.axis_index(DP) * feat, feat, 1)
    columns = jnp.concatenate([columns, jnp.zeros_like(columns)], axis=0)
    columns_by_zh = others(columns, "zh")

    from_zh = jnp.concatenate(by_zh + [columns] + columns_by_zh, axis=0)
    rows = [doc_states] + own_by_x + [from_zh] + others(from_zh, "x")

    named_rows, _ = lax.optimization_barrier((named_rows, from_zh))
    few = jnp.concatenate([dot(named_rows, w_key), dot(named_rows, w_value)], axis=1).astype(bf16)
    ctx_kv = spread(few, DP, 16).reshape(-1, 2 * HD)

    qkv, own_mean, branch, mix, normed, ctx_columns = call(
        forward_kernel,
        (
            shape(tok, 3 * HD, dtype=bf16),
            shape(docs, width),
            shape(docs, width),
            shape(docs, 2 * HD),
            shape(tok, width, dtype=bf16),
            shape(HD, feat),
        ),
        ["v"] + ["a"] * 4 + ["v"] * 9,
        scratch=[
            pltpu.VMEM((width, 3 * HD), bf16),
            pltpu.VMEM((HD, width), bf16),
            pltpu.SemaphoreType.DMA((4,)),
        ],
    )(gain_row, w_query, w_key, w_value, w_out, ctx_kv, *rows)

    pooled = own_mean + ring_sum(ring_sum(branch, "x"), "zh")
    message = jnp.concatenate(
        [pooled, mix, jnp.pad(wide(partners)[:, None], ((0, 0), (0, HD - 1)))], axis=1
    )
    message = pair(message, "zl")
    messages = jnp.stack([message] + others(message, "y"))
    total = 64
    loss, grad_out, grads, grad_ctx_keys, grad_ctx_values = call(
        loss_kernel,
        (
            shape(1, 1),
            shape(HD, feat),
            shape(tok, 3 * HD, dtype=bf16),
            shape(HD, HD),
            shape(HD, HD),
        ),
        ["v"] * 5,
        scratch=[
            pltpu.VMEM((total, width), f32),
            pltpu.VMEM((total, HD), f32),
            pltpu.VMEM((total, HD), f32),
            pltpu.VMEM((total, HD), f32),
            pltpu.VMEM((total, width), f32),
            pltpu.VMEM((total, HD), f32),
        ],
    )(w_out, messages, other(messages, "co"), ctx_kv, qkv)

    half = width // 2
    rows = 4 * context.shape[0]
    came = other(grad_ctx_keys, "co")
    came, grads = lax.optimization_barrier((came, grads))
    grad_ctx_keys = grad_ctx_keys + came
    grad_ctx_keys = grad_ctx_keys + other(grad_ctx_keys, "zl")
    by_y = others(grad_ctx_keys, "y")
    grad_ctx, part, *sent = call(
        context_kernel,
        (shape(HD, 2 * HD), shape(rows, half)) + (shape(rows, half, dtype=bf16),) * 3,
        ["v"] * 7,
        scratch=[pltpu.VMEM((4 * rows, half), f32)],
    )(grad_ctx_keys, *by_y, grad_ctx_values, w_key, w_value)
    came = [shift(a, "x", k) for k, a in zip((1, 2, 3), sent)]
    part, *sent = call(
        middle_kernel,
        (shape(rows // 4, half),) * 4,
        ["v"] * 4,
        scratch=[pltpu.VMEM((rows, half), f32)],
    )(part, *came)
    one, two, three = [shift(a, "zh", k) for k, a in zip((1, 2, 3), sent)]
    part = (part + two) + (one + three)
    grad_context = call(finish_kernel, shape(*context.shape), ["v"] * 4, flops=10**9)(
        context, gain_row, part, other(part, "co")
    )

    theirs, mine = (
        call(
            functools.partial(weight_kernel, side),
            shape(8, feat, 3 * HD, dtype=bf16),
            ["v"] * 2,
        )(normed, grads)
        for side in (1, 0)
    )
    came, _ = lax.optimization_barrier((other(theirs, "co"), by_y[0]))
    mine, *sent = call(
        weight_y_kernel,
        (shape(2, feat, 3 * HD),) + (shape(2, feat, 3 * HD, dtype=bf16),) * 3,
        ["v"] * 2,
    )(mine, came)
    came = [shift(a, "y", k) for k, a in zip((1, 2, 3), sent)]
    mine, theirs = call(
        weight_z_kernel,
        (shape(feat, 3 * HD), shape(feat, 3 * HD, dtype=bf16)),
        ["v"] * 4,
    )(mine, *came)
    grad_query, grad_key, grad_value = call(
        weight_last_kernel, (shape(feat, HD),) * 3, ["v"] * 4
    )(mine, other(theirs, "zl"), ctx_columns, grad_ctx)
    return loss.reshape(()), grad_context, grad_query, grad_key, grad_value, grad_out


def solution(mesh):
    split = Mesh(mesh.devices.reshape(4, 4, 2, 4, 2), EVERY)
    in_specs = (
        P(DP, CTX),
        P(CTX, None),
        P(),
        P(None, CTX),
        P(None, CTX),
        P(None, CTX),
        P(CTX, None),
        P(DP),
    )
    out_specs = (P(), P(CTX, None), P(DP, CTX), P(DP, CTX), P(DP, CTX), P(CTX, DP))
    return jax.shard_map(
        shards, mesh=split, in_specs=in_specs, out_specs=out_specs, check_vma=False
    )
```

```python
import functools

import jax
import jax.numpy as jnp
from jax import lax
from jax.experimental import pallas as pl
from jax.experimental.pallas import tpu as pltpu
from jax.sharding import Mesh, PartitionSpec as P

HD = 128
DOC_LEN = 64

EPS = 1e-05
TEMPERATURE = 0.05
LOSS_SCALE = 65536.0
EXACT = lax.Precision.HIGHEST
FACTOR = HD**-0.5

CTX = ("zh", "x")
DP = ("zl", "y", "co")
EVERY = CTX + DP

f32 = jnp.float32
bf16 = jnp.bfloat16

ROWS_BY_ROWS = (((1,), (1,)), ((), ()))
COLS_BY_COLS = (((0,), (0,)), ((), ()))


def wide(a):
    return a.astype(f32)


def dot(a, b):
    return jnp.dot(a, b, preferred_element_type=f32)


def dot_nt(a, b, precision=None):
    return lax.dot_general(a, b, ROWS_BY_ROWS, precision=precision, preferred_element_type=f32)


def dot_tn(a, b, precision=None):
    return lax.dot_general(a, b, COLS_BY_COLS, precision=precision, preferred_element_type=f32)


def split(a, count):
    out = []
    for _ in range(count):
        head = a.astype(bf16)
        out.append(head)
        a = a - wide(head)
    return out


def stacked_pieces(a, count):
    return jnp.concatenate(split(a, count), axis=0)


def folded(a, count):
    rows = a.shape[0] // count
    return sum(a[i * rows : (i + 1) * rows] for i in reversed(range(count)))


def iota(shape, axis):
    return lax.broadcasted_iota(jnp.int32, shape, axis)


def as_row(column):
    n = column.shape[0]
    return jnp.sum(jnp.where(iota((n, n), 0) == iota((n, n), 1), column, 0.0), 0, keepdims=True)


def position():
    return [lax.axis_index(a) for a in EVERY]


def inverse_rms(a):
    return lax.rsqrt(jnp.mean(a * a, axis=-1, keepdims=True) + EPS)


def probabilities(q, k, ctx_keys):
    n = q.shape[0]
    same = iota((n, n), 0) // DOC_LEN == iota((n, n), 1) // DOC_LEN
    ctx_exps = jnp.exp(dot_nt(q, ctx_keys) * FACTOR)
    own_exps = jnp.where(same, jnp.exp(dot_nt(q, k) * FACTOR), 0.0)
    total = jnp.sum(ctx_exps, 1, keepdims=True) + jnp.sum(own_exps, 1, keepdims=True)
    return ctx_exps / total, own_exps / total


def call(kernel, out_shape, in_specs, scratch=(), vmem=16, flops=10**9):
    in_specs = [
        pl.BlockSpec(memory_space=pl.ANY if s == "a" else pltpu.VMEM) for s in in_specs
    ]
    return pl.pallas_call(
        kernel,
        out_shape=out_shape,
        in_specs=in_specs,
        out_specs=jax.tree.map(lambda _: pl.BlockSpec(memory_space=pltpu.VMEM), out_shape),
        scratch_shapes=scratch,
        compiler_params=pltpu.CompilerParams(vmem_limit_bytes=vmem * 2**20),
        cost_estimate=pl.CostEstimate(flops=flops, bytes_accessed=4 * 10**6, transcendentals=0),
    )


def shape(*dims, dtype=f32):
    return jax.ShapeDtypeStruct(dims, dtype)


def forward_kernel(gain, partners, wq, wk, wv, wo, ctx, z0, z1, z2, z3, *refs):
    qkv, own, branch, mix, normed, ctx_columns, weights, last, sems = refs
    pos = position()
    fetch = [
        pltpu.make_async_copy(w, weights.at[:, pl.ds(i * HD, HD)], sems.at[i])
        for i, w in enumerate((wq, wk, wv))
    ]
    fetch.append(pltpu.make_async_copy(wo, last, sems.at[3]))
    for copy in fetch:
        copy.start()
    tok, feat = qkv.shape[0], z0.shape[2]
    blocks = []
    for along_x, ref in enumerate((z0, z1, z2, z3)):
        blocks += [(ref, i, along_x, i) for i in range(4)]
        for i in range(4):
            place = ((pos[0] - i) & 3) * 4 + ((pos[1] - along_x) & 3)
            ctx_columns[pl.ds(pl.multiple_of(place * 8, 8), 8), :] = wide(ref[i, tok:, :])[:8]
    ctx_inv = jnp.sum(wide(ctx[:, 2 * HD :]), axis=1, keepdims=True)
    dp = (pos[2] * 4 + pos[3]) * 2 + pos[4]
    here = pl.ds(pl.multiple_of(dp * feat, feat), feat)
    ctx_columns[...] = ctx_columns[...] * ctx_inv * gain[:, here]
    docs = tok // DOC_LEN
    averaging = jnp.where(iota((8, tok), 0) == iota((8, tok), 1) // DOC_LEN, 1 / DOC_LEN, 0.0)
    averaging = averaging.astype(bf16)
    squares = jnp.zeros((tok, 1), f32)
    for ref, i, _, _ in blocks:
        rows = wide(ref[i, :tok, :])
        squares = squares + jnp.sum(rows * rows, axis=1, keepdims=True)
    inv = lax.rsqrt(squares / (16 * feat) + EPS)
    total = jnp.zeros((tok, 3 * HD), f32)
    for copy in fetch[:3]:
        copy.wait()
    for ref, i, along_x, along_z in blocks:
        place = ((pos[0] - along_z) & 3) * 4 + ((pos[1] - along_x) & 3)
        here = pl.ds(pl.multiple_of(place * feat, feat), feat)
        rows = ref[i, :tok, :]
        ready = (wide(rows) * inv * gain[:, here]).astype(bf16)
        normed[:, here] = ready
        total = total + dot(ready, weights[here, :])
        own[:, here] = dot(averaging, rows)[:docs]
    total = total.astype(bf16)
    qkv[...] = total
    q, k, v = total[:, :HD], total[:, HD : 2 * HD], total[:, 2 * HD :]
    ctx_probs, own_probs = probabilities(q, k, ctx[:, :HD])
    ctx_weights = ctx_probs.astype(bf16)
    mixture = dot(ctx_weights, ctx[:, HD : 2 * HD]) + dot(own_probs.astype(bf16), v)
    mean = dot(averaging, mixture.astype(bf16))
    mix[:, :HD] = mean[:docs]
    mix[:, HD : 2 * HD] = dot(averaging, ctx_weights)[:docs] * DOC_LEN
    mix[:, 2 * HD :] = jnp.broadcast_to(wide(partners[...]), (docs, HD))
    fetch[3].wait()
    branch[...] = folded(dot(stacked_pieces(mean, 3), last[...]), 3)[:docs]


def by_token(a):
    rows = [jnp.broadcast_to(a[i : i + 1], (DOC_LEN, a.shape[1])) for i in range(4)]
    return jnp.concatenate(rows, axis=0)


def backward(own, ctx, upstream, grads, grad_ctx_keys):
    q, k, v = (own[:, j * HD : (j + 1) * HD] for j in range(3))
    ctx_probs, own_probs = probabilities(q, k, ctx[:, :HD])
    ctx_dweights = by_token(dot_nt(upstream.astype(bf16), ctx[:, HD : 2 * HD]))
    own_dweights = by_token(dot_nt(upstream.astype(bf16), v))
    inner = jnp.sum(ctx_probs * ctx_dweights, 1, keepdims=True)
    inner = inner + jnp.sum(own_probs * own_dweights, 1, keepdims=True)
    ctx_dscores = (ctx_probs * (ctx_dweights - inner) * FACTOR).astype(bf16)
    own_dscores = (own_probs * (own_dweights - inner) * FACTOR).astype(bf16)
    grad_ctx_keys[...] = dot_tn(ctx_dscores, q)
    grads[:, :HD] = (dot(ctx_dscores, ctx[:, :HD]) + dot(own_dscores, k)).astype(bf16)
    grads[:, HD : 2 * HD] = dot_tn(own_dscores, q).astype(bf16)
    grad_v = dot_tn(own_probs.astype(bf16), by_token(upstream).astype(bf16))
    grads[:, 2 * HD :] = grad_v.astype(bf16)


def loss_kernel(wo, mine, theirs, ctx, own, *refs):
    loss, grad_out, grads, grad_ctx_keys, grad_ctx_values, pooled, mix, weights, extra, slope, up = refs
    pos = position()
    width = wo.shape[1]
    co, y, dp = pos[4], pos[3], (pos[2] * 4 + pos[3]) * 2 + pos[4]
    for i in range(8):
        messages, core = (mine, co) if i < 4 else (theirs, 1 - co)
        here = pl.ds(pl.multiple_of((core * 4 + ((y - i % 4) & 3)) * 8, 8), 8)
        pooled[here, :] = messages[i % 4, :, :width]
        mix[here, :] = messages[i % 4, :, width : width + HD]
        weights[here, :] = messages[i % 4, :, width + HD : width + 2 * HD]
        extra[here, :] = messages[i % 4, :, width + 2 * HD :]
    n = pooled.shape[0]
    vectors = pooled[...]
    length = jnp.sqrt(jnp.sum(vectors * vectors, axis=1, keepdims=True) + 1e-06)
    unit = vectors / length
    parts = stacked_pieces(vectors, 3)
    products = dot_nt(parts, parts)
    gram = jnp.zeros((n, n), f32)
    for i, j in ((2, 1), (1, 2), (2, 0), (1, 1), (0, 2), (1, 0), (0, 1), (0, 0)):
        gram = gram + products[i * n : (i + 1) * n, j * n : (j + 1) * n]
    scores = gram / (length * as_row(length)) / TEMPERATURE
    diagonal = iota((n, n), 0) == iota((n, n), 1)

    def document(axis):
        at = iota((n, n), axis)
        return (((at >> 2) & 1) * 32 + ((at >> 3) & 3) * 8 + (at >> 5) * 4 + (at & 3)).astype(f32)

    partners = extra[:, 0:1]
    chosen = jnp.where(partners == document(1), 1.0, 0.0)
    chosen_back = jnp.where(as_row(partners) == document(0), 1.0, 0.0)
    exps = jnp.where(diagonal, 0.0, jnp.exp(scores))
    sums = jnp.sum(exps, axis=1, keepdims=True)
    picked = jnp.sum(scores * chosen, axis=1, keepdims=True)
    loss[...] = jnp.sum(jnp.log(sums) - picked, axis=0, keepdims=True) / n
    coeff = (exps / sums - chosen) / n * LOSS_SCALE
    coeff_back = (exps / as_row(sums) - chosen_back) / n * LOSS_SCALE
    lead, second, third = split(coeff + coeff_back, 3)
    units = split(unit, 3)
    left = jnp.concatenate([third, second, second, lead, lead, lead], axis=1)
    right = jnp.concatenate([units[i] for i in (0, 1, 0, 2, 1, 0)], axis=0)
    grad_unit = dot(left, right) / TEMPERATURE
    radial = jnp.sum(unit * grad_unit, axis=1, keepdims=True)
    slope[...] = (grad_unit - unit * radial) / length
    part = slope[:, pl.ds(pl.multiple_of(dp * (width // 16), width // 16), width // 16)]
    grad_out[...] = dot_tn(mix[...], part, EXACT)
    upstream = folded(dot_nt(stacked_pieces(slope[...] / DOC_LEN, 3), wo[...]), 3)
    up[...] = wide(upstream.astype(bf16))
    grad_ctx_values[...] = dot_tn(weights[...], up[...], EXACT)
    upstream = up[pl.ds(pl.multiple_of(co * (n // 2) + y * 8, 8), 8), :]
    upstream = jnp.where(pos[2] == 0, upstream[:4], upstream[4:])
    upstream = jnp.concatenate([upstream, upstream], axis=0)
    backward(own, ctx, upstream, grads, grad_ctx_keys)


def context_kernel(own, one, two, three, values, wk, wv, total, out0, out1, out2, out3, part):
    pos = position()
    half = part.shape[1]
    grad = (own[...] + two[...]) + (one[...] + three[...])
    grad = jnp.concatenate([grad, values[...]], axis=1)
    total[...] = grad
    here = pl.ds(pl.multiple_of(pos[4] * half, half), half)
    got = dot_nt(stacked_pieces(grad[:, :HD], 2), wk[here, :])
    got = got + dot_nt(stacked_pieces(grad[:, HD:], 2), wv[here, :])
    part[...] = folded(got, 2)
    for k, out in enumerate((out0, out1, out2, out3)):
        at = (pos[1] + k) & 3
        rows = [part[pl.ds(pl.multiple_of(z * 32 + at * 8, 8), 8), :] for z in range(4)]
        out[...] = jnp.concatenate(rows, axis=0).astype(out.dtype)


def middle_kernel(own, one, two, three, out0, out1, out2, out3, total):
    pos = position()
    total[...] = (own[...] + wide(two[...])) + (wide(one[...]) + wide(three[...]))
    for k, out in enumerate((out0, out1, out2, out3)):
        at = (pos[0] + k) & 3
        out[...] = total[pl.ds(pl.multiple_of(at * 8, 8), 8), :]


def finish_kernel(context, gain, mine, theirs, out):
    pos = position()
    half = mine.shape[1]
    low = pos[4] == 0
    grad = jnp.concatenate(
        [jnp.where(low, mine[...], theirs[...]), jnp.where(low, theirs[...], mine[...])], axis=1
    )
    rows = wide(context[...])
    inv = inverse_rms(rows)
    scaled = gain[...] * grad
    out[...] = inv * scaled - rows * inv**3 * jnp.mean(rows * scaled, axis=1, keepdims=True)


def weight_kernel(side, normed, grads, out):
    feat = out.shape[1]
    core = position()[4]
    core = core if side == 0 else 1 - core
    right = grads[...]
    for i in range(8):
        here = pl.ds(pl.multiple_of((i * 2 + core) * feat, feat), feat)
        out[i] = dot_tn(normed[:, here], right).astype(bf16)


def weight_y_kernel(mine, came, out0, out1, out2, out3):
    y = position()[3]
    for k, out in enumerate((out0, out1, out2, out3)):
        for zl in range(2):
            chip = zl * 4 + ((y + k) & 3)
            out[zl] = (wide(mine[chip]) + wide(came[chip])).astype(out.dtype)


def weight_z_kernel(own, one, two, three, mine, theirs):
    pos = position()
    for zl in range(2):
        got = (own[zl] + wide(two[zl])) + (wide(one[zl]) + wide(three[zl]))

        @pl.when(pos[2] == zl)
        def _():
            mine[...] = got

        @pl.when(pos[2] != zl)
        def _():
            theirs[...] = got.astype(bf16)


def weight_last_kernel(mine, theirs, ctx_columns, grad_ctx, grad_query, grad_key, grad_value):
    total = mine[...] + wide(theirs[...])
    columns = ctx_columns[...].astype(bf16)
    lead, rest = split(grad_ctx[...], 2)
    from_ctx = dot_tn(columns, rest) + dot_tn(columns, lead)
    grad_query[...] = total[:, :HD]
    grad_key[...] = total[:, HD : 2 * HD] + from_ctx[:, :HD]
    grad_value[...] = total[:, 2 * HD :] + from_ctx[:, HD:]


def shift(a, axis, k):
    return lax.ppermute(a, axis, [(i, (i + k) % 4) for i in range(4)])


def others(a, axis):
    return [shift(a, axis, k) for k in (1, 2, 3)]


def other(a, axis):
    return lax.ppermute(a, axis, [(0, 1), (1, 0)])


def pair(a, axis):
    b = other(a, axis)
    first = lax.axis_index(axis) == 0
    return jnp.where(first, jnp.concatenate([a, b]), jnp.concatenate([b, a]))


def ring_sum(a, axis):
    one, two, three = others(a, axis)
    return (a + two) + (one + three)


def hlo_split(a, count):
    out = []
    for _ in range(count):
        out.append(lax.reduce_precision(a, 8, 7))
        a = a - out[-1]
    return out


def spread(block, axis, size):
    copies = jnp.broadcast_to(block[None], (size,) + block.shape)
    return lax.all_to_all(copies, axis, 0, 0)


def shards(doc_states, context, gain, w_query, w_key, w_value, w_out, partners):
    tok, feat = doc_states.shape
    docs = tok // DOC_LEN
    width = w_query.shape[0]
    gain_row = gain.reshape(1, width)

    ctx_part = lax.dynamic_slice_in_dim(context, lax.axis_index(DP) * feat, feat, 1)
    block = jnp.concatenate([doc_states, ctx_part, jnp.zeros_like(ctx_part)], axis=0)
    block = jnp.stack([block] + others(block, "zh"))
    rows = [block] + others(block, "x")

    swap = [(c * 16 + d, d * 16 + c) for c in range(16) for d in range(16)]
    named_rows = wide(lax.ppermute(context, EVERY, swap))
    named_rows, _ = lax.optimization_barrier((named_rows, block))
    inv = inverse_rms(named_rows)
    named_rows = (named_rows * inv * gain).astype(bf16)
    few = [dot(named_rows, w_key), dot(named_rows, w_value)] + hlo_split(inv, 3)
    few = jnp.concatenate([a.astype(bf16) for a in few], axis=1)
    few = jnp.pad(few, ((0, 0), (0, 3 * HD - few.shape[1])))
    ctx_kv = spread(few, DP, 16).reshape(-1, 3 * HD)

    qkv, own_mean, branch, mix, normed, ctx_columns = call(
        forward_kernel,
        (
            shape(tok, 3 * HD, dtype=bf16),
            shape(docs, width),
            shape(docs, width),
            shape(docs, 3 * HD),
            shape(tok, width, dtype=bf16),
            shape(HD, feat),
        ),
        ["v"] * 2 + ["a"] * 4 + ["v"] * 5,
        scratch=[
            pltpu.VMEM((width, 3 * HD), bf16),
            pltpu.VMEM((HD, width), bf16),
            pltpu.SemaphoreType.DMA((4,)),
        ],
        vmem=24,
    )(gain_row, partners[:, None], w_query, w_key, w_value, w_out, ctx_kv, *rows)

    pooled = own_mean + ring_sum(ring_sum(branch, "x"), "zh")
    message = jnp.concatenate([pooled, mix], axis=1)
    message = pair(message, "zl")
    messages = jnp.stack([message] + others(message, "y"))
    total = 64
    loss, grad_out, grads, grad_ctx_keys, grad_ctx_values = call(
        loss_kernel,
        (
            shape(1, 1),
            shape(HD, feat),
            shape(tok, 3 * HD, dtype=bf16),
            shape(HD, HD),
            shape(HD, HD),
        ),
        ["v"] * 5,
        scratch=[
            pltpu.VMEM((total, width), f32),
            pltpu.VMEM((total, HD), f32),
            pltpu.VMEM((total, HD), f32),
            pltpu.VMEM((total, HD), f32),
            pltpu.VMEM((total, width), f32),
            pltpu.VMEM((total, HD), f32),
        ],
        vmem=24,
    )(w_out, messages, other(messages, "co"), ctx_kv, qkv)

    half = width // 2
    rows = 4 * context.shape[0]
    came = other(grad_ctx_keys, "co")
    came, grads = lax.optimization_barrier((came, grads))
    grad_ctx_keys = grad_ctx_keys + came
    grad_ctx_keys = grad_ctx_keys + other(grad_ctx_keys, "zl")
    by_y = others(grad_ctx_keys, "y")
    grad_ctx, part, *sent = call(
        context_kernel,
        (shape(HD, 2 * HD), shape(rows, half)) + (shape(rows, half, dtype=bf16),) * 3,
        ["v"] * 7,
        scratch=[pltpu.VMEM((4 * rows, half), f32)],
    )(grad_ctx_keys, *by_y, grad_ctx_values, w_key, w_value)
    came = [shift(a, "x", k) for k, a in zip((1, 2, 3), sent)]
    part, *sent = call(
        middle_kernel,
        (shape(rows // 4, half),) * 4,
        ["v"] * 4,
        scratch=[pltpu.VMEM((rows, half), f32)],
    )(part, *came)
    one, two, three = [shift(a, "zh", k) for k, a in zip((1, 2, 3), sent)]
    part = (part + two) + (one + three)
    grad_context = call(finish_kernel, shape(*context.shape), ["v"] * 4, flops=10**9)(
        context, gain_row, part, other(part, "co")
    )

    theirs, mine = (
        call(
            functools.partial(weight_kernel, side),
            shape(8, feat, 3 * HD, dtype=bf16),
            ["v"] * 2,
        )(normed, grads)
        for side in (1, 0)
    )
    came, _ = lax.optimization_barrier((other(theirs, "co"), by_y[0]))
    mine, *sent = call(
        weight_y_kernel,
        (shape(2, feat, 3 * HD),) + (shape(2, feat, 3 * HD, dtype=bf16),) * 3,
        ["v"] * 2,
    )(mine, came)
    came = [shift(a, "y", k) for k, a in zip((1, 2, 3), sent)]
    mine, theirs = call(
        weight_z_kernel,
        (shape(feat, 3 * HD), shape(feat, 3 * HD, dtype=bf16)),
        ["v"] * 4,
    )(mine, *came)
    grad_query, grad_key, grad_value = call(
        weight_last_kernel, (shape(feat, HD),) * 3, ["v"] * 4
    )(mine, other(theirs, "zl"), ctx_columns, grad_ctx)
    return loss.reshape(()), grad_context, grad_query, grad_key, grad_value, grad_out


def solution(mesh):
    split = Mesh(mesh.devices.reshape(4, 4, 2, 4, 2), EVERY)
    in_specs = (
        P(DP, CTX),
        P(CTX, None),
        P(),
        P(None, CTX),
        P(None, CTX),
        P(None, CTX),
        P(CTX, None),
        P(DP),
    )
    out_specs = (P(), P(CTX, None), P(DP, CTX), P(DP, CTX), P(DP, CTX), P(CTX, DP))
    return jax.shard_map(
        shards, mesh=split, in_specs=in_specs, out_specs=out_specs, check_vma=False
    )
```

```python
import functools

import jax
import jax.numpy as jnp
from jax import lax
from jax.experimental import pallas as pl
from jax.experimental.pallas import tpu as pltpu
from jax.sharding import Mesh, PartitionSpec as P

HD = 128
DOC_LEN = 64

EPS = 1e-05
TEMPERATURE = 0.05
LOSS_SCALE = 65536.0
EXACT = lax.Precision.HIGHEST
FACTOR = HD**-0.5

CTX = ("zh", "x")
DP = ("zl", "y", "co")
EVERY = CTX + DP

f32 = jnp.float32
bf16 = jnp.bfloat16

ROWS_BY_ROWS = (((1,), (1,)), ((), ()))
COLS_BY_COLS = (((0,), (0,)), ((), ()))


def wide(a):
    return a.astype(f32)


def dot(a, b):
    return jnp.dot(a, b, preferred_element_type=f32)


def dot_nt(a, b, precision=None):
    return lax.dot_general(a, b, ROWS_BY_ROWS, precision=precision, preferred_element_type=f32)


def dot_tn(a, b, precision=None):
    return lax.dot_general(a, b, COLS_BY_COLS, precision=precision, preferred_element_type=f32)


def split(a, count):
    out = []
    for _ in range(count):
        head = a.astype(bf16)
        out.append(head)
        a = a - wide(head)
    return out


def stacked_pieces(a, count):
    return jnp.concatenate(split(a, count), axis=0)


def folded(a, count):
    rows = a.shape[0] // count
    return sum(a[i * rows : (i + 1) * rows] for i in reversed(range(count)))


def iota(shape, axis):
    return lax.broadcasted_iota(jnp.int32, shape, axis)


def as_row(column):
    n = column.shape[0]
    return jnp.sum(jnp.where(iota((n, n), 0) == iota((n, n), 1), column, 0.0), 0, keepdims=True)


def position():
    return [lax.axis_index(a) for a in EVERY]


def inverse_rms(a):
    return lax.rsqrt(jnp.mean(a * a, axis=-1, keepdims=True) + EPS)


def probabilities(q, k, ctx_keys):
    n = q.shape[0]
    same = iota((n, n), 0) // DOC_LEN == iota((n, n), 1) // DOC_LEN
    ctx_exps = jnp.exp(dot_nt(q, ctx_keys) * FACTOR)
    own_exps = jnp.where(same, jnp.exp(dot_nt(q, k) * FACTOR), 0.0)
    total = jnp.sum(ctx_exps, 1, keepdims=True) + jnp.sum(own_exps, 1, keepdims=True)
    return ctx_exps / total, own_exps / total


def call(kernel, out_shape, in_specs, scratch=(), vmem=16, flops=10**9):
    spaces = {"a": pl.ANY, "h": pltpu.HBM, "v": pltpu.VMEM}
    in_specs = [pl.BlockSpec(memory_space=spaces[s]) for s in in_specs]
    return pl.pallas_call(
        kernel,
        out_shape=out_shape,
        in_specs=in_specs,
        out_specs=jax.tree.map(lambda _: pl.BlockSpec(memory_space=pltpu.VMEM), out_shape),
        scratch_shapes=scratch,
        compiler_params=pltpu.CompilerParams(vmem_limit_bytes=vmem * 2**20),
        cost_estimate=pl.CostEstimate(flops=flops, bytes_accessed=4 * 10**6, transcendentals=0),
    )


def shape(*dims, dtype=f32):
    return jax.ShapeDtypeStruct(dims, dtype)


def forward_kernel(gain, partners, ctx, wq, wk, wv, wo, *refs):
    pieces, refs = refs[:8], refs[8:]
    qkv, own, branch, mix, normed, ctx_columns, weights, last, blocks, sems = refs
    pos = position()
    tok, feat = qkv.shape[0], blocks.shape[2]
    fetch = []
    for i, (near, far) in enumerate(zip(pieces[:4], pieces[4:])):
        fetch.append((near, blocks.at[4 * i]))
        fetch.append((far, blocks.at[pl.ds(4 * i + 1, 3)]))
    fetch += [(w, weights.at[:, pl.ds(i * HD, HD)]) for i, w in enumerate((wq, wk, wv))]
    fetch.append((wo, last))
    fetch = [pltpu.make_async_copy(a, b, sems.at[i]) for i, (a, b) in enumerate(fetch)]
    for copy in fetch:
        copy.start()
    for copy in fetch[:8]:
        copy.wait()
    places = [((pos[0] - i % 4) & 3) * 4 + ((pos[1] - i // 4) & 3) for i in range(16)]
    for i, place in enumerate(places):
        here = pl.ds(pl.multiple_of(place * 8, 8), 8)
        ctx_columns[here, :] = wide(blocks[i, tok:, :])[:8]
    ctx_inv = jnp.sum(wide(ctx[:, 2 * HD :]), axis=1, keepdims=True)
    dp = (pos[2] * 4 + pos[3]) * 2 + pos[4]
    here = pl.ds(pl.multiple_of(dp * feat, feat), feat)
    ctx_columns[...] = ctx_columns[...] * ctx_inv * gain[:, here]
    docs = tok // DOC_LEN
    averaging = jnp.where(iota((8, tok), 0) == iota((8, tok), 1) // DOC_LEN, 1 / DOC_LEN, 0.0)
    averaging = averaging.astype(bf16)
    squares = jnp.zeros((tok, 1), f32)
    for i in range(16):
        rows = wide(blocks[i, :tok, :])
        squares = squares + jnp.sum(rows * rows, axis=1, keepdims=True)
    inv = lax.rsqrt(squares / (16 * feat) + EPS)
    total = jnp.zeros((tok, 3 * HD), f32)
    for copy in fetch[8:11]:
        copy.wait()
    for i, place in enumerate(places):
        here = pl.ds(pl.multiple_of(place * feat, feat), feat)
        rows = blocks[i, :tok, :]
        ready = (wide(rows) * inv * gain[:, here]).astype(bf16)
        normed[:, here] = ready
        total = total + dot(ready, weights[here, :])
        own[:, here] = dot(averaging, rows)[:docs]
    total = total.astype(bf16)
    qkv[...] = total
    q, k, v = total[:, :HD], total[:, HD : 2 * HD], total[:, 2 * HD :]
    ctx_probs, own_probs = probabilities(q, k, ctx[:, :HD])
    ctx_weights = ctx_probs.astype(bf16)
    mixture = dot(ctx_weights, ctx[:, HD : 2 * HD]) + dot(own_probs.astype(bf16), v)
    mean = dot(averaging, mixture.astype(bf16))
    mix[:, :HD] = mean[:docs]
    mix[:, HD : 2 * HD] = dot(averaging, ctx_weights)[:docs] * DOC_LEN
    mix[:, 2 * HD :] = jnp.broadcast_to(wide(partners[...]), (docs, HD))
    fetch[11].wait()
    branch[...] = folded(dot(stacked_pieces(mean, 3), last[...]), 3)[:docs]


def by_token(a):
    rows = [jnp.broadcast_to(a[i : i + 1], (DOC_LEN, a.shape[1])) for i in range(4)]
    return jnp.concatenate(rows, axis=0)


def backward(own, ctx, upstream, grads, grad_ctx_keys):
    q, k, v = (own[:, j * HD : (j + 1) * HD] for j in range(3))
    ctx_probs, own_probs = probabilities(q, k, ctx[:, :HD])
    ctx_dweights = by_token(dot_nt(upstream.astype(bf16), ctx[:, HD : 2 * HD]))
    own_dweights = by_token(dot_nt(upstream.astype(bf16), v))
    inner = jnp.sum(ctx_probs * ctx_dweights, 1, keepdims=True)
    inner = inner + jnp.sum(own_probs * own_dweights, 1, keepdims=True)
    ctx_dscores = (ctx_probs * (ctx_dweights - inner) * FACTOR).astype(bf16)
    own_dscores = (own_probs * (own_dweights - inner) * FACTOR).astype(bf16)
    grad_ctx_keys[...] = dot_tn(ctx_dscores, q)
    grads[:, :HD] = (dot(ctx_dscores, ctx[:, :HD]) + dot(own_dscores, k)).astype(bf16)
    grads[:, HD : 2 * HD] = dot_tn(own_dscores, q).astype(bf16)
    grad_v = dot_tn(own_probs.astype(bf16), by_token(upstream).astype(bf16))
    grads[:, 2 * HD :] = grad_v.astype(bf16)


def loss_kernel(wo, mine, theirs, ctx, own, *refs):
    loss, grad_out, grads, grad_ctx_keys, grad_ctx_values, pooled, mix, weights, extra, slope, up = refs
    pos = position()
    width = wo.shape[1]
    co, y, dp = pos[4], pos[3], (pos[2] * 4 + pos[3]) * 2 + pos[4]
    for i in range(8):
        messages, core = (mine, co) if i < 4 else (theirs, 1 - co)
        here = pl.ds(pl.multiple_of((core * 4 + ((y - i % 4) & 3)) * 8, 8), 8)
        pooled[here, :] = messages[i % 4, :, :width]
        mix[here, :] = messages[i % 4, :, width : width + HD]
        weights[here, :] = messages[i % 4, :, width + HD : width + 2 * HD]
        extra[here, :] = messages[i % 4, :, width + 2 * HD :]
    n = pooled.shape[0]
    vectors = pooled[...]
    length = jnp.sqrt(jnp.sum(vectors * vectors, axis=1, keepdims=True) + 1e-06)
    unit = vectors / length
    parts = stacked_pieces(vectors, 3)
    products = dot_nt(parts, parts)
    gram = jnp.zeros((n, n), f32)
    for i, j in ((2, 1), (1, 2), (2, 0), (1, 1), (0, 2), (1, 0), (0, 1), (0, 0)):
        gram = gram + products[i * n : (i + 1) * n, j * n : (j + 1) * n]
    scores = gram / (length * as_row(length)) / TEMPERATURE
    diagonal = iota((n, n), 0) == iota((n, n), 1)

    def document(axis):
        at = iota((n, n), axis)
        return (((at >> 2) & 1) * 32 + ((at >> 3) & 3) * 8 + (at >> 5) * 4 + (at & 3)).astype(f32)

    partners = extra[:, 0:1]
    chosen = jnp.where(partners == document(1), 1.0, 0.0)
    chosen_back = jnp.where(as_row(partners) == document(0), 1.0, 0.0)
    exps = jnp.where(diagonal, 0.0, jnp.exp(scores))
    sums = jnp.sum(exps, axis=1, keepdims=True)
    picked = jnp.sum(scores * chosen, axis=1, keepdims=True)
    loss[...] = jnp.sum(jnp.log(sums) - picked, axis=0, keepdims=True) / n
    coeff = (exps / sums - chosen) / n * LOSS_SCALE
    coeff_back = (exps / as_row(sums) - chosen_back) / n * LOSS_SCALE
    lead, second, third = split(coeff + coeff_back, 3)
    units = split(unit, 3)
    left = jnp.concatenate([third, second, second, lead, lead, lead], axis=1)
    right = jnp.concatenate([units[i] for i in (0, 1, 0, 2, 1, 0)], axis=0)
    grad_unit = dot(left, right) / TEMPERATURE
    radial = jnp.sum(unit * grad_unit, axis=1, keepdims=True)
    slope[...] = (grad_unit - unit * radial) / length
    part = slope[:, pl.ds(pl.multiple_of(dp * (width // 16), width // 16), width // 16)]
    grad_out[...] = dot_tn(mix[...], part, EXACT)
    upstream = folded(dot_nt(stacked_pieces(slope[...] / DOC_LEN, 3), wo[...]), 3)
    up[...] = wide(upstream.astype(bf16))
    grad_ctx_values[...] = dot_tn(weights[...], up[...], EXACT)
    upstream = up[pl.ds(pl.multiple_of(co * (n // 2) + y * 8, 8), 8), :]
    upstream = jnp.where(pos[2] == 0, upstream[:4], upstream[4:])
    upstream = jnp.concatenate([upstream, upstream], axis=0)
    backward(own, ctx, upstream, grads, grad_ctx_keys)


def context_kernel(own, one, two, three, values, wk, wv, total, out0, out1, out2, out3, part):
    pos = position()
    half = part.shape[1]
    grad = (own[...] + two[...]) + (one[...] + three[...])
    grad = jnp.concatenate([grad, values[...]], axis=1)
    total[...] = grad
    here = pl.ds(pl.multiple_of(pos[4] * half, half), half)
    got = dot_nt(stacked_pieces(grad[:, :HD], 2), wk[here, :])
    got = got + dot_nt(stacked_pieces(grad[:, HD:], 2), wv[here, :])
    part[...] = folded(got, 2)
    for k, out in enumerate((out0, out1, out2, out3)):
        at = (pos[1] + k) & 3
        rows = [part[pl.ds(pl.multiple_of(z * 32 + at * 8, 8), 8), :] for z in range(4)]
        out[...] = jnp.concatenate(rows, axis=0).astype(out.dtype)


def middle_kernel(own, one, two, three, out0, out1, out2, out3, total):
    pos = position()
    total[...] = (own[...] + wide(two[...])) + (wide(one[...]) + wide(three[...]))
    for k, out in enumerate((out0, out1, out2, out3)):
        at = (pos[0] + k) & 3
        out[...] = total[pl.ds(pl.multiple_of(at * 8, 8), 8), :]


def finish_kernel(context, gain, mine, theirs, out):
    pos = position()
    half = mine.shape[1]
    low = pos[4] == 0
    grad = jnp.concatenate(
        [jnp.where(low, mine[...], theirs[...]), jnp.where(low, theirs[...], mine[...])], axis=1
    )
    rows = wide(context[...])
    inv = inverse_rms(rows)
    scaled = gain[...] * grad
    out[...] = inv * scaled - rows * inv**3 * jnp.mean(rows * scaled, axis=1, keepdims=True)


def weight_kernel(side, normed, grads, out):
    feat = out.shape[1]
    core = position()[4]
    core = core if side == 0 else 1 - core
    right = grads[...]
    for i in range(8):
        here = pl.ds(pl.multiple_of((i * 2 + core) * feat, feat), feat)
        out[i] = dot_tn(normed[:, here], right).astype(bf16)


def weight_y_kernel(mine, came, out0, out1, out2, out3):
    y = position()[3]
    for k, out in enumerate((out0, out1, out2, out3)):
        for zl in range(2):
            chip = zl * 4 + ((y + k) & 3)
            out[zl] = (wide(mine[chip]) + wide(came[chip])).astype(out.dtype)


def weight_z_kernel(own, one, two, three, mine, theirs):
    pos = position()
    for zl in range(2):
        got = (own[zl] + wide(two[zl])) + (wide(one[zl]) + wide(three[zl]))

        @pl.when(pos[2] == zl)
        def _():
            mine[...] = got

        @pl.when(pos[2] != zl)
        def _():
            theirs[...] = got.astype(bf16)


def weight_last_kernel(mine, theirs, ctx_columns, grad_ctx, grad_query, grad_key, grad_value):
    total = mine[...] + wide(theirs[...])
    columns = ctx_columns[...].astype(bf16)
    lead, rest = split(grad_ctx[...], 2)
    from_ctx = dot_tn(columns, rest) + dot_tn(columns, lead)
    grad_query[...] = total[:, :HD]
    grad_key[...] = total[:, HD : 2 * HD] + from_ctx[:, :HD]
    grad_value[...] = total[:, 2 * HD :] + from_ctx[:, HD:]


def shift(a, axis, k):
    return lax.ppermute(a, axis, [(i, (i + k) % 4) for i in range(4)])


def others(a, axis):
    return [shift(a, axis, k) for k in (1, 2, 3)]


def other(a, axis):
    return lax.ppermute(a, axis, [(0, 1), (1, 0)])


def pair(a, axis):
    b = other(a, axis)
    first = lax.axis_index(axis) == 0
    return jnp.where(first, jnp.concatenate([a, b]), jnp.concatenate([b, a]))


def ring_sum(a, axis):
    one, two, three = others(a, axis)
    return (a + two) + (one + three)


def hlo_split(a, count):
    out = []
    for _ in range(count):
        out.append(lax.reduce_precision(a, 8, 7))
        a = a - out[-1]
    return out


def spread(block, axis, size):
    copies = jnp.broadcast_to(block[None], (size,) + block.shape)
    return lax.all_to_all(copies, axis, 0, 0)


def shards(doc_states, context, gain, w_query, w_key, w_value, w_out, partners):
    tok, feat = doc_states.shape
    docs = tok // DOC_LEN
    width = w_query.shape[0]
    gain_row = gain.reshape(1, width)

    ctx_part = lax.dynamic_slice_in_dim(context, lax.axis_index(DP) * feat, feat, 1)
    block = jnp.concatenate([doc_states, ctx_part, jnp.zeros_like(ctx_part)], axis=0)
    from_zh = jnp.stack(others(block, "zh"))
    rows = [block] + others(block, "x") + [from_zh] + others(from_zh, "x")

    swap = [(c * 16 + d, d * 16 + c) for c in range(16) for d in range(16)]
    named_rows = wide(lax.ppermute(context, EVERY, swap))
    named_rows, _ = lax.optimization_barrier((named_rows, from_zh))
    inv = inverse_rms(named_rows)
    named_rows = (named_rows * inv * gain).astype(bf16)
    few = [dot(named_rows, w_key), dot(named_rows, w_value)] + hlo_split(inv, 3)
    few = jnp.concatenate([a.astype(bf16) for a in few], axis=1)
    few = jnp.pad(few, ((0, 0), (0, 3 * HD - few.shape[1])))
    ctx_kv = spread(few, DP, 16).reshape(-1, 3 * HD)

    qkv, own_mean, branch, mix, normed, ctx_columns = call(
        forward_kernel,
        (
            shape(tok, 3 * HD, dtype=bf16),
            shape(docs, width),
            shape(docs, width),
            shape(docs, 3 * HD),
            shape(tok, width, dtype=bf16),
            shape(HD, feat),
        ),
        ["v"] * 3 + ["h"] * 4 + ["a"] * 8,
        scratch=[
            pltpu.VMEM((width, 3 * HD), bf16),
            pltpu.VMEM((HD, width), bf16),
            pltpu.VMEM((16,) + block.shape, bf16),
            pltpu.SemaphoreType.DMA((12,)),
        ],
        vmem=24,
    )(gain_row, partners[:, None], ctx_kv, w_query, w_key, w_value, w_out, *rows)

    branch = ring_sum(branch, "x") + own_mean / 4
    message = spread(jnp.concatenate([branch, mix], axis=1), ("zh", "zl"), 8)
    message = message.reshape(4, 2 * docs, -1)
    mix = lax.dynamic_index_in_dim(message[:, :, width:], lax.axis_index("zh"), 0, keepdims=False)
    message = jnp.concatenate([jnp.sum(message[:, :, :width], axis=0), mix], axis=1)
    messages = jnp.stack([message] + others(message, "y"))
    total = 64
    loss, grad_out, grads, grad_ctx_keys, grad_ctx_values = call(
        loss_kernel,
        (
            shape(1, 1),
            shape(HD, feat),
            shape(tok, 3 * HD, dtype=bf16),
            shape(HD, HD),
            shape(HD, HD),
        ),
        ["v"] * 5,
        scratch=[
            pltpu.VMEM((total, width), f32),
            pltpu.VMEM((total, HD), f32),
            pltpu.VMEM((total, HD), f32),
            pltpu.VMEM((total, HD), f32),
            pltpu.VMEM((total, width), f32),
            pltpu.VMEM((total, HD), f32),
        ],
        vmem=24,
    )(w_out, messages, other(messages, "co"), ctx_kv, qkv)

    half = width // 2
    rows = 4 * context.shape[0]
    came = other(grad_ctx_keys, "co")
    came, grads = lax.optimization_barrier((came, grads))
    grad_ctx_keys = grad_ctx_keys + came
    grad_ctx_keys = grad_ctx_keys + other(grad_ctx_keys, "zl")
    by_y = others(grad_ctx_keys, "y")
    grad_ctx, part, *sent = call(
        context_kernel,
        (shape(HD, 2 * HD), shape(rows, half)) + (shape(rows, half, dtype=bf16),) * 3,
        ["v"] * 7,
        scratch=[pltpu.VMEM((4 * rows, half), f32)],
    )(grad_ctx_keys, *by_y, grad_ctx_values, w_key, w_value)
    came = [shift(a, "x", k) for k, a in zip((1, 2, 3), sent)]
    part, *sent = call(
        middle_kernel,
        (shape(rows // 4, half),) * 4,
        ["v"] * 4,
        scratch=[pltpu.VMEM((rows, half), f32)],
    )(part, *came)
    one, two, three = [shift(a, "zh", k) for k, a in zip((1, 2, 3), sent)]
    part = (part + two) + (one + three)
    grad_context = call(finish_kernel, shape(*context.shape), ["v"] * 4, flops=10**9)(
        context, gain_row, part, other(part, "co")
    )

    theirs, mine = (
        call(
            functools.partial(weight_kernel, side),
            shape(8, feat, 3 * HD, dtype=bf16),
            ["v"] * 2,
        )(normed, grads)
        for side in (1, 0)
    )
    came, _ = lax.optimization_barrier((other(theirs, "co"), by_y[0]))
    mine, *sent = call(
        weight_y_kernel,
        (shape(2, feat, 3 * HD),) + (shape(2, feat, 3 * HD, dtype=bf16),) * 3,
        ["v"] * 2,
    )(mine, came)
    came = [shift(a, "y", k) for k, a in zip((1, 2, 3), sent)]
    mine, theirs = call(
        weight_z_kernel,
        (shape(feat, 3 * HD), shape(feat, 3 * HD, dtype=bf16)),
        ["v"] * 4,
    )(mine, *came)
    grad_query, grad_key, grad_value = call(
        weight_last_kernel, (shape(feat, HD),) * 3, ["v"] * 4
    )(mine, other(theirs, "zl"), ctx_columns, grad_ctx)
    return loss.reshape(()), grad_context, grad_query, grad_key, grad_value, grad_out


def solution(mesh):
    split = Mesh(mesh.devices.reshape(4, 4, 2, 4, 2), EVERY)
    in_specs = (
        P(DP, CTX),
        P(CTX, None),
        P(),
        P(None, CTX),
        P(None, CTX),
        P(None, CTX),
        P(CTX, None),
        P(DP),
    )
    out_specs = (P(), P(CTX, None), P(DP, CTX), P(DP, CTX), P(DP, CTX), P(CTX, DP))
    return jax.shard_map(
        shards, mesh=split, in_specs=in_specs, out_specs=out_specs, check_vma=False
    )
```

```python
import functools

import jax
import jax.numpy as jnp
from jax import lax
from jax.experimental import pallas as pl
from jax.experimental.pallas import tpu as pltpu
from jax.sharding import Mesh, PartitionSpec as P

HD = 128
DOC_LEN = 64

EPS = 1e-05
TEMPERATURE = 0.05
LOSS_SCALE = 65536.0
EXACT = lax.Precision.HIGHEST
FACTOR = HD**-0.5

CTX = ("zh", "x")
DP = ("zl", "y", "co")
EVERY = CTX + DP

f32 = jnp.float32
bf16 = jnp.bfloat16

ROWS_BY_ROWS = (((1,), (1,)), ((), ()))
COLS_BY_COLS = (((0,), (0,)), ((), ()))


def wide(a):
    return a.astype(f32)


def dot(a, b):
    return jnp.dot(a, b, preferred_element_type=f32)


def dot_nt(a, b, precision=None):
    return lax.dot_general(a, b, ROWS_BY_ROWS, precision=precision, preferred_element_type=f32)


def dot_tn(a, b, precision=None):
    return lax.dot_general(a, b, COLS_BY_COLS, precision=precision, preferred_element_type=f32)


def split(a, count):
    out = []
    for _ in range(count):
        head = a.astype(bf16)
        out.append(head)
        a = a - wide(head)
    return out


def stacked_pieces(a, count):
    return jnp.concatenate(split(a, count), axis=0)


def folded(a, count):
    rows = a.shape[0] // count
    return sum(a[i * rows : (i + 1) * rows] for i in reversed(range(count)))


def iota(shape, axis):
    return lax.broadcasted_iota(jnp.int32, shape, axis)


def as_row(column):
    n = column.shape[0]
    return jnp.sum(jnp.where(iota((n, n), 0) == iota((n, n), 1), column, 0.0), 0, keepdims=True)


def position():
    return [lax.axis_index(a) for a in EVERY]


def inverse_rms(a):
    return lax.rsqrt(jnp.mean(a * a, axis=-1, keepdims=True) + EPS)


def probabilities(q, k, ctx_keys):
    n = q.shape[0]
    same = iota((n, n), 0) // DOC_LEN == iota((n, n), 1) // DOC_LEN
    ctx_exps = jnp.exp(dot_nt(q, ctx_keys) * FACTOR)
    own_exps = jnp.where(same, jnp.exp(dot_nt(q, k) * FACTOR), 0.0)
    total = jnp.sum(ctx_exps, 1, keepdims=True) + jnp.sum(own_exps, 1, keepdims=True)
    return ctx_exps / total, own_exps / total


def call(kernel, out_shape, in_specs, scratch=(), vmem=16, flops=10**9, accessed=0):
    in_specs = [
        pl.BlockSpec(memory_space=pl.ANY if s == "a" else pltpu.VMEM) for s in in_specs
    ]
    return pl.pallas_call(
        kernel,
        out_shape=out_shape,
        in_specs=in_specs,
        out_specs=jax.tree.map(lambda _: pl.BlockSpec(memory_space=pltpu.VMEM), out_shape),
        scratch_shapes=scratch,
        compiler_params=pltpu.CompilerParams(vmem_limit_bytes=vmem * 2**20),
        cost_estimate=pl.CostEstimate(flops=flops, bytes_accessed=accessed, transcendentals=0),
    )


def shape(*dims, dtype=f32):
    return jax.ShapeDtypeStruct(dims, dtype)


def block_kernel(rows, context, out):
    pos = position()
    tok, feat = rows.shape
    out[:tok, :] = rows[...]
    here = ((pos[2] * 4 + pos[3]) * 2 + pos[4]) * feat
    part = wide(context[:, pl.ds(pl.multiple_of(here, feat), feat)])
    out[tok:, :] = jnp.concatenate([part, jnp.zeros_like(part)], axis=0).astype(bf16)


def forward_kernel(gain, partners, wq, wk, wv, wo, ctx, *refs):
    pieces, refs = refs[:4], refs[4:]
    qkv, own, branch, mix, normed, ctx_columns, weights, last, stacks, sems = refs
    pos = position()
    fetch = [
        pltpu.make_async_copy(w, weights.at[:, pl.ds(i * HD, HD)], sems.at[i])
        for i, w in enumerate((wq, wk, wv))
    ]
    fetch.append(pltpu.make_async_copy(wo, last, sems.at[3]))
    arrive = [
        pltpu.make_async_copy(piece, stacks.at[i], sems.at[4 + i]) for i, piece in enumerate(pieces)
    ]
    for copy in arrive + fetch:
        copy.start()
    tok, feat = qkv.shape[0], stacks.shape[3]
    for copy in arrive:
        copy.wait()
    blocks = []
    for along_x in range(4):
        ref = stacks.at[along_x]
        blocks += [(ref, i, along_x, i) for i in range(4)]
        for i in range(4):
            place = ((pos[0] - i) & 3) * 4 + ((pos[1] - along_x) & 3)
            ctx_columns[pl.ds(pl.multiple_of(place * 8, 8), 8), :] = wide(ref[i, tok:, :])[:8]
    ctx_inv = jnp.sum(wide(ctx[:, 2 * HD :]), axis=1, keepdims=True)
    dp = (pos[2] * 4 + pos[3]) * 2 + pos[4]
    here = pl.ds(pl.multiple_of(dp * feat, feat), feat)
    ctx_columns[...] = ctx_columns[...] * ctx_inv * gain[:, here]
    docs = tok // DOC_LEN
    averaging = jnp.where(iota((8, tok), 0) == iota((8, tok), 1) // DOC_LEN, 1 / DOC_LEN, 0.0)
    averaging = averaging.astype(bf16)
    squares = jnp.zeros((tok, 1), f32)
    for ref, i, _, _ in blocks:
        rows = wide(ref[i, :tok, :])
        squares = squares + jnp.sum(rows * rows, axis=1, keepdims=True)
    inv = lax.rsqrt(squares / (16 * feat) + EPS)
    total = jnp.zeros((tok, 3 * HD), f32)
    for copy in fetch[:3]:
        copy.wait()
    for ref, i, along_x, along_z in blocks:
        place = ((pos[0] - along_z) & 3) * 4 + ((pos[1] - along_x) & 3)
        here = pl.ds(pl.multiple_of(place * feat, feat), feat)
        rows = ref[i, :tok, :]
        ready = (wide(rows) * inv * gain[:, here]).astype(bf16)
        normed[:, here] = ready
        total = total + dot(ready, weights[here, :])
        own[:, here] = dot(averaging, rows)[:docs]
    total = total.astype(bf16)
    qkv[...] = total
    q, k, v = total[:, :HD], total[:, HD : 2 * HD], total[:, 2 * HD :]
    ctx_probs, own_probs = probabilities(q, k, ctx[:, :HD])
    ctx_weights = ctx_probs.astype(bf16)
    mixture = dot(ctx_weights, ctx[:, HD : 2 * HD]) + dot(own_probs.astype(bf16), v)
    mean = dot(averaging, mixture.astype(bf16))
    mix[:, :HD] = mean[:docs]
    mix[:, HD : 2 * HD] = dot(averaging, ctx_weights)[:docs] * DOC_LEN
    mix[:, 2 * HD :] = jnp.broadcast_to(wide(partners[...]), (docs, HD))
    fetch[3].wait()
    branch[...] = folded(dot(stacked_pieces(mean, 3), last[...]), 3)[:docs]


def by_token(a):
    rows = [jnp.broadcast_to(a[i : i + 1], (DOC_LEN, a.shape[1])) for i in range(4)]
    return jnp.concatenate(rows, axis=0)


def backward(own, ctx, upstream, grads, grad_ctx_keys):
    q, k, v = (own[:, j * HD : (j + 1) * HD] for j in range(3))
    ctx_probs, own_probs = probabilities(q, k, ctx[:, :HD])
    ctx_dweights = by_token(dot_nt(upstream.astype(bf16), ctx[:, HD : 2 * HD]))
    own_dweights = by_token(dot_nt(upstream.astype(bf16), v))
    inner = jnp.sum(ctx_probs * ctx_dweights, 1, keepdims=True)
    inner = inner + jnp.sum(own_probs * own_dweights, 1, keepdims=True)
    ctx_dscores = (ctx_probs * (ctx_dweights - inner) * FACTOR).astype(bf16)
    own_dscores = (own_probs * (own_dweights - inner) * FACTOR).astype(bf16)
    grad_ctx_keys[...] = dot_tn(ctx_dscores, q)
    grads[:, :HD] = (dot(ctx_dscores, ctx[:, :HD]) + dot(own_dscores, k)).astype(bf16)
    grads[:, HD : 2 * HD] = dot_tn(own_dscores, q).astype(bf16)
    grad_v = dot_tn(own_probs.astype(bf16), by_token(upstream).astype(bf16))
    grads[:, 2 * HD :] = grad_v.astype(bf16)


def loss_kernel(wo, ctx, own, *refs):
    messages, refs = refs[:8], refs[8:]
    loss, grad_out, grads, grad_ctx_keys, grad_ctx_values, pooled, mix, weights, extra, slope, up = refs
    pos = position()
    width = wo.shape[1]
    co, y, dp = pos[4], pos[3], (pos[2] * 4 + pos[3]) * 2 + pos[4]
    for i in range(8):
        message, core = messages[i], co if i < 4 else 1 - co
        here = pl.ds(pl.multiple_of((core * 4 + ((y - i % 4) & 3)) * 8, 8), 8)
        pooled[here, :] = message[:, :width]
        mix[here, :] = message[:, width : width + HD]
        weights[here, :] = message[:, width + HD : width + 2 * HD]
        extra[here, :] = message[:, width + 2 * HD :]
    n = pooled.shape[0]
    vectors = pooled[...]
    length = jnp.sqrt(jnp.sum(vectors * vectors, axis=1, keepdims=True) + 1e-06)
    unit = vectors / length
    parts = stacked_pieces(vectors, 3)
    products = dot_nt(parts, parts)
    gram = jnp.zeros((n, n), f32)
    for i, j in ((2, 1), (1, 2), (2, 0), (1, 1), (0, 2), (1, 0), (0, 1), (0, 0)):
        gram = gram + products[i * n : (i + 1) * n, j * n : (j + 1) * n]
    scores = gram / (length * as_row(length)) / TEMPERATURE
    diagonal = iota((n, n), 0) == iota((n, n), 1)

    def document(axis):
        at = iota((n, n), axis)
        return (((at >> 2) & 1) * 32 + ((at >> 3) & 3) * 8 + (at >> 5) * 4 + (at & 3)).astype(f32)

    partners = extra[:, 0:1]
    chosen = jnp.where(partners == document(1), 1.0, 0.0)
    chosen_back = jnp.where(as_row(partners) == document(0), 1.0, 0.0)
    exps = jnp.where(diagonal, 0.0, jnp.exp(scores))
    sums = jnp.sum(exps, axis=1, keepdims=True)
    picked = jnp.sum(scores * chosen, axis=1, keepdims=True)
    loss[...] = jnp.sum(jnp.log(sums) - picked, axis=0, keepdims=True) / n
    coeff = (exps / sums - chosen) / n * LOSS_SCALE
    coeff_back = (exps / as_row(sums) - chosen_back) / n * LOSS_SCALE
    lead, second, third = split(coeff + coeff_back, 3)
    units = split(unit, 3)
    left = jnp.concatenate([third, second, second, lead, lead, lead], axis=1)
    right = jnp.concatenate([units[i] for i in (0, 1, 0, 2, 1, 0)], axis=0)
    grad_unit = dot(left, right) / TEMPERATURE
    radial = jnp.sum(unit * grad_unit, axis=1, keepdims=True)
    slope[...] = (grad_unit - unit * radial) / length
    part = slope[:, pl.ds(pl.multiple_of(dp * (width // 16), width // 16), width // 16)]
    grad_out[...] = dot_tn(mix[...], part, EXACT)
    upstream = folded(dot_nt(stacked_pieces(slope[...] / DOC_LEN, 3), wo[...]), 3)
    up[...] = wide(upstream.astype(bf16))
    grad_ctx_values[...] = dot_tn(weights[...], up[...], EXACT)
    upstream = up[pl.ds(pl.multiple_of(co * (n // 2) + y * 8, 8), 8), :]
    upstream = jnp.where(pos[2] == 0, upstream[:4], upstream[4:])
    upstream = jnp.concatenate([upstream, upstream], axis=0)
    backward(own, ctx, upstream, grads, grad_ctx_keys)


def context_kernel(one, two, values, wk, wv, total, out0, out1, out2, out3, part):
    pos = position()
    half = part.shape[1]
    grad = one[...] + two[...]
    grad = jnp.concatenate([grad, values[...]], axis=1)
    total[...] = grad
    here = pl.ds(pl.multiple_of(pos[4] * half, half), half)
    got = dot_nt(stacked_pieces(grad[:, :HD], 2), wk[here, :])
    got = got + dot_nt(stacked_pieces(grad[:, HD:], 2), wv[here, :])
    part[...] = folded(got, 2)
    for k, out in enumerate((out0, out1, out2, out3)):
        at = (pos[1] + k) & 3
        rows = [part[pl.ds(pl.multiple_of(z * 32 + at * 8, 8), 8), :] for z in range(4)]
        out[...] = jnp.concatenate(rows, axis=0).astype(out.dtype)


def middle_kernel(own, one, two, three, out0, out1, out2, out3, total):
    pos = position()
    total[...] = (own[...] + wide(two[...])) + (wide(one[...]) + wide(three[...]))
    for k, out in enumerate((out0, out1, out2, out3)):
        at = (pos[0] + k) & 3
        out[...] = total[pl.ds(pl.multiple_of(at * 8, 8), 8), :].astype(out.dtype)


def finish_kernel(context, gain, mine, theirs, out):
    pos = position()
    half = mine.shape[1]
    low = pos[4] == 0
    grad = jnp.concatenate(
        [jnp.where(low, mine[...], theirs[...]), jnp.where(low, theirs[...], mine[...])], axis=1
    )
    rows = wide(context[...])
    inv = inverse_rms(rows)
    scaled = gain[...] * grad
    out[...] = inv * scaled - rows * inv**3 * jnp.mean(rows * scaled, axis=1, keepdims=True)


def weight_kernel(side, normed, grads, out):
    feat = out.shape[1]
    core = position()[4]
    core = core if side == 0 else 1 - core
    right = grads[...]
    for i in range(8):
        here = pl.ds(pl.multiple_of((i * 2 + core) * feat, feat), feat)
        out[i] = dot_tn(normed[:, here], right).astype(bf16)


def weight_y_kernel(mine, came, out0, out1, out2, out3):
    y = position()[3]
    for k, out in enumerate((out0, out1, out2, out3)):
        for zl in range(2):
            chip = zl * 4 + ((y + k) & 3)
            out[zl] = (wide(mine[chip]) + wide(came[chip])).astype(out.dtype)


def weight_z_kernel(own, one, two, three, mine, theirs):
    pos = position()
    for zl in range(2):
        got = (own[zl] + wide(two[zl])) + (wide(one[zl]) + wide(three[zl]))

        @pl.when(pos[2] == zl)
        def _():
            mine[...] = got

        @pl.when(pos[2] != zl)
        def _():
            theirs[...] = got.astype(bf16)


def weight_last_kernel(mine, theirs, ctx_columns, grad_ctx, grad_query, grad_key, grad_value):
    total = mine[...] + wide(theirs[...])
    columns = ctx_columns[...].astype(bf16)
    lead, rest = split(grad_ctx[...], 2)
    from_ctx = dot_tn(columns, rest) + dot_tn(columns, lead)
    grad_query[...] = total[:, :HD]
    grad_key[...] = total[:, HD : 2 * HD] + from_ctx[:, :HD]
    grad_value[...] = total[:, 2 * HD :] + from_ctx[:, HD:]


def shift(a, axis, k):
    return lax.ppermute(a, axis, [(i, (i + k) % 4) for i in range(4)])


def others(a, axis):
    return [shift(a, axis, k) for k in (1, 2, 3)]


def other(a, axis):
    return lax.ppermute(a, axis, [(0, 1), (1, 0)])


def pair(a, axis):
    b = other(a, axis)
    first = lax.axis_index(axis) == 0
    return jnp.where(first, jnp.concatenate([a, b]), jnp.concatenate([b, a]))


def ring_sum(a, axis):
    one, two, three = others(a, axis)
    return (a + two) + (one + three)


def hlo_split(a, count):
    out = []
    for _ in range(count):
        out.append(lax.reduce_precision(a, 8, 7))
        a = a - out[-1]
    return out


def spread(block, axis, size):
    copies = jnp.broadcast_to(block[None], (size,) + block.shape)
    return lax.all_to_all(copies, axis, 0, 0)


def shards(doc_states, context, gain, w_query, w_key, w_value, w_out, partners):
    tok, feat = doc_states.shape
    docs = tok // DOC_LEN
    width = w_query.shape[0]
    gain_row = gain.reshape(1, width)

    block = call(block_kernel, shape(tok + 16, feat, dtype=bf16), ["v"] * 2)(doc_states, context)
    block = jnp.stack([block] + others(block, "zh"))
    rows = [block] + others(block, "x")

    swap = [(c * 16 + d, d * 16 + c) for c in range(16) for d in range(16)]
    named_rows = wide(lax.ppermute(context, EVERY, swap))
    named_rows, _ = lax.optimization_barrier((named_rows, block))
    inv = inverse_rms(named_rows)
    named_rows = (named_rows * inv * gain).astype(bf16)
    few = [dot(named_rows, w_key), dot(named_rows, w_value)] + hlo_split(inv, 3)
    few = jnp.concatenate([a.astype(bf16) for a in few], axis=1)
    few = jnp.pad(few, ((0, 0), (0, 3 * HD - few.shape[1])))
    ctx_kv = spread(few, DP, 16).reshape(-1, 3 * HD)

    qkv, own_mean, branch, mix, normed, ctx_columns = call(
        forward_kernel,
        (
            shape(tok, 3 * HD, dtype=bf16),
            shape(docs, width),
            shape(docs, width),
            shape(docs, 3 * HD),
            shape(tok, width, dtype=bf16),
            shape(HD, feat),
        ),
        ["v"] * 2 + ["a"] * 4 + ["v"] + ["a"] * 4,
        scratch=[
            pltpu.VMEM((width, 3 * HD), bf16),
            pltpu.VMEM((HD, width), bf16),
            pltpu.VMEM((4,) + block.shape, bf16),
            pltpu.SemaphoreType.DMA((8,)),
        ],
        vmem=24,
    )(gain_row, partners[:, None], w_query, w_key, w_value, w_out, ctx_kv, *rows)

    pooled = own_mean + ring_sum(ring_sum(branch, "x"), "zh")
    message = jnp.concatenate([pooled, mix], axis=1)
    message = pair(message, "zl")
    messages = [message] + others(message, "y")
    total = 64
    loss, grad_out, grads, grad_ctx_keys, grad_ctx_values = call(
        loss_kernel,
        (
            shape(1, 1),
            shape(HD, feat),
            shape(tok, 3 * HD, dtype=bf16),
            shape(HD, HD),
            shape(HD, HD),
        ),
        ["v"] * 11,
        scratch=[
            pltpu.VMEM((total, width), f32),
            pltpu.VMEM((total, HD), f32),
            pltpu.VMEM((total, HD), f32),
            pltpu.VMEM((total, HD), f32),
            pltpu.VMEM((total, width), f32),
            pltpu.VMEM((total, HD), f32),
        ],
        vmem=24,
    )(w_out, ctx_kv, qkv, *messages, *[other(m, "co") for m in messages])

    half = width // 2
    rows = 4 * context.shape[0]
    one, two, three = others(grad_ctx_keys, "y")
    by_y = (grad_ctx_keys + two) + (one + three)
    grad_ctx_keys = by_y + other(by_y, "co")
    grad_ctx, part, *sent = call(
        context_kernel,
        (shape(HD, 2 * HD), shape(rows, half)) + (shape(rows, half, dtype=bf16),) * 3,
        ["v"] * 5,
        scratch=[pltpu.VMEM((4 * rows, half), f32)],
    )(grad_ctx_keys, other(grad_ctx_keys, "zl"), grad_ctx_values, w_key, w_value)
    came = [shift(a, "x", k) for k, a in zip((1, 2, 3), sent)]
    part, *sent = call(
        middle_kernel,
        (shape(rows // 4, half),) + (shape(rows // 4, half, dtype=bf16),) * 3,
        ["v"] * 4,
        scratch=[pltpu.VMEM((rows, half), f32)],
    )(part, *came)
    one, two, three = [wide(shift(a, "zh", k)) for k, a in zip((1, 2, 3), sent)]
    part = (part + two) + (one + three)
    grad_context = call(finish_kernel, shape(*context.shape), ["v"] * 4, flops=10**9)(
        context, gain_row, part, other(part, "co")
    )

    theirs, mine = (
        call(
            functools.partial(weight_kernel, side),
            shape(8, feat, 3 * HD, dtype=bf16),
            ["v"] * 2,
        )(normed, grads)
        for side in (1, 0)
    )
    came, _ = lax.optimization_barrier((other(theirs, "co"), by_y))
    mine, *sent = call(
        weight_y_kernel,
        (shape(2, feat, 3 * HD),) + (shape(2, feat, 3 * HD, dtype=bf16),) * 3,
        ["v"] * 2,
    )(mine, came)
    came = [shift(a, "y", k) for k, a in zip((1, 2, 3), sent)]
    mine, theirs = call(
        weight_z_kernel,
        (shape(feat, 3 * HD), shape(feat, 3 * HD, dtype=bf16)),
        ["v"] * 4,
    )(mine, *came)
    grad_query, grad_key, grad_value = call(
        weight_last_kernel, (shape(feat, HD),) * 3, ["v"] * 4
    )(mine, other(theirs, "zl"), ctx_columns, grad_ctx)
    return loss.reshape(()), grad_context, grad_query, grad_key, grad_value, grad_out


def solution(mesh):
    split = Mesh(mesh.devices.reshape(4, 4, 2, 4, 2), EVERY)
    in_specs = (
        P(DP, CTX),
        P(CTX, None),
        P(),
        P(None, CTX),
        P(None, CTX),
        P(None, CTX),
        P(CTX, None),
        P(DP),
    )
    out_specs = (P(), P(CTX, None), P(DP, CTX), P(DP, CTX), P(DP, CTX), P(CTX, DP))
    return jax.shard_map(
        shards, mesh=split, in_specs=in_specs, out_specs=out_specs, check_vma=False
    )
```

```python
import functools

import jax
import jax.numpy as jnp
from jax import lax
from jax.experimental import pallas as pl
from jax.experimental.pallas import tpu as pltpu
from jax.sharding import Mesh, PartitionSpec as P

HD = 128
DOC_LEN = 64

EPS = 1e-05
TEMPERATURE = 0.05
LOSS_SCALE = 65536.0
EXACT = lax.Precision.HIGHEST
FACTOR = HD**-0.5

CTX = ("zh", "x")
DP = ("zl", "y", "co")
EVERY = CTX + DP

f32 = jnp.float32
bf16 = jnp.bfloat16

ROWS_BY_ROWS = (((1,), (1,)), ((), ()))
COLS_BY_COLS = (((0,), (0,)), ((), ()))


def wide(a):
    return a.astype(f32)


def dot(a, b):
    return jnp.dot(a, b, preferred_element_type=f32)


def dot_nt(a, b, precision=None):
    return lax.dot_general(a, b, ROWS_BY_ROWS, precision=precision, preferred_element_type=f32)


def dot_tn(a, b, precision=None):
    return lax.dot_general(a, b, COLS_BY_COLS, precision=precision, preferred_element_type=f32)


def split(a, count):
    out = []
    for _ in range(count):
        head = a.astype(bf16)
        out.append(head)
        a = a - wide(head)
    return out


def stacked_pieces(a, count):
    return jnp.concatenate(split(a, count), axis=0)


def folded(a, count):
    rows = a.shape[0] // count
    return sum(a[i * rows : (i + 1) * rows] for i in reversed(range(count)))


def iota(shape, axis):
    return lax.broadcasted_iota(jnp.int32, shape, axis)


def as_row(column):
    n = column.shape[0]
    return jnp.sum(jnp.where(iota((n, n), 0) == iota((n, n), 1), column, 0.0), 0, keepdims=True)


def position():
    return [lax.axis_index(a) for a in EVERY]


def inverse_rms(a):
    return lax.rsqrt(jnp.mean(a * a, axis=-1, keepdims=True) + EPS)


def probabilities(q, k, ctx_keys):
    n = q.shape[0]
    same = iota((n, n), 0) // DOC_LEN == iota((n, n), 1) // DOC_LEN
    ctx_exps = jnp.exp(dot_nt(q, ctx_keys) * FACTOR)
    own_exps = jnp.where(same, jnp.exp(dot_nt(q, k) * FACTOR), 0.0)
    total = jnp.sum(ctx_exps, 1, keepdims=True) + jnp.sum(own_exps, 1, keepdims=True)
    return ctx_exps / total, own_exps / total


def call(kernel, out_shape, in_specs, scratch=(), vmem=16, flops=10**9, accessed=0):
    in_specs = [
        pl.BlockSpec(memory_space=pl.ANY if s == "a" else pltpu.VMEM) for s in in_specs
    ]
    return pl.pallas_call(
        kernel,
        out_shape=out_shape,
        in_specs=in_specs,
        out_specs=jax.tree.map(lambda _: pl.BlockSpec(memory_space=pltpu.VMEM), out_shape),
        scratch_shapes=scratch,
        compiler_params=pltpu.CompilerParams(vmem_limit_bytes=vmem * 2**20),
        cost_estimate=pl.CostEstimate(flops=flops, bytes_accessed=accessed, transcendentals=0),
    )


def shape(*dims, dtype=f32):
    return jax.ShapeDtypeStruct(dims, dtype)


def block_kernel(rows, context, out):
    pos = position()
    tok, feat = rows.shape
    out[:tok, :] = rows[...]
    here = ((pos[2] * 4 + pos[3]) * 2 + pos[4]) * feat
    part = wide(context[:, pl.ds(pl.multiple_of(here, feat), feat)])
    out[tok:, :] = jnp.concatenate([part, jnp.zeros_like(part)], axis=0).astype(bf16)


def forward_kernel(gain, partners, weights, wo, ctx, *refs):
    pieces, refs = refs[:4], refs[4:]
    qkv, own, branch, mix, normed, ctx_columns, last, stacks, sems = refs
    pos = position()
    fetch = [pltpu.make_async_copy(wo, last, sems.at[0])]
    arrive = [
        pltpu.make_async_copy(piece, stacks.at[i], sems.at[1 + i]) for i, piece in enumerate(pieces)
    ]
    for copy in arrive + fetch:
        copy.start()
    tok, feat = qkv.shape[0], stacks.shape[3]
    for copy in arrive:
        copy.wait()
    blocks = []
    for along_x in range(4):
        ref = stacks.at[along_x]
        blocks += [(ref, i, along_x, i) for i in range(4)]
        for i in range(4):
            place = ((pos[0] - i) & 3) * 4 + ((pos[1] - along_x) & 3)
            ctx_columns[pl.ds(pl.multiple_of(place * 8, 8), 8), :] = wide(ref[i, tok:, :])[:8]
    ctx_inv = jnp.sum(wide(ctx[:, 2 * HD :]), axis=1, keepdims=True)
    dp = (pos[2] * 4 + pos[3]) * 2 + pos[4]
    here = pl.ds(pl.multiple_of(dp * feat, feat), feat)
    ctx_columns[...] = ctx_columns[...] * ctx_inv * gain[:, here]
    docs = tok // DOC_LEN
    averaging = jnp.where(iota((8, tok), 0) == iota((8, tok), 1) // DOC_LEN, 1 / DOC_LEN, 0.0)
    averaging = averaging.astype(bf16)
    squares = jnp.zeros((tok, 1), f32)
    for ref, i, _, _ in blocks:
        rows = wide(ref[i, :tok, :])
        squares = squares + jnp.sum(rows * rows, axis=1, keepdims=True)
    inv = lax.rsqrt(squares / (16 * feat) + EPS)
    total = jnp.zeros((tok, 3 * HD), f32)
    for ref, i, along_x, along_z in blocks:
        place = ((pos[0] - along_z) & 3) * 4 + ((pos[1] - along_x) & 3)
        here = pl.ds(pl.multiple_of(place * feat, feat), feat)
        rows = ref[i, :tok, :]
        ready = (wide(rows) * inv * gain[:, here]).astype(bf16)
        normed[:, here] = ready
        total = total + dot(ready, weights[here, :])
        own[:, here] = dot(averaging, rows)[:docs]
    total = total.astype(bf16)
    qkv[...] = total
    q, k, v = total[:, :HD], total[:, HD : 2 * HD], total[:, 2 * HD :]
    ctx_probs, own_probs = probabilities(q, k, ctx[:, :HD])
    ctx_weights = ctx_probs.astype(bf16)
    mixture = dot(ctx_weights, ctx[:, HD : 2 * HD]) + dot(own_probs.astype(bf16), v)
    mean = dot(averaging, mixture.astype(bf16))
    mix[:, :HD] = mean[:docs]
    mix[:, HD : 2 * HD] = dot(averaging, ctx_weights)[:docs] * DOC_LEN
    mix[:, 2 * HD :] = jnp.broadcast_to(wide(partners[...]), (docs, HD))
    fetch[0].wait()
    branch[...] = folded(dot(stacked_pieces(mean, 3), last[...]), 3)[:docs]


def by_token(a):
    rows = [jnp.broadcast_to(a[i : i + 1], (DOC_LEN, a.shape[1])) for i in range(4)]
    return jnp.concatenate(rows, axis=0)


def backward(own, ctx, upstream, grads, grad_ctx_keys):
    q, k, v = (own[:, j * HD : (j + 1) * HD] for j in range(3))
    ctx_probs, own_probs = probabilities(q, k, ctx[:, :HD])
    ctx_dweights = by_token(dot_nt(upstream.astype(bf16), ctx[:, HD : 2 * HD]))
    own_dweights = by_token(dot_nt(upstream.astype(bf16), v))
    inner = jnp.sum(ctx_probs * ctx_dweights, 1, keepdims=True)
    inner = inner + jnp.sum(own_probs * own_dweights, 1, keepdims=True)
    ctx_dscores = (ctx_probs * (ctx_dweights - inner) * FACTOR).astype(bf16)
    own_dscores = (own_probs * (own_dweights - inner) * FACTOR).astype(bf16)
    grad_ctx_keys[...] = dot_tn(ctx_dscores, q)
    grads[:, :HD] = (dot(ctx_dscores, ctx[:, :HD]) + dot(own_dscores, k)).astype(bf16)
    grads[:, HD : 2 * HD] = dot_tn(own_dscores, q).astype(bf16)
    grad_v = dot_tn(own_probs.astype(bf16), by_token(upstream).astype(bf16))
    grads[:, 2 * HD :] = grad_v.astype(bf16)


def loss_kernel(wo, ctx, own, *refs):
    messages, refs = refs[:8], refs[8:]
    loss, grad_out, grads, grad_ctx_keys, grad_ctx_values, pooled, mix, weights, extra, slope, up = refs
    pos = position()
    width = wo.shape[1]
    co, y, dp = pos[4], pos[3], (pos[2] * 4 + pos[3]) * 2 + pos[4]
    for i in range(8):
        message, core = messages[i], co if i < 4 else 1 - co
        here = pl.ds(pl.multiple_of((core * 4 + ((y - i % 4) & 3)) * 8, 8), 8)
        pooled[here, :] = message[:, :width]
        mix[here, :] = message[:, width : width + HD]
        weights[here, :] = message[:, width + HD : width + 2 * HD]
        extra[here, :] = message[:, width + 2 * HD :]
    n = pooled.shape[0]
    vectors = pooled[...]
    length = jnp.sqrt(jnp.sum(vectors * vectors, axis=1, keepdims=True) + 1e-06)
    unit = vectors / length
    parts = stacked_pieces(vectors, 3)
    products = dot_nt(parts, parts)
    gram = jnp.zeros((n, n), f32)
    for i, j in ((2, 1), (1, 2), (2, 0), (1, 1), (0, 2), (1, 0), (0, 1), (0, 0)):
        gram = gram + products[i * n : (i + 1) * n, j * n : (j + 1) * n]
    scores = gram / (length * as_row(length)) / TEMPERATURE
    diagonal = iota((n, n), 0) == iota((n, n), 1)

    def document(axis):
        at = iota((n, n), axis)
        return (((at >> 2) & 1) * 32 + ((at >> 3) & 3) * 8 + (at >> 5) * 4 + (at & 3)).astype(f32)

    partners = extra[:, 0:1]
    chosen = jnp.where(partners == document(1), 1.0, 0.0)
    chosen_back = jnp.where(as_row(partners) == document(0), 1.0, 0.0)
    exps = jnp.where(diagonal, 0.0, jnp.exp(scores))
    sums = jnp.sum(exps, axis=1, keepdims=True)
    picked = jnp.sum(scores * chosen, axis=1, keepdims=True)
    loss[...] = jnp.sum(jnp.log(sums) - picked, axis=0, keepdims=True) / n
    coeff = (exps / sums - chosen) / n * LOSS_SCALE
    coeff_back = (exps / as_row(sums) - chosen_back) / n * LOSS_SCALE
    lead, second, third = split(coeff + coeff_back, 3)
    units = split(unit, 3)
    left = jnp.concatenate([third, second, second, lead, lead, lead], axis=1)
    right = jnp.concatenate([units[i] for i in (0, 1, 0, 2, 1, 0)], axis=0)
    grad_unit = dot(left, right) / TEMPERATURE
    radial = jnp.sum(unit * grad_unit, axis=1, keepdims=True)
    slope[...] = (grad_unit - unit * radial) / length
    part = slope[:, pl.ds(pl.multiple_of(dp * (width // 16), width // 16), width // 16)]
    grad_out[...] = dot_tn(mix[...], part, EXACT)
    upstream = folded(dot_nt(stacked_pieces(slope[...] / DOC_LEN, 3), wo[...]), 3)
    up[...] = wide(upstream.astype(bf16))
    grad_ctx_values[...] = dot_tn(weights[...], up[...], EXACT)
    upstream = up[pl.ds(pl.multiple_of(co * (n // 2) + y * 8, 8), 8), :]
    upstream = jnp.where(pos[2] == 0, upstream[:4], upstream[4:])
    upstream = jnp.concatenate([upstream, upstream], axis=0)
    backward(own, ctx, upstream, grads, grad_ctx_keys)


def context_kernel(one, two, values, wk, wv, total, out0, out1, out2, out3, part):
    pos = position()
    half = part.shape[1]
    grad = one[...] + two[...]
    grad = jnp.concatenate([grad, values[...]], axis=1)
    total[...] = grad
    here = pl.ds(pl.multiple_of(pos[4] * half, half), half)
    got = dot_nt(stacked_pieces(grad[:, :HD], 2), wk[here, :])
    got = got + dot_nt(stacked_pieces(grad[:, HD:], 2), wv[here, :])
    part[...] = folded(got, 2)
    for k, out in enumerate((out0, out1, out2, out3)):
        at = (pos[1] + k) & 3
        rows = [part[pl.ds(pl.multiple_of(z * 32 + at * 8, 8), 8), :] for z in range(4)]
        out[...] = jnp.concatenate(rows, axis=0).astype(out.dtype)


def middle_kernel(own, one, two, three, out0, out1, out2, out3, total):
    pos = position()
    total[...] = (own[...] + wide(two[...])) + (wide(one[...]) + wide(three[...]))
    for k, out in enumerate((out0, out1, out2, out3)):
        at = (pos[0] + k) & 3
        out[...] = total[pl.ds(pl.multiple_of(at * 8, 8), 8), :].astype(out.dtype)


def finish_kernel(context, gain, mine, theirs, out):
    pos = position()
    half = mine.shape[1]
    low = pos[4] == 0
    grad = jnp.concatenate(
        [jnp.where(low, mine[...], theirs[...]), jnp.where(low, theirs[...], mine[...])], axis=1
    )
    rows = wide(context[...])
    inv = inverse_rms(rows)
    scaled = gain[...] * grad
    out[...] = inv * scaled - rows * inv**3 * jnp.mean(rows * scaled, axis=1, keepdims=True)


def weight_kernel(side, normed, grads, out):
    feat = out.shape[1]
    core = position()[4]
    core = core if side == 0 else 1 - core
    right = grads[...]
    for i in range(8):
        here = pl.ds(pl.multiple_of((i * 2 + core) * feat, feat), feat)
        out[i] = dot_tn(normed[:, here], right).astype(bf16)


def weight_y_kernel(mine, came, out0, out1, out2, out3):
    y = position()[3]
    for k, out in enumerate((out0, out1, out2, out3)):
        for zl in range(2):
            chip = zl * 4 + ((y + k) & 3)
            out[zl] = (wide(mine[chip]) + wide(came[chip])).astype(out.dtype)


def weight_z_kernel(own, one, two, three, mine, theirs):
    pos = position()
    for zl in range(2):
        got = (own[zl] + wide(two[zl])) + (wide(one[zl]) + wide(three[zl]))

        @pl.when(pos[2] == zl)
        def _():
            mine[...] = got

        @pl.when(pos[2] != zl)
        def _():
            theirs[...] = got.astype(bf16)


def weight_last_kernel(mine, theirs, ctx_columns, grad_ctx, grad_query, grad_key, grad_value):
    total = mine[...] + wide(theirs[...])
    columns = ctx_columns[...].astype(bf16)
    lead, rest = split(grad_ctx[...], 2)
    from_ctx = dot_tn(columns, rest) + dot_tn(columns, lead)
    grad_query[...] = total[:, :HD]
    grad_key[...] = total[:, HD : 2 * HD] + from_ctx[:, :HD]
    grad_value[...] = total[:, 2 * HD :] + from_ctx[:, HD:]


def shift(a, axis, k):
    return lax.ppermute(a, axis, [(i, (i + k) % 4) for i in range(4)])


def others(a, axis):
    return [shift(a, axis, k) for k in (1, 2, 3)]


def other(a, axis):
    return lax.ppermute(a, axis, [(0, 1), (1, 0)])


def pair(a, axis):
    b = other(a, axis)
    first = lax.axis_index(axis) == 0
    return jnp.where(first, jnp.concatenate([a, b]), jnp.concatenate([b, a]))


def ring_sum(a, axis):
    one, two, three = others(a, axis)
    return (a + two) + (one + three)


def hlo_split(a, count):
    out = []
    for _ in range(count):
        out.append(lax.reduce_precision(a, 8, 7))
        a = a - out[-1]
    return out


def spread(block, axis, size):
    copies = jnp.broadcast_to(block[None], (size,) + block.shape)
    return lax.all_to_all(copies, axis, 0, 0)


def shards(doc_states, context, gain, w_query, w_key, w_value, w_out, partners):
    tok, feat = doc_states.shape
    docs = tok // DOC_LEN
    width = w_query.shape[0]
    gain_row = gain.reshape(1, width)

    block = call(block_kernel, shape(tok + 16, feat, dtype=bf16), ["v"] * 2)(doc_states, context)
    block = jnp.stack([block] + others(block, "zh"))
    rows = [block] + others(block, "x")

    swap = [(c * 16 + d, d * 16 + c) for c in range(16) for d in range(16)]
    named_rows = wide(lax.ppermute(context, EVERY, swap))
    projections = jnp.concatenate([w_query, w_key, w_value], axis=1)
    named_rows, _, projections = lax.optimization_barrier((named_rows, block, projections))
    inv = inverse_rms(named_rows)
    named_rows = (named_rows * inv * gain).astype(bf16)
    few = [dot(named_rows, projections)[:, HD:]] + hlo_split(inv, 3)
    few = jnp.concatenate([a.astype(bf16) for a in few], axis=1)
    few = jnp.pad(few, ((0, 0), (0, 3 * HD - few.shape[1])))
    ctx_kv = spread(few, DP, 16).reshape(-1, 3 * HD)

    qkv, own_mean, branch, mix, normed, ctx_columns = call(
        forward_kernel,
        (
            shape(tok, 3 * HD, dtype=bf16),
            shape(docs, width),
            shape(docs, width),
            shape(docs, 3 * HD),
            shape(tok, width, dtype=bf16),
            shape(HD, feat),
        ),
        ["v"] * 3 + ["a"] + ["v"] + ["a"] * 4,
        scratch=[
            pltpu.VMEM((HD, width), bf16),
            pltpu.VMEM((4,) + block.shape, bf16),
            pltpu.SemaphoreType.DMA((5,)),
        ],
        vmem=24,
    )(gain_row, partners[:, None], projections, w_out, ctx_kv, *rows)

    pooled = own_mean + ring_sum(ring_sum(branch, "x"), "zh")
    message = jnp.concatenate([pooled, mix], axis=1)
    message = pair(message, "zl")
    messages = [message] + others(message, "y")
    total = 64
    loss, grad_out, grads, grad_ctx_keys, grad_ctx_values = call(
        loss_kernel,
        (
            shape(1, 1),
            shape(HD, feat),
            shape(tok, 3 * HD, dtype=bf16),
            shape(HD, HD),
            shape(HD, HD),
        ),
        ["v"] * 11,
        scratch=[
            pltpu.VMEM((total, width), f32),
            pltpu.VMEM((total, HD), f32),
            pltpu.VMEM((total, HD), f32),
            pltpu.VMEM((total, HD), f32),
            pltpu.VMEM((total, width), f32),
            pltpu.VMEM((total, HD), f32),
        ],
        vmem=24,
    )(w_out, ctx_kv, qkv, *messages, *[other(m, "co") for m in messages])

    half = width // 2
    rows = 4 * context.shape[0]
    one, two, three = others(grad_ctx_keys, "y")
    by_y = (grad_ctx_keys + two) + (one + three)
    grad_ctx_keys = by_y + other(by_y, "co")
    grad_ctx, part, *sent = call(
        context_kernel,
        (shape(HD, 2 * HD), shape(rows, half)) + (shape(rows, half, dtype=bf16),) * 3,
        ["v"] * 5,
        scratch=[pltpu.VMEM((4 * rows, half), f32)],
    )(grad_ctx_keys, other(grad_ctx_keys, "zl"), grad_ctx_values, w_key, w_value)
    came = [shift(a, "x", k) for k, a in zip((1, 2, 3), sent)]
    part, *sent = call(
        middle_kernel,
        (shape(rows // 4, half),) + (shape(rows // 4, half, dtype=bf16),) * 3,
        ["v"] * 4,
        scratch=[pltpu.VMEM((rows, half), f32)],
    )(part, *came)
    one, two, three = [wide(shift(a, "zh", k)) for k, a in zip((1, 2, 3), sent)]
    part = (part + two) + (one + three)
    grad_context = call(finish_kernel, shape(*context.shape), ["v"] * 4, flops=10**9)(
        context, gain_row, part, other(part, "co")
    )

    theirs, mine = (
        call(
            functools.partial(weight_kernel, side),
            shape(8, feat, 3 * HD, dtype=bf16),
            ["v"] * 2,
        )(normed, grads)
        for side in (1, 0)
    )
    came, _ = lax.optimization_barrier((other(theirs, "co"), by_y))
    mine, *sent = call(
        weight_y_kernel,
        (shape(2, feat, 3 * HD),) + (shape(2, feat, 3 * HD, dtype=bf16),) * 3,
        ["v"] * 2,
    )(mine, came)
    came = [shift(a, "y", k) for k, a in zip((1, 2, 3), sent)]
    mine, theirs = call(
        weight_z_kernel,
        (shape(feat, 3 * HD), shape(feat, 3 * HD, dtype=bf16)),
        ["v"] * 4,
    )(mine, *came)
    grad_query, grad_key, grad_value = call(
        weight_last_kernel, (shape(feat, HD),) * 3, ["v"] * 4
    )(mine, other(theirs, "zl"), ctx_columns, grad_ctx)
    return loss.reshape(()), grad_context, grad_query, grad_key, grad_value, grad_out


def solution(mesh):
    split = Mesh(mesh.devices.reshape(4, 4, 2, 4, 2), EVERY)
    in_specs = (
        P(DP, CTX),
        P(CTX, None),
        P(),
        P(None, CTX),
        P(None, CTX),
        P(None, CTX),
        P(CTX, None),
        P(DP),
    )
    out_specs = (P(), P(CTX, None), P(DP, CTX), P(DP, CTX), P(DP, CTX), P(CTX, DP))
    return jax.shard_map(
        shards, mesh=split, in_specs=in_specs, out_specs=out_specs, check_vma=False
    )
```
